32 devices in a mesh: lat: 16 (over z, y, core), lon: 2 (over x).
Axes of the slice: x: 2, y: 2, z: 4, core: 2. Of those that a mesh axis runs over, the one named last changes fastest.
Arguments:
- state_field: bfloat16 [73, 128, 256], P(None, 'lat', 'lon'), may hold values from -6 to 6
- support_rows: int32 [64, 5], P('lat'), may hold values from -2 to 2, as said below
- window_bands: int32 [16], replicated, may hold values from 0 to 63, as said below
- conv_weight: bfloat16 [5, 3, 73, 256], replicated, may hold values from -0.1875 to 0.1875
- w_query: bfloat16 [256, 256], replicated
- w_key: bfloat16 [256, 256], replicated
- w_value: bfloat16 [256, 256], replicated, may hold values from -0.375 to 0.375
- w_out: bfloat16 [256, 256], replicated, may hold values from -0.75 to 0.75
Outputs:
- window_out: bfloat16 [16, 128, 256], P('lat', 'lon')
The draws below stay inside these ranges and needn't reach their ends.
Inputs may be any that keep to these rules, and one draw needn't show every extreme that they name: `support_rows`: each row is a permutation of the 5 offsets from -2 to 2. `window_bands`: 16 distinct token bands.
All inputs are finite; a program needn't handle non-finite values.
Results may differ from the reference program's by a relative error of at most 0.019.
Values may be sent and summed in bfloat16 or wider, within the bound.
No kernel may reach another device: no remote copies, remote signals or barrier semaphores. Data moves between devices by JAX's collectives and lax.ppermute only.
A program may use at most 64 MiB of HBM per device.

```python
import math
import jax
import jax.numpy as jnp
from jax import lax

C_IN = 73
D = 256
H = 4
KS = 5
NLAT = 64
NLON = 128
QB = 16


def draw_support_rows(key, part):
    branch_keys = jax.random.split(jax.random.fold_in(key, 3), NLAT)

    def one_band(band_key):
        return jax.random.permutation(band_key, KS)
    table = jax.vmap(one_band)(branch_keys)
    return (table - KS // 2).astype(jnp.int32)


def draw_window_bands(key, part):
    inner = jax.random.permutation(jax.random.fold_in(key, 5), NLAT - 2)[:QB - 2] + 1
    chosen = jnp.concatenate([jnp.array([0, NLAT - 1], dtype=jnp.int32), inner.astype(jnp.int32)])
    return jax.random.permutation(jax.random.fold_in(key, 6), chosen).astype(jnp.int32)


def shared_key_matrix(key):
    base = jax.random.normal(jax.random.fold_in(key, 11), (D, D), jnp.float32)
    return jnp.clip(base, -6.0, 6.0) * D ** (-0.5)


def draw_w_key(key, part):
    return shared_key_matrix(key).astype(jnp.bfloat16)


def draw_w_query(key, part):
    base = jax.random.normal(jax.random.fold_in(key, 13), (D, D), jnp.float32)
    drawn = jnp.clip(base, -6.0, 6.0) * (3.0 * D ** (-0.5))
    return drawn.astype(jnp.bfloat16)


def steps_of(own_key, extent, shards, low, high):
    def one(axis_at, parts):
        draws = jax.random.uniform(jax.random.fold_in(jax.random.fold_in(own_key, 6), axis_at), (parts,), jnp.float32, low / len(shards), high / len(shards))
        return jnp.repeat(jnp.exp(draws), extent[axis_at] // parts).reshape((-1,) + (1,) * (len(extent) - axis_at - 1))

    gain = one(*shards[0])
    for cut in shards[1:]:
        gain = gain * one(*cut)
    return gain


def bell_draw(rng, extent, scale, reach, pieces=(), kind=jnp.bfloat16):
    drawn = scale * jax.random.normal(rng, extent, jnp.float32)
    if pieces:
        drawn = drawn * steps_of(rng, extent, pieces, -0.22, 0.18)
    return jnp.clip(drawn, -reach, reach).astype(kind)


def setup_inputs(seed: int = 0) -> dict:
    seeds = jax.random.split(jax.random.key(seed), 9)
    state_field = bell_draw(seeds[0], (C_IN, 2 * NLAT, 2 * NLON), 1.0, 6.0, ((1, 16), (2, 2)))
    support_rows = draw_support_rows(jax.random.fold_in(seeds[8], 71), 0)
    window_bands = draw_window_bands(jax.random.fold_in(seeds[8], 71), 0)
    conv_weight = bell_draw(seeds[3], (KS, 3, C_IN, D), (KS * 3 * C_IN) ** -0.5, 0.1875)
    w_query = draw_w_query(jax.random.fold_in(seeds[8], 71), 0)
    w_key = draw_w_key(jax.random.fold_in(seeds[8], 71), 0)
    w_value = bell_draw(seeds[6], (D, D), D ** -0.5, 0.375)
    w_out = bell_draw(seeds[7], (D, D), (D // 4) ** -0.5, 0.75)
    return {"state_field": state_field, "support_rows": support_rows, "window_bands": window_bands, "conv_weight": conv_weight, "w_query": w_query, "w_key": w_key, "w_value": w_value, "w_out": w_out}


def conv_features(extended, support_rows, conv_weight):
    bands = support_rows.shape[0]
    width = (extended.shape[2] - 1) // 2
    row_index = 2 * jnp.arange(bands, dtype=jnp.int32)[:, None] + support_rows.astype(jnp.int32) + 2
    picked = jnp.take(extended, row_index, axis=1)
    tapped = jnp.stack([picked[..., column_tap:column_tap + 2 * width:2] for column_tap in range(3)], axis=3)
    patches = jnp.transpose(tapped, (1, 4, 2, 3, 0)).reshape(bands * width, -1)
    raw = jnp.dot(patches, conv_weight.reshape(-1, conv_weight.shape[-1]), preferred_element_type=jnp.float32)
    factor = lax.rsqrt(lax.optimization_barrier(jnp.mean(raw * raw, axis=-1, keepdims=True)) + 1e-06)
    return (raw * factor).astype(jnp.bfloat16).reshape(bands, width, -1)

def reference(state_field, support_rows, window_bands, conv_weight, w_query, w_key, w_value, w_out):
    padded = jnp.pad(state_field, ((0, 0), (2, 2), (0, 0)))
    extended = jnp.concatenate([padded[:, :, -1:], padded], axis=2)
    features = conv_features(extended, support_rows, conv_weight)
    flat = features.reshape(-1, D)
    head_size = D // H
    queries = jnp.dot(flat, w_query, preferred_element_type=jnp.float32).astype(jnp.bfloat16).reshape(NLAT, NLON, D)
    keys = jnp.dot(flat, w_key, preferred_element_type=jnp.float32).astype(jnp.bfloat16)
    values = jnp.dot(flat, w_value, preferred_element_type=jnp.float32).astype(jnp.bfloat16)
    keys_wide = keys.astype(jnp.float32).reshape(-1, H, head_size)
    values_wide = values.astype(jnp.float32).reshape(-1, H, head_size)
    window = queries[window_bands.astype(jnp.int32)].reshape(QB * NLON, H, head_size)
    centre = (jnp.arange(NLAT, dtype=jnp.float32) + 0.5) * (math.pi / NLAT) - math.pi / 2
    log_area = jnp.repeat(jnp.log(jnp.cos(centre)), NLON)
    total_rows = QB * NLON
    block_rows = math.gcd(total_rows, 256)
    blocks = window.reshape(total_rows // block_rows, block_rows, H, head_size)
    scale = 1.0 / math.sqrt(head_size)

    def one_block(block_queries):
        scores = jnp.einsum('qhd,khd->qhk', block_queries.astype(jnp.float32), keys_wide) * scale + log_area
        highest = lax.optimization_barrier(jnp.max(scores, axis=-1, keepdims=True))
        weights = jnp.exp(scores - highest)
        totals = lax.optimization_barrier(jnp.sum(weights, axis=-1))
        probs = lax.optimization_barrier(weights.astype(jnp.bfloat16)).astype(jnp.float32)
        mixed = jnp.einsum('qhk,khd->qhd', probs, values_wide)
        return (mixed / totals[..., None]).astype(jnp.bfloat16)
    attended = lax.map(one_block, blocks).reshape(total_rows, D)
    result = jnp.dot(attended, w_out, preferred_element_type=jnp.float32).astype(jnp.bfloat16)
    return result.reshape(QB, NLON, D)
```

```python
import math

import jax
import jax.numpy as jnp
from jax import lax
from jax.experimental import pallas as pl
from jax.experimental.pallas import tpu as pltpu
from jax.sharding import PartitionSpec as P

D = 256
H = 4
AXES = ("lat", "lon")
F32 = jnp.float32
BF16 = jnp.bfloat16


def padded(x, sides, width):
    for axis, dim in sides:
        devices, length = (lax.axis_size(axis), x.shape[dim])
        up = [(i, (i + 1) % devices) for i in range(devices - 1)]
        down = [(j, i) for i, j in up]
        last = lax.slice_in_dim(x, length - width, length, axis=dim)
        leading = lax.slice_in_dim(x, 0, width, axis=dim)
        before = lax.ppermute(last, axis, up)
        after = lax.ppermute(leading, axis, down)
        x = jnp.concatenate([before, x, after], axis=dim)
    return x


def shifted(x, axis, by):
    devices = lax.axis_size(axis)
    return lax.ppermute(x, axis, [(i, (i + by) % devices) for i in range(devices)])


def conv_features(extended, support_rows, conv_weight):
    bands = support_rows.shape[0]
    width = (extended.shape[2] - 1) // 2
    row_index = 2 * jnp.arange(bands, dtype=jnp.int32)[:, None] + support_rows + 2
    picked = jnp.take(extended, row_index, axis=1)
    tapped = jnp.stack(
        [picked[..., column_tap : column_tap + 2 * width : 2] for column_tap in range(3)], axis=3
    )
    patches = jnp.transpose(tapped, (1, 4, 2, 3, 0)).reshape(bands * width, -1)
    raw = jnp.dot(
        patches, conv_weight.reshape(-1, conv_weight.shape[-1]), preferred_element_type=F32
    )
    factor = lax.rsqrt(jnp.mean(raw * raw, axis=-1, keepdims=True) + 1e-06)
    return (raw * factor).astype(BF16).reshape(bands, width, -1)


def absorb(carry, block_keys, block_values, block_area, queries, scale):
    running_max, running_sum, mixed = carry
    scores = (
        jnp.einsum("qhd,khd->qhk", queries, block_keys, preferred_element_type=F32) * scale
        + block_area
    )
    new_max = jnp.maximum(running_max, jnp.max(scores, axis=-1))
    factor = jnp.exp(running_max - new_max)
    weights = jnp.exp(scores - new_max[..., None])
    running_sum = running_sum * factor + jnp.sum(weights, axis=-1)
    update = jnp.einsum(
        "qhk,khd->qhd", weights.astype(BF16), block_values, preferred_element_type=F32
    )
    mixed = mixed * factor[..., None] + update
    return (new_max, running_sum, mixed)


def sweep(carry, keys, values, queries, band_total):
    rows = keys.shape[0]
    lon_tile = keys.shape[1]
    head_size = D // H
    band_block = math.gcd(rows, max(1, 512 // lon_tile))
    blocks = rows // band_block
    block_len = band_block * lon_tile
    keys_blocks = keys.reshape(blocks, block_len, H, head_size)
    values_blocks = values.reshape(blocks, block_len, H, head_size)
    band_index = jnp.arange(rows, dtype=jnp.int32)
    area_rows = jnp.repeat(log_area(band_index, band_total), lon_tile).reshape(blocks, block_len)
    scale = 1.0 / math.sqrt(head_size)

    def step_block(state, inputs):
        return (absorb(state, inputs[0], inputs[1], inputs[2], queries, scale), None)

    result, unused = lax.scan(step_block, carry, (keys_blocks, values_blocks, area_rows))
    return result


def log_area(bands, band_total):
    centre = (bands.astype(F32) + 0.5) * (math.pi / band_total) - math.pi / 2
    return jnp.log(jnp.cos(centre))


def general(state_field, support_rows, window_bands, conv_weight, w_query, w_key, w_value, w_out):
    lat_tile = support_rows.shape[0]
    lon_tile = state_field.shape[2] // 2
    whole_lon = lon_tile * lax.axis_size("lon")
    band_total = lat_tile * lax.axis_size("lat")
    head_size = D // H
    extended = padded(state_field, (("lat", 1),), 2)
    western = shifted(extended[:, :, -1:], "lon", 1)
    extended = jnp.concatenate([western, extended], axis=2)
    features = conv_features(extended, support_rows, conv_weight)
    slot_count = window_bands.shape[0] // lax.axis_size("lat")
    piece = lax.all_gather(features, "lat", axis=0, tiled=True)
    mine = lax.dynamic_slice_in_dim(
        window_bands, lax.axis_index("lat") * slot_count, slot_count, axis=0
    )
    picked = jnp.take(piece, mine, axis=0)
    gathered = lax.all_gather(picked, "lon", axis=1, tiled=True)
    query_count = slot_count * whole_lon
    queries = jnp.dot(gathered.reshape(query_count, D), w_query, preferred_element_type=F32)
    queries = queries.astype(BF16).reshape(query_count, H, head_size)
    initial = (
        jnp.full((query_count, H), -1e30, F32),
        jnp.zeros((query_count, H), F32),
        jnp.zeros((query_count, H, head_size), F32),
    )
    piece_rows = piece.reshape(-1, D)
    keys = jnp.dot(piece_rows, w_key, preferred_element_type=F32).astype(BF16)
    values = jnp.dot(piece_rows, w_value, preferred_element_type=F32).astype(BF16)
    running_max, running_sum, mixed = sweep(
        initial, keys.reshape(piece.shape), values.reshape(piece.shape), queries, band_total
    )
    best = lax.pmax(running_max, "lon")
    factor = jnp.exp(running_max - best)
    scaled_mix = (mixed * factor[..., None]).reshape(slot_count, whole_lon, D)
    scaled_sum = (running_sum * factor).reshape(slot_count, whole_lon, H)
    mix_share, sum_share = (
        lax.psum_scatter(part.astype(BF16), "lon", scatter_dimension=1, tiled=True).astype(F32)
        for part in (scaled_mix, scaled_sum)
    )
    attended = mix_share.reshape(slot_count, lon_tile, H, head_size) / sum_share[..., None]
    attended = attended.astype(BF16).reshape(slot_count * lon_tile, D)
    result = jnp.dot(attended, w_out, preferred_element_type=F32).astype(BF16)
    return result.reshape(slot_count, lon_tile, D)


def exchange(x, lat_mask, lon_mask):
    lats, lons = lax.axis_size("lat"), lax.axis_size("lon")
    pairs = [
        (i * lons + j, (i ^ lat_mask) * lons + (j ^ lon_mask))
        for i in range(lats)
        for j in range(lons)
    ]
    return lax.ppermute(x, AXES, pairs)


def vertical(x, cross):
    lats, lons = lax.axis_size("lat"), lax.axis_size("lon")
    pairs = []
    for i in range(lats):
        for j in range(lons):
            source = i - 1 if j == 0 else i + 1
            if 0 <= source < lats:
                pairs.append((source * lons + (j ^ cross), i * lons + j))
    return lax.ppermute(x, AXES, pairs)


def conv_kernel(
    rows_ref, own_ref, other_ref, edge_ref, edge_other_ref, weight_ref, out_ref,
    strided, taken, patches, weights,
):
    channels, rows, lons = own_ref.shape
    slots, taps = weight_ref.shape[:2]
    deep = taken.shape[1]
    width = lons
    bands = out_ref.shape[0] // width
    tail = jnp.zeros(((deep - channels) * rows, lons), F32)
    for side, ref in enumerate((own_ref, other_ref)):
        strided[side, 0 : channels * rows] = ref[...].astype(F32).reshape(channels * rows, lons)
        strided[side, channels * rows :] = tail
    column = lax.broadcasted_iota(jnp.int32, (2 * lons, taps * width), 0)
    place = lax.broadcasted_iota(jnp.int32, (2 * lons, taps * width), 1)
    wanted = lax.rem(2 * (place % width) + place // width - 1 + 2 * lons, 2 * lons)
    choose = (column == wanted).astype(F32).astype(BF16)
    lines = []
    for row in range(rows):
        lines.append(
            jnp.concatenate(
                [strided[side, pl.ds(row, deep, stride=rows), :] for side in range(2)], axis=1
            )
        )
    edge_rows = edge_ref.shape[0]
    short = jnp.zeros((deep - channels, 2 * lons), F32)
    for row in range(edge_rows):
        line = jnp.concatenate(
            [edge_ref[row].astype(F32), edge_other_ref[row].astype(F32)], axis=1
        )
        lines.append(jnp.concatenate([line, short], axis=0))
    split = jnp.dot(
        jnp.concatenate(lines, axis=0).astype(BF16), choose, preferred_element_type=F32
    ).astype(BF16)
    for row in range(rows):
        taken[edge_rows + row] = split[row * deep : (row + 1) * deep]
    for row in range(edge_rows):
        piece = split[(rows + row) * deep : (rows + row + 1) * deep]
        taken[row] = piece
        taken[edge_rows + rows + row] = piece
    blank = jnp.zeros((deep - channels, weight_ref.shape[3]), BF16)
    for slot in range(slots):
        for band in range(bands):
            line = taken[rows_ref[band, slot]]
            for tap in range(taps):
                at = (slot * taps + tap) * deep
                patches[at : at + deep, band * width : (band + 1) * width] = line[
                    :, tap * width : (tap + 1) * width
                ]
        for tap in range(taps):
            at = (slot * taps + tap) * deep
            weights[at : at + deep] = jnp.concatenate([weight_ref[slot, tap], blank], axis=0)
    raw = lax.dot_general(
        patches[...], weights[...], (((0,), (0,)), ((), ())), preferred_element_type=F32
    )
    factor = lax.rsqrt(jnp.mean(raw * raw, axis=-1, keepdims=True) + 1e-06)
    out_ref[...] = (raw * factor).astype(BF16)


def features_of(own, other, edge, edge_other, row_index, conv_weight):
    channels, rows, lons = own.shape
    slots, taps, _, width = conv_weight.shape
    bands = row_index.shape[0]
    deep = -(-channels // 16) * 16
    vmem = pl.BlockSpec(memory_space=pltpu.VMEM)
    return pl.pallas_call(
        conv_kernel,
        out_shape=jax.ShapeDtypeStruct((bands * lons, width), BF16),
        in_specs=[pl.BlockSpec(memory_space=pltpu.SMEM)] + [vmem] * 5,
        out_specs=vmem,
        scratch_shapes=[
            pltpu.VMEM((2, deep * rows, lons), F32),
            pltpu.VMEM((rows + 2 * edge.shape[0], deep, taps * lons), BF16),
            pltpu.VMEM((slots * taps * deep, bands * lons), BF16),
            pltpu.VMEM((slots * taps * deep, width), BF16),
        ],
        compiler_params=pltpu.CompilerParams(vmem_limit_bytes=32 * 2**20),
        cost_estimate=pl.CostEstimate(
            flops=2 * slots * taps * deep * bands * lons * width,
            bytes_accessed=2 * (conv_weight.size + 2 * own.size),
            transcendentals=0,
        ),
        name="conv",
    )(row_index, own, other, edge, edge_other, conv_weight)


def select_kernel(where_ref, near_ref, far_ref, out_ref, sems):
    slots, rows, _ = out_ref.shape

    def copy(slot, ref):
        start = pl.multiple_of(where_ref[slot, 1], rows)
        return pltpu.make_async_copy(ref.at[pl.ds(start, rows)], out_ref.at[slot], sems.at[slot])

    for slot in range(slots):
        kind = where_ref[slot, 0]

        @pl.when(kind == 0)
        def _():
            copy(slot, near_ref).start()

        @pl.when(kind == 1)
        def _():
            copy(slot, far_ref).start()

        @pl.when(kind == 2)
        def _():
            out_ref[slot] = jnp.zeros(out_ref.shape[1:], out_ref.dtype)

    for slot in range(slots):

        @pl.when(where_ref[slot, 0] != 2)
        def _():
            copy(slot, near_ref).wait()


def selected(where, near, far, rows):
    slots = where.shape[0]
    return pl.pallas_call(
        select_kernel,
        out_shape=jax.ShapeDtypeStruct((slots, rows, near.shape[1]), near.dtype),
        in_specs=[
            pl.BlockSpec(memory_space=pltpu.SMEM),
            pl.BlockSpec(memory_space=pl.ANY),
            pl.BlockSpec(memory_space=pl.ANY),
        ],
        out_specs=pl.BlockSpec(memory_space=pltpu.VMEM),
        scratch_shapes=[pltpu.SemaphoreType.DMA((slots,))],
        name="select",
    )(where, near, far)


def split3(x):
    high = x.astype(BF16).astype(F32)
    middle = (x - high).astype(BF16).astype(F32)
    return high, middle, x - high - middle


def attend_kernel(
    mine_ref, sel_ref, got_ref, near_ref, far_ref, area_ref, wq_ref, wk_ref, wv_ref,
    send_ref, keep_ref, lse_ref, scores, outs, lses,
):
    slots, rows, width = sel_ref.shape
    count = slots * rows
    head_size = width // H
    half = near_ref.shape[0]
    chunk = math.gcd(half, 512)
    token = (sel_ref[...] + got_ref[...]).reshape(count, width)
    query = jnp.dot(token, wq_ref[...], preferred_element_type=F32).astype(BF16).astype(F32)
    query = query * (1.0 / math.sqrt(head_size))
    lane = lax.broadcasted_iota(jnp.int32, (1, width), 1) // head_size
    spread = jnp.concatenate(
        [jnp.where(lane == head, query, 0.0) for head in range(H)], axis=0
    ).astype(BF16)
    turned = lax.dot_general(
        spread, wk_ref[...], (((1,), (1,)), ((), ())), preferred_element_type=F32
    ).astype(BF16)
    parts = [(ref, at) for ref in (near_ref, far_ref) for at in range(0, half, chunk)]
    best = jnp.full((H * count, 128), -jnp.inf, F32)
    for index, (ref, at) in enumerate(parts):
        block = lax.dot_general(
            turned, ref[at : at + chunk], (((1,), (1,)), ((), ())), preferred_element_type=F32
        )
        block = block + area_ref[:, index * chunk : (index + 1) * chunk]
        scores[:, index * chunk : (index + 1) * chunk] = block
        for lanes in range(0, chunk, 128):
            best = jnp.maximum(best, block[:, lanes : lanes + 128])
    top = jnp.max(best, axis=1, keepdims=True)
    total = jnp.zeros((H * count, 128), F32)
    mixed = jnp.zeros((H * count, width), F32)
    for index, (ref, at) in enumerate(parts):
        weight = jnp.exp(scores[:, index * chunk : (index + 1) * chunk] - top)
        for lanes in range(0, chunk, 128):
            total = total + weight[:, lanes : lanes + 128]
        mixed = mixed + jnp.dot(
            weight.astype(BF16), ref[at : at + chunk], preferred_element_type=F32
        )
    total = jnp.sum(total, axis=1, keepdims=True)
    value = jnp.dot((mixed / total).astype(BF16), wv_ref[...], preferred_element_type=F32)
    lse = top + jnp.log(total)
    out = jnp.zeros((count, width), F32)
    stat_lane = lax.broadcasted_iota(jnp.int32, (1, 128), 1)
    stats = jnp.zeros((count, 128), F32)
    for head in range(H):
        out = jnp.where(lane == head, value[head * count : (head + 1) * count], out)
        for order, piece in enumerate(split3(lse[head * count : (head + 1) * count])):
            stats = jnp.where(stat_lane == 3 * head + order, piece, stats)
    outs[...] = out.reshape(outs.shape)
    lses[...] = stats.reshape(lses.shape)
    own = mine_ref[0]
    half_slots = slots // 2
    keep_ref[...] = outs[pl.ds(own * half_slots, half_slots)]
    lse_ref[...] = lses[pl.ds(own * half_slots, half_slots)]
    send_ref[:, :, 0:width] = outs[pl.ds((1 - own) * half_slots, half_slots)].astype(BF16)
    send_ref[:, :, width:] = lses[pl.ds((1 - own) * half_slots, half_slots)].astype(BF16)


def attended(mine, sel, got, near, far, area, w_query, w_key, w_value):
    slots, rows, width = sel.shape
    keys = near.shape[0] + far.shape[0]
    count = slots * rows
    vmem = pl.BlockSpec(memory_space=pltpu.VMEM)
    half_slots = slots // 2
    return pl.pallas_call(
        attend_kernel,
        out_shape=(
            jax.ShapeDtypeStruct((half_slots, rows, width + 128), BF16),
            jax.ShapeDtypeStruct((half_slots, rows, width), F32),
            jax.ShapeDtypeStruct((half_slots, rows, 128), F32),
        ),
        in_specs=[pl.BlockSpec(memory_space=pltpu.SMEM)] + [vmem] * 8,
        out_specs=(vmem, vmem, vmem),
        scratch_shapes=[
            pltpu.VMEM((H * count, keys), F32),
            pltpu.VMEM((slots, rows, width), F32),
            pltpu.VMEM((slots, rows, 128), F32),
        ],
        compiler_params=pltpu.CompilerParams(vmem_limit_bytes=48 * 2**20),
        cost_estimate=pl.CostEstimate(
            flops=4 * H * count * keys * width,
            bytes_accessed=2 * keys * width,
            transcendentals=H * count * keys,
        ),
        name="attend",
    )(mine, sel, got, near, far, area, w_query, w_key, w_value)


def finish_kernel(keep_ref, lse_ref, got_ref, wo_ref, out_ref):
    slots, rows, width = keep_ref.shape
    head_size = width // H
    count = slots * rows
    keep = keep_ref[...].reshape(count, width)
    got = got_ref[:, :, 0:width].astype(F32).reshape(count, width)
    ours = lse_ref[...].reshape(count, 128)
    theirs = got_ref[:, :, width:].astype(F32).reshape(count, 128)
    lane = lax.broadcasted_iota(jnp.int32, (1, width), 1) // head_size
    share = jnp.zeros((count, width), F32)
    for head in range(H):
        own = ours[:, 3 * head : 3 * head + 1] + ours[:, 3 * head + 1 : 3 * head + 2]
        own = own + ours[:, 3 * head + 2 : 3 * head + 3]
        far = theirs[:, 3 * head : 3 * head + 1] + theirs[:, 3 * head + 1 : 3 * head + 2]
        far = far + theirs[:, 3 * head + 2 : 3 * head + 3]
        top = jnp.maximum(own, far)
        own = jnp.exp(own - top)
        far = jnp.exp(far - top)
        share = jnp.where(lane == head, own / (own + far), share)
    mixed = (keep * share + got * (1.0 - share)).astype(BF16)
    result = jnp.dot(mixed, wo_ref[...], preferred_element_type=F32).astype(BF16)
    out_ref[...] = result.reshape(out_ref.shape)


def finished(keep, lse, got, w_out):
    vmem = pl.BlockSpec(memory_space=pltpu.VMEM)
    return pl.pallas_call(
        finish_kernel,
        out_shape=jax.ShapeDtypeStruct(keep.shape, BF16),
        in_specs=[vmem] * 4,
        out_specs=vmem,
        name="finish",
    )(keep, lse, got, w_out)


def gathered(block, masks):
    blocks = {(0, 0): block}
    for size in range(1, len(masks) + 1):
        for start in range(len(masks)):
            if size == len(masks) and start > 0:
                break
            chosen = [masks[(start + k) % len(masks)] for k in range(size)]
            key = (0, 0)
            for mask in chosen:
                key = (key[0] ^ mask[0], key[1] ^ mask[1])
            step = chosen[-1]
            before = (key[0] ^ step[0], key[1] ^ step[1])
            if key not in blocks:
                blocks[key] = exchange(blocks[before], *step)
    return blocks


def halves(state_field, support_rows, window_bands, conv_weight, w_query, w_key, w_value, w_out):
    lats = lax.axis_size("lat")
    lat, lon = lax.axis_index("lat"), lax.axis_index("lon")
    channels, rows, lons = state_field.shape
    lat_tile = support_rows.shape[0]
    bands = lat_tile // 2
    lon_tile = lons // 2
    band_total = lat_tile * lats
    half = lats // 2

    other = exchange(state_field, 0, 1)
    top = jnp.transpose(state_field[:, :2], (1, 0, 2))
    bottom = jnp.transpose(state_field[:, rows - 2 :], (1, 0, 2))
    edge = vertical(jnp.where(lon == 0, bottom, top), 0)
    edge_other = vertical(jnp.where(lon == 0, top, bottom), 1)
    row_index = 2 * jnp.arange(lat_tile, dtype=jnp.int32)[:, None] + support_rows + 2
    row_index = lax.dynamic_slice_in_dim(row_index, lon * bands, bands, axis=0)
    features = features_of(state_field, other, edge, edge_other, row_index, conv_weight)

    masks = [(0, 1)] + [(1 << k, 0) for k in range(1, half.bit_length() - 1)]
    blocks = gathered(features, masks)
    order = [(i, j) for i in range(0, half, 2) for j in range(2)]
    near = jnp.concatenate([blocks[key] for key in order], axis=0)
    far = exchange(near, 1, 0)

    size = bands * lons
    slot_count = window_bands.shape[0] // lats
    pair_slots = jnp.concatenate(
        [(lat % half + k * half) * slot_count + jnp.arange(slot_count) for k in range(2)]
    )
    wanted = window_bands[pair_slots]
    owner = wanted // lat_tile
    owner_lon = (wanted % lat_tile) // bands
    apart = (owner ^ lat) % half
    place = ((apart - apart % 2) + (owner_lon ^ lon)) * size
    place = place + (wanted % bands) * lons + (owner_lon ^ lon) * lon_tile
    kind = jnp.where(owner // half == lat // half, apart % 2, 2)
    where = jnp.stack([kind, place], axis=1).astype(jnp.int32)
    sel = selected(where, near, far, lon_tile)
    got = exchange(sel, half, 0)

    masks_lat = jnp.array([i + core for core in range(2) for i, j in order], jnp.int32)
    masks_lon = jnp.array([j for core in range(2) for i, j in order], jnp.int32)
    first = (lat ^ masks_lat) * lat_tile + (lon ^ masks_lon) * bands
    key_band = first[:, None] + jnp.arange(bands, dtype=jnp.int32)[None, :]
    area = jnp.repeat(log_area(key_band.reshape(-1), band_total), lons)[None, :]
    mine = (lat // half).astype(jnp.int32).reshape(1)
    send, keep, lse = attended(mine, sel, got, near, far, area, w_query, w_key, w_value)
    return finished(keep, lse, exchange(send, half, 0), w_out)


def solution(mesh):
    lats, lons = mesh.shape["lat"], mesh.shape["lon"]
    paired = lons == 2 and lats >= 4 and lats & (lats - 1) == 0
    return jax.shard_map(
        halves if paired else general,
        mesh=mesh,
        in_specs=(P(None, "lat", "lon"), P("lat", None), P(), P(), P(), P(), P(), P()),
        out_specs=P("lat", "lon", None),
        check_vma=False,
    )
```

```python
import math

import jax
import jax.numpy as jnp
from jax import lax
from jax.experimental import pallas as pl
from jax.experimental.pallas import tpu as pltpu
from jax.sharding import PartitionSpec as P

D = 256
H = 4
AXES = ("lat", "lon")
F32 = jnp.float32
BF16 = jnp.bfloat16


def padded(x, sides, width):
    for axis, dim in sides:
        devices, length = (lax.axis_size(axis), x.shape[dim])
        up = [(i, (i + 1) % devices) for i in range(devices - 1)]
        down = [(j, i) for i, j in up]
        last = lax.slice_in_dim(x, length - width, length, axis=dim)
        leading = lax.slice_in_dim(x, 0, width, axis=dim)
        before = lax.ppermute(last, axis, up)
        after = lax.ppermute(leading, axis, down)
        x = jnp.concatenate([before, x, after], axis=dim)
    return x


def shifted(x, axis, by):
    devices = lax.axis_size(axis)
    return lax.ppermute(x, axis, [(i, (i + by) % devices) for i in range(devices)])


def conv_features(extended, support_rows, conv_weight):
    bands = support_rows.shape[0]
    width = (extended.shape[2] - 1) // 2
    row_index = 2 * jnp.arange(bands, dtype=jnp.int32)[:, None] + support_rows + 2
    picked = jnp.take(extended, row_index, axis=1)
    tapped = jnp.stack(
        [picked[..., column_tap : column_tap + 2 * width : 2] for column_tap in range(3)], axis=3
    )
    patches = jnp.transpose(tapped, (1, 4, 2, 3, 0)).reshape(bands * width, -1)
    raw = jnp.dot(
        patches, conv_weight.reshape(-1, conv_weight.shape[-1]), preferred_element_type=F32
    )
    factor = lax.rsqrt(jnp.mean(raw * raw, axis=-1, keepdims=True) + 1e-06)
    return (raw * factor).astype(BF16).reshape(bands, width, -1)


def absorb(carry, block_keys, block_values, block_area, queries, scale):
    running_max, running_sum, mixed = carry
    scores = (
        jnp.einsum("qhd,khd->qhk", queries, block_keys, preferred_element_type=F32) * scale
        + block_area
    )
    new_max = jnp.maximum(running_max, jnp.max(scores, axis=-1))
    factor = jnp.exp(running_max - new_max)
    weights = jnp.exp(scores - new_max[..., None])
    running_sum = running_sum * factor + jnp.sum(weights, axis=-1)
    update = jnp.einsum(
        "qhk,khd->qhd", weights.astype(BF16), block_values, preferred_element_type=F32
    )
    mixed = mixed * factor[..., None] + update
    return (new_max, running_sum, mixed)


def sweep(carry, keys, values, queries, band_total):
    rows = keys.shape[0]
    lon_tile = keys.shape[1]
    head_size = D // H
    band_block = math.gcd(rows, max(1, 512 // lon_tile))
    blocks = rows // band_block
    block_len = band_block * lon_tile
    keys_blocks = keys.reshape(blocks, block_len, H, head_size)
    values_blocks = values.reshape(blocks, block_len, H, head_size)
    band_index = jnp.arange(rows, dtype=jnp.int32)
    area_rows = jnp.repeat(log_area(band_index, band_total), lon_tile).reshape(blocks, block_len)
    scale = 1.0 / math.sqrt(head_size)

    def step_block(state, inputs):
        return (absorb(state, inputs[0], inputs[1], inputs[2], queries, scale), None)

    result, unused = lax.scan(step_block, carry, (keys_blocks, values_blocks, area_rows))
    return result


def log_area(bands, band_total):
    centre = (bands.astype(F32) + 0.5) * (math.pi / band_total) - math.pi / 2
    return jnp.log(jnp.cos(centre))


def general(state_field, support_rows, window_bands, conv_weight, w_query, w_key, w_value, w_out):
    lat_tile = support_rows.shape[0]
    lon_tile = state_field.shape[2] // 2
    whole_lon = lon_tile * lax.axis_size("lon")
    band_total = lat_tile * lax.axis_size("lat")
    head_size = D // H
    extended = padded(state_field, (("lat", 1),), 2)
    western = shifted(extended[:, :, -1:], "lon", 1)
    extended = jnp.concatenate([western, extended], axis=2)
    features = conv_features(extended, support_rows, conv_weight)
    slot_count = window_bands.shape[0] // lax.axis_size("lat")
    piece = lax.all_gather(features, "lat", axis=0, tiled=True)
    mine = lax.dynamic_slice_in_dim(
        window_bands, lax.axis_index("lat") * slot_count, slot_count, axis=0
    )
    picked = jnp.take(piece, mine, axis=0)
    gathered = lax.all_gather(picked, "lon", axis=1, tiled=True)
    query_count = slot_count * whole_lon
    queries = jnp.dot(gathered.reshape(query_count, D), w_query, preferred_element_type=F32)
    queries = queries.astype(BF16).reshape(query_count, H, head_size)
    initial = (
        jnp.full((query_count, H), -1e30, F32),
        jnp.zeros((query_count, H), F32),
        jnp.zeros((query_count, H, head_size), F32),
    )
    piece_rows = piece.reshape(-1, D)
    keys = jnp.dot(piece_rows, w_key, preferred_element_type=F32).astype(BF16)
    values = jnp.dot(piece_rows, w_value, preferred_element_type=F32).astype(BF16)
    running_max, running_sum, mixed = sweep(
        initial, keys.reshape(piece.shape), values.reshape(piece.shape), queries, band_total
    )
    best = lax.pmax(running_max, "lon")
    factor = jnp.exp(running_max - best)
    scaled_mix = (mixed * factor[..., None]).reshape(slot_count, whole_lon, D)
    scaled_sum = (running_sum * factor).reshape(slot_count, whole_lon, H)
    mix_share, sum_share = (
        lax.psum_scatter(part.astype(BF16), "lon", scatter_dimension=1, tiled=True).astype(F32)
        for part in (scaled_mix, scaled_sum)
    )
    attended = mix_share.reshape(slot_count, lon_tile, H, head_size) / sum_share[..., None]
    attended = attended.astype(BF16).reshape(slot_count * lon_tile, D)
    result = jnp.dot(attended, w_out, preferred_element_type=F32).astype(BF16)
    return result.reshape(slot_count, lon_tile, D)


def exchange(x, lat_mask, lon_mask):
    lats, lons = lax.axis_size("lat"), lax.axis_size("lon")
    pairs = [
        (i * lons + j, (i ^ lat_mask) * lons + (j ^ lon_mask))
        for i in range(lats)
        for j in range(lons)
    ]
    return lax.ppermute(x, AXES, pairs)


def vertical(x, cross):
    lats, lons = lax.axis_size("lat"), lax.axis_size("lon")
    pairs = []
    for i in range(lats):
        for j in range(lons):
            source = i - 1 if j == 0 else i + 1
            if 0 <= source < lats:
                pairs.append((source * lons + (j ^ cross), i * lons + j))
    return lax.ppermute(x, AXES, pairs)


def conv_kernel(
    rows_ref, own_ref, other_ref, edge_ref, edge_other_ref, weight_ref, out_ref,
    strided, taken, patches, weights,
):
    channels, rows, lons = own_ref.shape
    slots, taps = weight_ref.shape[:2]
    deep = taken.shape[1]
    width = lons
    bands = out_ref.shape[0] // width
    tail = jnp.zeros(((deep - channels) * rows, lons), F32)
    for side, ref in enumerate((own_ref, other_ref)):
        strided[side, 0 : channels * rows] = ref[...].astype(F32).reshape(channels * rows, lons)
        strided[side, channels * rows :] = tail
    column = lax.broadcasted_iota(jnp.int32, (2 * lons, taps * width), 0)
    place = lax.broadcasted_iota(jnp.int32, (2 * lons, taps * width), 1)
    wanted = lax.rem(2 * (place % width) + place // width - 1 + 2 * lons, 2 * lons)
    choose = (column == wanted).astype(F32).astype(BF16)
    lines = []
    for row in range(rows):
        lines.append(
            jnp.concatenate(
                [strided[side, pl.ds(row, deep, stride=rows), :] for side in range(2)], axis=1
            )
        )
    edge_rows = edge_ref.shape[0]
    short = jnp.zeros((deep - channels, 2 * lons), F32)
    for row in range(edge_rows):
        line = jnp.concatenate(
            [edge_ref[row].astype(F32), edge_other_ref[row].astype(F32)], axis=1
        )
        lines.append(jnp.concatenate([line, short], axis=0))
    split = jnp.dot(
        jnp.concatenate(lines, axis=0).astype(BF16), choose, preferred_element_type=F32
    ).astype(BF16)
    for row in range(rows):
        taken[edge_rows + row] = split[row * deep : (row + 1) * deep]
    for row in range(edge_rows):
        piece = split[(rows + row) * deep : (rows + row + 1) * deep]
        taken[row] = piece
        taken[edge_rows + rows + row] = piece
    blank = jnp.zeros((deep - channels, weight_ref.shape[3]), BF16)
    for slot in range(slots):
        for band in range(bands):
            line = taken[rows_ref[band, slot]]
            for tap in range(taps):
                at = (slot * taps + tap) * deep
                patches[at : at + deep, band * width : (band + 1) * width] = line[
                    :, tap * width : (tap + 1) * width
                ]
        for tap in range(taps):
            at = (slot * taps + tap) * deep
            weights[at : at + deep] = jnp.concatenate([weight_ref[slot, tap], blank], axis=0)
    raw = lax.dot_general(
        patches[...], weights[...], (((0,), (0,)), ((), ())), preferred_element_type=F32
    )
    factor = lax.rsqrt(jnp.mean(raw * raw, axis=-1, keepdims=True) + 1e-06)
    out_ref[...] = (raw * factor).astype(BF16)


def features_of(own, other, edge, edge_other, row_index, conv_weight):
    channels, rows, lons = own.shape
    slots, taps, _, width = conv_weight.shape
    bands = row_index.shape[0]
    deep = -(-channels // 16) * 16
    vmem = pl.BlockSpec(memory_space=pltpu.VMEM)
    return pl.pallas_call(
        conv_kernel,
        out_shape=jax.ShapeDtypeStruct((bands * lons, width), BF16),
        in_specs=[pl.BlockSpec(memory_space=pltpu.SMEM)] + [vmem] * 5,
        out_specs=vmem,
        scratch_shapes=[
            pltpu.VMEM((2, deep * rows, lons), F32),
            pltpu.VMEM((rows + 2 * edge.shape[0], deep, taps * lons), BF16),
            pltpu.VMEM((slots * taps * deep, bands * lons), BF16),
            pltpu.VMEM((slots * taps * deep, width), BF16),
        ],
        compiler_params=pltpu.CompilerParams(vmem_limit_bytes=12 * 2**20),
        cost_estimate=pl.CostEstimate(
            flops=2 * slots * taps * deep * bands * lons * width,
            bytes_accessed=2 * (conv_weight.size + 2 * own.size),
            transcendentals=0,
        ),
        name="conv",
    )(row_index, own, other, edge, edge_other, conv_weight)


def select_kernel(where_ref, near_ref, far_ref, out_ref):
    slots, rows, _ = out_ref.shape
    for slot in range(slots):
        kind = where_ref[slot, 0]
        start = pl.multiple_of(where_ref[slot, 1], rows)

        @pl.when(kind == 0)
        def _():
            out_ref[slot] = near_ref[pl.ds(start, rows)]

        @pl.when(kind == 1)
        def _():
            out_ref[slot] = far_ref[pl.ds(start, rows)]

        @pl.when(kind == 2)
        def _():
            out_ref[slot] = jnp.zeros(out_ref.shape[1:], out_ref.dtype)


def selected(where, near, far, rows):
    slots = where.shape[0]
    vmem = pl.BlockSpec(memory_space=pltpu.VMEM)
    return pl.pallas_call(
        select_kernel,
        out_shape=jax.ShapeDtypeStruct((slots, rows, near.shape[1]), near.dtype),
        in_specs=[pl.BlockSpec(memory_space=pltpu.SMEM), vmem, vmem],
        out_specs=vmem,
        compiler_params=pltpu.CompilerParams(vmem_limit_bytes=2**20 + 2 * 2 * near.size),
        name="select",
    )(where, near, far)


def split3(x):
    high = x.astype(BF16).astype(F32)
    middle = (x - high).astype(BF16).astype(F32)
    return high, middle, x - high - middle


def attend_kernel(
    mine_ref, sel_ref, got_ref, near_ref, far_ref, area_ref, wq_ref, wk_ref, wv_ref,
    send_ref, keep_ref, lse_ref, scores, outs, lses,
):
    slots, rows, width = sel_ref.shape
    count = slots * rows
    head_size = width // H
    half = near_ref.shape[0]
    chunk = math.gcd(half, 512)
    token = (sel_ref[...] + got_ref[...]).reshape(count, width)
    query = jnp.dot(token, wq_ref[...], preferred_element_type=F32).astype(BF16).astype(F32)
    query = query * (1.0 / math.sqrt(head_size))
    lane = lax.broadcasted_iota(jnp.int32, (1, width), 1) // head_size
    spread = jnp.concatenate(
        [jnp.where(lane == head, query, 0.0) for head in range(H)], axis=0
    ).astype(BF16)
    turned = lax.dot_general(
        spread, wk_ref[...], (((1,), (1,)), ((), ())), preferred_element_type=F32
    ).astype(BF16)
    parts = [(ref, at) for ref in (near_ref, far_ref) for at in range(0, half, chunk)]
    best = jnp.full((H * count, 128), -jnp.inf, F32)
    for index, (ref, at) in enumerate(parts):
        block = lax.dot_general(
            turned, ref[at : at + chunk], (((1,), (1,)), ((), ())), preferred_element_type=F32
        )
        block = block + area_ref[:, index * chunk : (index + 1) * chunk]
        scores[:, index * chunk : (index + 1) * chunk] = block
        for lanes in range(0, chunk, 128):
            best = jnp.maximum(best, block[:, lanes : lanes + 128])
    top = jnp.max(best, axis=1, keepdims=True)
    total = jnp.zeros((H * count, 128), F32)
    mixed = jnp.zeros((H * count, width), F32)
    for index, (ref, at) in enumerate(parts):
        weight = jnp.exp(scores[:, index * chunk : (index + 1) * chunk] - top)
        for lanes in range(0, chunk, 128):
            total = total + weight[:, lanes : lanes + 128]
        mixed = mixed + jnp.dot(
            weight.astype(BF16), ref[at : at + chunk], preferred_element_type=F32
        )
    total = jnp.sum(total, axis=1, keepdims=True)
    value = jnp.dot((mixed / total).astype(BF16), wv_ref[...], preferred_element_type=F32)
    lse = top + jnp.log(total)
    out = jnp.zeros((count, width), F32)
    stat_lane = lax.broadcasted_iota(jnp.int32, (1, 128), 1)
    stats = jnp.zeros((count, 128), F32)
    for head in range(H):
        out = jnp.where(lane == head, value[head * count : (head + 1) * count], out)
        for order, piece in enumerate(split3(lse[head * count : (head + 1) * count])):
            stats = jnp.where(stat_lane == 3 * head + order, piece, stats)
    outs[...] = out.reshape(outs.shape)
    lses[...] = stats.reshape(lses.shape)
    own = mine_ref[0]
    half_slots = slots // 2
    keep_ref[...] = outs[pl.ds(own * half_slots, half_slots)]
    lse_ref[...] = lses[pl.ds(own * half_slots, half_slots)]
    send_ref[:, :, 0:width] = outs[pl.ds((1 - own) * half_slots, half_slots)].astype(BF16)
    send_ref[:, :, width:] = lses[pl.ds((1 - own) * half_slots, half_slots)].astype(BF16)


def attended(mine, sel, got, near, far, area, w_query, w_key, w_value):
    slots, rows, width = sel.shape
    keys = near.shape[0] + far.shape[0]
    count = slots * rows
    vmem = pl.BlockSpec(memory_space=pltpu.VMEM)
    half_slots = slots // 2
    return pl.pallas_call(
        attend_kernel,
        out_shape=(
            jax.ShapeDtypeStruct((half_slots, rows, width + 128), BF16),
            jax.ShapeDtypeStruct((half_slots, rows, width), F32),
            jax.ShapeDtypeStruct((half_slots, rows, 128), F32),
        ),
        in_specs=[pl.BlockSpec(memory_space=pltpu.SMEM)] + [vmem] * 8,
        out_specs=(vmem, vmem, vmem),
        scratch_shapes=[
            pltpu.VMEM((H * count, keys), F32),
            pltpu.VMEM((slots, rows, width), F32),
            pltpu.VMEM((slots, rows, 128), F32),
        ],
        compiler_params=pltpu.CompilerParams(vmem_limit_bytes=24 * 2**20),
        cost_estimate=pl.CostEstimate(
            flops=4 * H * count * keys * width,
            bytes_accessed=2 * keys * width,
            transcendentals=H * count * keys,
        ),
        name="attend",
    )(mine, sel, got, near, far, area, w_query, w_key, w_value)


def finish_kernel(keep_ref, lse_ref, got_ref, wo_ref, out_ref):
    slots, rows, width = keep_ref.shape
    head_size = width // H
    count = slots * rows
    keep = keep_ref[...].reshape(count, width)
    got = got_ref[:, :, 0:width].astype(F32).reshape(count, width)
    ours = lse_ref[...].reshape(count, 128)
    theirs = got_ref[:, :, width:].astype(F32).reshape(count, 128)
    lane = lax.broadcasted_iota(jnp.int32, (1, width), 1) // head_size
    share = jnp.zeros((count, width), F32)
    for head in range(H):
        own = ours[:, 3 * head : 3 * head + 1] + ours[:, 3 * head + 1 : 3 * head + 2]
        own = own + ours[:, 3 * head + 2 : 3 * head + 3]
        far = theirs[:, 3 * head : 3 * head + 1] + theirs[:, 3 * head + 1 : 3 * head + 2]
        far = far + theirs[:, 3 * head + 2 : 3 * head + 3]
        top = jnp.maximum(own, far)
        own = jnp.exp(own - top)
        far = jnp.exp(far - top)
        share = jnp.where(lane == head, own / (own + far), share)
    mixed = (keep * share + got * (1.0 - share)).astype(BF16)
    result = jnp.dot(mixed, wo_ref[...], preferred_element_type=F32).astype(BF16)
    out_ref[...] = result.reshape(out_ref.shape)


def finished(keep, lse, got, w_out):
    vmem = pl.BlockSpec(memory_space=pltpu.VMEM)
    return pl.pallas_call(
        finish_kernel,
        out_shape=jax.ShapeDtypeStruct(keep.shape, BF16),
        in_specs=[vmem] * 4,
        out_specs=vmem,
        compiler_params=pltpu.CompilerParams(vmem_limit_bytes=4 * 2**20),
        name="finish",
    )(keep, lse, got, w_out)


def gathered(block, masks):
    blocks = {(0, 0): block}
    for size in range(1, len(masks) + 1):
        for start in range(len(masks)):
            if size == len(masks) and start > 0:
                break
            chosen = [masks[(start + k) % len(masks)] for k in range(size)]
            key = (0, 0)
            for mask in chosen:
                key = (key[0] ^ mask[0], key[1] ^ mask[1])
            step = chosen[-1]
            before = (key[0] ^ step[0], key[1] ^ step[1])
            if key not in blocks:
                blocks[key] = exchange(blocks[before], *step)
    return blocks


def halves(state_field, support_rows, window_bands, conv_weight, w_query, w_key, w_value, w_out):
    lats = lax.axis_size("lat")
    lat, lon = lax.axis_index("lat"), lax.axis_index("lon")
    channels, rows, lons = state_field.shape
    lat_tile = support_rows.shape[0]
    bands = lat_tile // 2
    lon_tile = lons // 2
    band_total = lat_tile * lats
    half = lats // 2

    other = exchange(state_field, 0, 1)
    top = jnp.transpose(state_field[:, :2], (1, 0, 2))
    bottom = jnp.transpose(state_field[:, rows - 2 :], (1, 0, 2))
    edge = vertical(jnp.where(lon == 0, bottom, top), 0)
    edge_other = vertical(jnp.where(lon == 0, top, bottom), 1)
    row_index = 2 * jnp.arange(lat_tile, dtype=jnp.int32)[:, None] + support_rows + 2
    row_index = lax.dynamic_slice_in_dim(row_index, lon * bands, bands, axis=0)
    features = features_of(state_field, other, edge, edge_other, row_index, conv_weight)

    masks = [(0, 1)] + [(1 << k, 0) for k in range(1, half.bit_length() - 1)]
    blocks = gathered(features, masks)
    order = [(i, j) for i in range(0, half, 2) for j in range(2)]
    near = jnp.concatenate([blocks[key] for key in order], axis=0)
    far = exchange(near, 1, 0)

    size = bands * lons
    slot_count = window_bands.shape[0] // lats
    pair_slots = jnp.concatenate(
        [(lat % half + k * half) * slot_count + jnp.arange(slot_count) for k in range(2)]
    )
    wanted = window_bands[pair_slots]
    owner = wanted // lat_tile
    owner_lon = (wanted % lat_tile) // bands
    apart = (owner ^ lat) % half
    place = ((apart - apart % 2) + (owner_lon ^ lon)) * size
    place = place + (wanted % bands) * lons + (owner_lon ^ lon) * lon_tile
    kind = jnp.where(owner // half == lat // half, apart % 2, 2)
    where = jnp.stack([kind, place], axis=1).astype(jnp.int32)
    sel = selected(where, near, far, lon_tile)
    got = exchange(sel, half, 0)

    masks_lat = jnp.array([i + core for core in range(2) for i, j in order], jnp.int32)
    masks_lon = jnp.array([j for core in range(2) for i, j in order], jnp.int32)
    first = (lat ^ masks_lat) * lat_tile + (lon ^ masks_lon) * bands
    key_band = first[:, None] + jnp.arange(bands, dtype=jnp.int32)[None, :]
    area = jnp.repeat(log_area(key_band.reshape(-1), band_total), lons)[None, :]
    mine = (lat // half).astype(jnp.int32).reshape(1)
    send, keep, lse = attended(mine, sel, got, near, far, area, w_query, w_key, w_value)
    return finished(keep, lse, exchange(send, half, 0), w_out)


def solution(mesh):
    lats, lons = mesh.shape["lat"], mesh.shape["lon"]
    paired = lons == 2 and lats >= 4 and lats & (lats - 1) == 0
    return jax.shard_map(
        halves if paired else general,
        mesh=mesh,
        in_specs=(P(None, "lat", "lon"), P("lat", None), P(), P(), P(), P(), P(), P()),
        out_specs=P("lat", "lon", None),
        check_vma=False,
    )
```

```python
import functools
import math

import jax
import jax.numpy as jnp
from jax import lax
from jax.experimental import pallas as pl
from jax.experimental.pallas import tpu as pltpu
from jax.sharding import PartitionSpec as P

D = 256
H = 4
AXES = ("lat", "lon")
LOG2E = 1.0 / math.log(2.0)
F32 = jnp.float32
BF16 = jnp.bfloat16


def padded(x, sides, width):
    for axis, dim in sides:
        devices, length = (lax.axis_size(axis), x.shape[dim])
        up = [(i, (i + 1) % devices) for i in range(devices - 1)]
        down = [(j, i) for i, j in up]
        last = lax.slice_in_dim(x, length - width, length, axis=dim)
        leading = lax.slice_in_dim(x, 0, width, axis=dim)
        before = lax.ppermute(last, axis, up)
        after = lax.ppermute(leading, axis, down)
        x = jnp.concatenate([before, x, after], axis=dim)
    return x


def shifted(x, axis, by):
    devices = lax.axis_size(axis)
    return lax.ppermute(x, axis, [(i, (i + by) % devices) for i in range(devices)])


def conv_features(extended, support_rows, conv_weight):
    bands = support_rows.shape[0]
    width = (extended.shape[2] - 1) // 2
    row_index = 2 * jnp.arange(bands, dtype=jnp.int32)[:, None] + support_rows + 2
    picked = jnp.take(extended, row_index, axis=1)
    tapped = jnp.stack(
        [picked[..., column_tap : column_tap + 2 * width : 2] for column_tap in range(3)], axis=3
    )
    patches = jnp.transpose(tapped, (1, 4, 2, 3, 0)).reshape(bands * width, -1)
    raw = jnp.dot(
        patches, conv_weight.reshape(-1, conv_weight.shape[-1]), preferred_element_type=F32
    )
    factor = lax.rsqrt(jnp.mean(raw * raw, axis=-1, keepdims=True) + 1e-06)
    return (raw * factor).astype(BF16).reshape(bands, width, -1)


def absorb(carry, block_keys, block_values, block_area, queries, scale):
    running_max, running_sum, mixed = carry
    scores = (
        jnp.einsum("qhd,khd->qhk", queries, block_keys, preferred_element_type=F32) * scale
        + block_area
    )
    new_max = jnp.maximum(running_max, jnp.max(scores, axis=-1))
    factor = jnp.exp(running_max - new_max)
    weights = jnp.exp(scores - new_max[..., None])
    running_sum = running_sum * factor + jnp.sum(weights, axis=-1)
    update = jnp.einsum(
        "qhk,khd->qhd", weights.astype(BF16), block_values, preferred_element_type=F32
    )
    mixed = mixed * factor[..., None] + update
    return (new_max, running_sum, mixed)


def sweep(carry, keys, values, queries, band_total):
    rows = keys.shape[0]
    lon_tile = keys.shape[1]
    head_size = D // H
    band_block = math.gcd(rows, max(1, 512 // lon_tile))
    blocks = rows // band_block
    block_len = band_block * lon_tile
    keys_blocks = keys.reshape(blocks, block_len, H, head_size)
    values_blocks = values.reshape(blocks, block_len, H, head_size)
    band_index = jnp.arange(rows, dtype=jnp.int32)
    area_rows = jnp.repeat(log_area(band_index, band_total), lon_tile).reshape(blocks, block_len)
    scale = 1.0 / math.sqrt(head_size)

    def step_block(state, inputs):
        return (absorb(state, inputs[0], inputs[1], inputs[2], queries, scale), None)

    result, unused = lax.scan(step_block, carry, (keys_blocks, values_blocks, area_rows))
    return result


def log_area(bands, band_total):
    centre = (bands.astype(F32) + 0.5) * (math.pi / band_total) - math.pi / 2
    return jnp.log(jnp.cos(centre))


def general(state_field, support_rows, window_bands, conv_weight, w_query, w_key, w_value, w_out):
    lat_tile = support_rows.shape[0]
    lon_tile = state_field.shape[2] // 2
    whole_lon = lon_tile * lax.axis_size("lon")
    band_total = lat_tile * lax.axis_size("lat")
    head_size = D // H
    extended = padded(state_field, (("lat", 1),), 2)
    western = shifted(extended[:, :, -1:], "lon", 1)
    extended = jnp.concatenate([western, extended], axis=2)
    features = conv_features(extended, support_rows, conv_weight)
    slot_count = window_bands.shape[0] // lax.axis_size("lat")
    piece = lax.all_gather(features, "lat", axis=0, tiled=True)
    mine = lax.dynamic_slice_in_dim(
        window_bands, lax.axis_index("lat") * slot_count, slot_count, axis=0
    )
    picked = jnp.take(piece, mine, axis=0)
    gathered = lax.all_gather(picked, "lon", axis=1, tiled=True)
    query_count = slot_count * whole_lon
    queries = jnp.dot(gathered.reshape(query_count, D), w_query, preferred_element_type=F32)
    queries = queries.astype(BF16).reshape(query_count, H, head_size)
    initial = (
        jnp.full((query_count, H), -1e30, F32),
        jnp.zeros((query_count, H), F32),
        jnp.zeros((query_count, H, head_size), F32),
    )
    piece_rows = piece.reshape(-1, D)
    keys = jnp.dot(piece_rows, w_key, preferred_element_type=F32).astype(BF16)
    values = jnp.dot(piece_rows, w_value, preferred_element_type=F32).astype(BF16)
    running_max, running_sum, mixed = sweep(
        initial, keys.reshape(piece.shape), values.reshape(piece.shape), queries, band_total
    )
    best = lax.pmax(running_max, "lon")
    factor = jnp.exp(running_max - best)
    scaled_mix = (mixed * factor[..., None]).reshape(slot_count, whole_lon, D)
    scaled_sum = (running_sum * factor).reshape(slot_count, whole_lon, H)
    mix_share, sum_share = (
        lax.psum_scatter(part.astype(BF16), "lon", scatter_dimension=1, tiled=True).astype(F32)
        for part in (scaled_mix, scaled_sum)
    )
    attended = mix_share.reshape(slot_count, lon_tile, H, head_size) / sum_share[..., None]
    attended = attended.astype(BF16).reshape(slot_count * lon_tile, D)
    result = jnp.dot(attended, w_out, preferred_element_type=F32).astype(BF16)
    return result.reshape(slot_count, lon_tile, D)


def exchange(x, lat_mask, lon_mask):
    lats, lons = lax.axis_size("lat"), lax.axis_size("lon")
    pairs = [
        (i * lons + j, (i ^ lat_mask) * lons + (j ^ lon_mask))
        for i in range(lats)
        for j in range(lons)
    ]
    return lax.ppermute(x, AXES, pairs)


def vertical(x):
    lats, lons = lax.axis_size("lat"), lax.axis_size("lon")
    pairs = []
    for i in range(1, lats):
        j = i % lons
        pairs += [((i - 1) * lons + j, i * lons + j), (i * lons + j, (i - 1) * lons + j)]
    return lax.ppermute(x, AXES, pairs)


def lines_of(ref, strided, deep):
    channels, rows, lons = ref.shape
    strided[0 : channels * rows] = ref[...].astype(F32).reshape(channels * rows, lons)
    strided[channels * rows :] = jnp.zeros(((deep - channels) * rows, lons), F32)
    return [strided[pl.ds(row, deep, stride=rows), :].astype(BF16) for row in range(rows)]


def rows_kernel(lower_ref, own_ref, lines_ref, same_ref, cross_ref, strided):
    rows, deep, _ = lines_ref.shape
    edge = same_ref.shape[0]
    lines = lines_of(own_ref, strided, deep)
    for row in range(rows):
        lines_ref[row] = lines[row]
    lower = lower_ref[0] != 0
    for row in range(edge):
        top, bottom = lines[row], lines[rows - edge + row]
        same_ref[row] = jnp.where(lower, bottom, top)
        cross_ref[row] = jnp.where(lower, top, bottom)


def rows_of(lower, own, edge, deep):
    _, rows, lons = own.shape
    vmem = pl.BlockSpec(memory_space=pltpu.VMEM)
    return pl.pallas_call(
        rows_kernel,
        out_shape=(
            jax.ShapeDtypeStruct((rows, deep, lons), BF16),
            jax.ShapeDtypeStruct((edge, deep, lons), BF16),
            jax.ShapeDtypeStruct((edge, deep, lons), BF16),
        ),
        in_specs=[pl.BlockSpec(memory_space=pltpu.SMEM), vmem],
        out_specs=(vmem, vmem, vmem),
        scratch_shapes=[pltpu.VMEM((deep * rows, lons), F32)],
        compiler_params=pltpu.CompilerParams(vmem_limit_bytes=4 * 2**20),
        name="rows",
    )(lower, own)


def weights_kernel(weight_ref, out_ref):
    slots, taps, channels, width = weight_ref.shape
    deep = out_ref.shape[0] // (slots * taps)
    blank = jnp.zeros((deep - channels, width), BF16)
    for slot in range(slots):
        for tap in range(taps):
            at = (slot * taps + tap) * deep
            out_ref[at : at + deep] = jnp.concatenate([weight_ref[slot, tap], blank], axis=0)


def weights_of(conv_weight, deep):
    slots, taps, _, width = conv_weight.shape
    vmem = pl.BlockSpec(memory_space=pltpu.VMEM)
    return pl.pallas_call(
        weights_kernel,
        out_shape=jax.ShapeDtypeStruct((slots * taps * deep, width), BF16),
        in_specs=[vmem],
        out_specs=vmem,
        compiler_params=pltpu.CompilerParams(vmem_limit_bytes=4 * 2**20),
        cost_estimate=pl.CostEstimate(
            flops=0, bytes_accessed=4 * conv_weight.size, transcendentals=0
        ),
        name="weights",
    )(conv_weight)


def conv_kernel(
    rows_ref, own_ref, other_ref, edge_ref, weight_ref, out_ref, taken, patches
):
    rows, deep, lons = own_ref.shape
    edge = edge_ref.shape[0] // 2
    width = lons
    bands = out_ref.shape[0] // width
    slots = rows_ref.shape[1]
    taps = weight_ref.shape[0] // (slots * deep)
    column = lax.broadcasted_iota(jnp.int32, (2 * lons, taps * width), 0)
    place = lax.broadcasted_iota(jnp.int32, (2 * lons, taps * width), 1)
    wanted = lax.rem(2 * (place % width) + place // width - 1 + 2 * lons, 2 * lons)
    choose = (column == wanted).astype(F32).astype(BF16)
    near = [own_ref[row] for row in range(rows)] + [edge_ref[row] for row in range(edge)]
    far = [other_ref[row] for row in range(rows)] + [edge_ref[edge + row] for row in range(edge)]
    both = jnp.concatenate(
        [jnp.concatenate(near, axis=0), jnp.concatenate(far, axis=0)], axis=1
    )
    split = jnp.dot(both, choose, preferred_element_type=F32).astype(BF16)
    for row in range(rows):
        taken[edge + row] = split[row * deep : (row + 1) * deep]
    for row in range(edge):
        piece = split[(rows + row) * deep : (rows + row + 1) * deep]
        taken[row] = piece
        taken[edge + rows + row] = piece
    for slot in range(slots):
        for band in range(bands):
            line = taken[rows_ref[band, slot]]
            for tap in range(taps):
                at = (slot * taps + tap) * deep
                patches[at : at + deep, band * width : (band + 1) * width] = line[
                    :, tap * width : (tap + 1) * width
                ]
    raw = lax.dot_general(
        patches[...], weight_ref[...], (((0,), (0,)), ((), ())), preferred_element_type=F32
    )
    factor = lax.rsqrt(jnp.mean(raw * raw, axis=-1, keepdims=True) + 1e-06)
    out_ref[...] = (raw * factor).astype(BF16)


def features_of(own, other, edge, row_index, weights):
    rows, deep, lons = own.shape
    width = weights.shape[1]
    bands = row_index.shape[0]
    taps = weights.shape[0] // (row_index.shape[1] * deep)
    vmem = pl.BlockSpec(memory_space=pltpu.VMEM)
    return pl.pallas_call(
        conv_kernel,
        out_shape=jax.ShapeDtypeStruct((bands * lons, width), BF16),
        in_specs=[pl.BlockSpec(memory_space=pltpu.SMEM)] + [vmem] * 4,
        out_specs=vmem,
        scratch_shapes=[
            pltpu.VMEM((rows + edge.shape[0], deep, taps * lons), BF16),
            pltpu.VMEM((weights.shape[0], bands * lons), BF16),
        ],
        compiler_params=pltpu.CompilerParams(vmem_limit_bytes=12 * 2**20),
        name="conv",
    )(row_index, own, other, edge, weights)


def select_kernel(where_ref, near_ref, own_ref, pair_ref, other_ref):
    slots, rows, _ = own_ref.shape
    for index in range(4 * slots):
        start = pl.multiple_of(where_ref[index, 1], rows)
        picked = near_ref[pl.ds(start, rows)]
        picked = jnp.where(where_ref[index, 0] != 0, picked, jnp.zeros_like(picked))
        if index < 2 * slots:
            (own_ref if index < slots else pair_ref)[index % slots] = picked
        else:
            other_ref[index - 2 * slots] = picked


def selected(where, near, rows):
    slots = where.shape[0] // 4
    vmem = pl.BlockSpec(memory_space=pltpu.VMEM)
    shape = jax.ShapeDtypeStruct((slots, rows, near.shape[1]), near.dtype)
    both = jax.ShapeDtypeStruct((2 * slots, rows, near.shape[1]), near.dtype)
    return pl.pallas_call(
        select_kernel,
        out_shape=(shape, shape, both),
        in_specs=[pl.BlockSpec(memory_space=pltpu.SMEM), vmem],
        out_specs=(vmem, vmem, vmem),
        compiler_params=pltpu.CompilerParams(vmem_limit_bytes=2**20 + 2 * near.size),
        name="select",
    )(where, near)


def split3(x):
    high = x.astype(BF16).astype(F32)
    middle = (x - high).astype(BF16).astype(F32)
    return high, middle, x - high - middle


def attend_kernel(
    keys_count, sel_ref, got_ref, area_ref, wq_ref, wk_ref, wv_ref, *refs
):
    held, (out_ref, *rest) = refs[:keys_count], refs[keys_count:]
    slots, rows, width = sel_ref.shape
    count = slots * rows
    head_size = width // H
    token = (sel_ref[...] + got_ref[...]).reshape(count, width)
    query = jnp.dot(token, wq_ref[...], preferred_element_type=F32).astype(BF16)
    lane = lax.broadcasted_iota(jnp.int32, (1, width), 1) // head_size
    spread = jnp.concatenate(
        [jnp.where(lane == head, query, jnp.zeros_like(query)) for head in range(H)], axis=0
    )
    turned = lax.dot_general(
        spread, wk_ref[...], (((1,), (1,)), ((), ())), preferred_element_type=F32
    )
    turned = (turned * (LOG2E / math.sqrt(head_size))).astype(BF16)
    parts, begin = [], 0
    for ref in held:
        for at in range(0, ref.shape[0], 512):
            chunk = min(512, ref.shape[0] - at)
            parts.append((ref, at, begin, chunk))
            begin += chunk
    top = None
    for ref, at, begin, chunk in parts:
        keys = ref[at : at + chunk]
        block = lax.dot_general(
            turned, keys, (((1,), (1,)), ((), ())), preferred_element_type=F32
        )
        block = block + area_ref[:, begin : begin + chunk]
        best = block[:, 0:128]
        for lanes in range(128, chunk, 128):
            best = jnp.maximum(best, block[:, lanes : lanes + 128])
        best = jnp.max(best, axis=1, keepdims=True)
        if top is not None:
            best = jnp.maximum(top, best)
        weight = jnp.exp2(block - best)
        added = weight[:, 0:128]
        for lanes in range(128, chunk, 128):
            added = added + weight[:, lanes : lanes + 128]
        update = jnp.dot(weight.astype(BF16), keys, preferred_element_type=F32)
        if top is None:
            total, mixed = added, update
        else:
            factor = jnp.exp2(top - best)
            total, mixed = total * factor + added, mixed * factor + update
        top = best
    total = jnp.sum(total, axis=1, keepdims=True)
    value = jnp.dot((mixed / total).astype(BF16), wv_ref[...], preferred_element_type=F32)
    lse = top + jnp.log2(total)
    out = jnp.zeros((count, width), F32)
    stat_lane = lax.broadcasted_iota(jnp.int32, (1, 128), 1)
    stats = jnp.zeros((count, 128), F32)
    for head in range(H):
        out = jnp.where(lane == head, value[head * count : (head + 1) * count], out)
        for order, piece in enumerate(split3(lse[head * count : (head + 1) * count])):
            stats = jnp.where(stat_lane == 3 * head + order, piece, stats)
    out_ref[:, :, 0:width] = out.reshape(sel_ref.shape).astype(out_ref.dtype)
    stats = stats.reshape(slots, rows, 128)
    if rest:
        rest[0][...] = stats
    else:
        out_ref[:, :, width:] = stats.astype(out_ref.dtype)


def attended(sent, sel, got, area, w_query, w_key, w_value, held):
    slots, rows, width = sel.shape
    keys = sum(part.shape[0] for part in held)
    count = slots * rows
    vmem = pl.BlockSpec(memory_space=pltpu.VMEM)
    if sent:
        out_shape = (jax.ShapeDtypeStruct((slots, rows, width + 128), BF16),)
    else:
        out_shape = (
            jax.ShapeDtypeStruct((slots, rows, width), F32),
            jax.ShapeDtypeStruct((slots, rows, 128), F32),
        )
    return pl.pallas_call(
        functools.partial(attend_kernel, len(held)),
        out_shape=out_shape,
        in_specs=[vmem] * (6 + len(held)),
        out_specs=(vmem,) * len(out_shape),
        compiler_params=pltpu.CompilerParams(vmem_limit_bytes=20 * 2**20),
        cost_estimate=pl.CostEstimate(
            flops=4 * H * count * keys * width,
            bytes_accessed=2 * keys * width,
            transcendentals=H * count * keys,
        ),
        name="attend_sent" if sent else "attend_kept",
    )(sel, got, area, w_query, w_key, w_value, *held)


def finish_kernel(keep_ref, lse_ref, got_ref, wo_ref, out_ref):
    slots, rows, width = keep_ref.shape
    count = slots * rows
    keep = keep_ref[...].reshape(count, width)
    got = got_ref[:, :, 0:width].astype(F32).reshape(count, width)
    ours = lse_ref[...].reshape(count, 128).astype(BF16)
    theirs = got_ref[:, :, width:].reshape(count, 128)
    piece = lax.broadcasted_iota(jnp.int32, (128, width), 0) // 3
    head = lax.broadcasted_iota(jnp.int32, (128, width), 1) // (width // H)
    spread = (piece == head).astype(F32).astype(BF16)
    sums = jnp.dot(
        jnp.concatenate([ours, theirs], axis=0), spread, preferred_element_type=F32
    )
    own, far = sums[:count], sums[count:]
    top = jnp.maximum(own, far)
    own = jnp.exp2(own - top)
    far = jnp.exp2(far - top)
    mixed = ((keep * own + got * far) / (own + far)).astype(BF16)
    result = jnp.dot(mixed, wo_ref[...], preferred_element_type=F32).astype(BF16)
    out_ref[...] = result.reshape(out_ref.shape)


def finished(keep, lse, got, w_out):
    vmem = pl.BlockSpec(memory_space=pltpu.VMEM)
    return pl.pallas_call(
        finish_kernel,
        out_shape=jax.ShapeDtypeStruct(keep.shape, BF16),
        in_specs=[vmem] * 4,
        out_specs=vmem,
        compiler_params=pltpu.CompilerParams(vmem_limit_bytes=4 * 2**20),
        name="finish",
    )(keep, lse, got, w_out)


def gathered(block, masks):
    blocks = {(0, 0): block}
    for size in range(1, len(masks) + 1):
        for start in range(len(masks)):
            if size == len(masks) and start > 0:
                break
            chosen = [masks[(start + k) % len(masks)] for k in range(size)]
            key = (0, 0)
            for mask in chosen:
                key = (key[0] ^ mask[0], key[1] ^ mask[1])
            step = chosen[-1]
            before = (key[0] ^ step[0], key[1] ^ step[1])
            if key not in blocks:
                blocks[key] = exchange(blocks[before], *step)
    return blocks


def halves(state_field, support_rows, window_bands, conv_weight, w_query, w_key, w_value, w_out):
    lats = lax.axis_size("lat")
    lat, lon = lax.axis_index("lat"), lax.axis_index("lon")
    channels, rows, lons = state_field.shape
    lat_tile = support_rows.shape[0]
    bands = lat_tile // 2
    lon_tile = lons // 2
    band_total = lat_tile * lats
    pair = lats // 2

    deep = -(-channels // 16) * 16
    lower = (lon ^ lat) & 1
    own, same, cross = rows_of(lower.astype(jnp.int32).reshape(1), state_field, 2, deep)
    edge = vertical(jnp.concatenate([same, exchange(cross, 0, 1)], axis=0))
    other = exchange(own, 0, 1)
    weights = weights_of(conv_weight, deep)
    row_index = 2 * jnp.arange(lat_tile, dtype=jnp.int32)[:, None] + support_rows + 2
    row_index = lax.dynamic_slice_in_dim(row_index, lower * bands, bands, axis=0)
    features = features_of(own, other, edge, row_index, weights)

    bits = [1 << k for k in range(1, lats.bit_length() - 1) if 1 << k != pair]
    masks = [(0, 1)] + [(bit, 0) for bit in bits]
    blocks = gathered(features, masks)
    order = [(i, j) for i in range(0, pair, 2) for j in range(2)]
    near = jnp.concatenate([blocks[key] for key in order], axis=0)

    size = bands * lons
    slot_count = window_bands.shape[0] // lats
    sides = jnp.stack([lat, lat ^ pair, lat ^ 1, lat ^ pair ^ 1])
    wanted = window_bands[
        (sides[:, None] * slot_count + jnp.arange(slot_count)[None, :]).reshape(-1)
    ]
    owner = wanted // lat_tile
    band = wanted % lat_tile
    owner_lower = band // bands
    turn = owner_lower ^ (owner & 1) ^ lon
    apart = owner ^ lat
    place = ((apart & (pair - 2)) + turn) * size + band % bands * lons + turn * lon_tile
    within = apart & (pair | 1) == 0
    where = jnp.stack([within.astype(jnp.int32), place.astype(jnp.int32)], axis=1)
    sel_own, sel_pair, sel_other = selected(where, near, lon_tile)
    got_other = exchange(sel_other, 1, 0)
    sel_own = sel_own + got_other[:slot_count]
    sel_pair = sel_pair + got_other[slot_count:]
    sel_own, sel_pair, near = lax.optimization_barrier((sel_own, sel_pair, near))
    got_pair = exchange(sel_own, pair, 0)
    got_own = exchange(sel_pair, pair, 0)
    held = (near, exchange(near, 1, 0))

    step = jnp.arange(2 * len(order) * bands, dtype=jnp.int32)
    masks = (step // bands) % len(order)
    tile = lat ^ ((masks & ~1) | (step // (len(order) * bands)))
    key_band = tile * lat_tile + ((tile ^ lon ^ masks) & 1) * bands + step % bands
    area = LOG2E * log_area(key_band, band_total)
    area = jnp.repeat(area, lons)[None, :]
    shared = (area, w_query, w_key, w_value, held)
    (send,) = attended(True, sel_pair, got_pair, *shared)
    received = exchange(send, pair, 0)
    keep, lse = attended(False, sel_own, got_own, *shared)
    return finished(keep, lse, received, w_out)


def solution(mesh):
    lats, lons = mesh.shape["lat"], mesh.shape["lon"]
    paired = lons == 2 and lats >= 4 and lats & (lats - 1) == 0
    return jax.shard_map(
        halves if paired else general,
        mesh=mesh,
        in_specs=(P(None, "lat", "lon"), P("lat", None), P(), P(), P(), P(), P(), P()),
        out_specs=P("lat", "lon", None),
        check_vma=False,
    )
```

```python
import functools
import math

import jax
import jax.numpy as jnp
from jax import lax
from jax.experimental import pallas as pl
from jax.experimental.pallas import tpu as pltpu
from jax.sharding import PartitionSpec as P

D = 256
H = 4
AXES = ("lat", "lon")
LOG2E = 1.0 / math.log(2.0)
F32 = jnp.float32
BF16 = jnp.bfloat16


def padded(x, sides, width):
    for axis, dim in sides:
        devices, length = (lax.axis_size(axis), x.shape[dim])
        up = [(i, (i + 1) % devices) for i in range(devices - 1)]
        down = [(j, i) for i, j in up]
        last = lax.slice_in_dim(x, length - width, length, axis=dim)
        leading = lax.slice_in_dim(x, 0, width, axis=dim)
        before = lax.ppermute(last, axis, up)
        after = lax.ppermute(leading, axis, down)
        x = jnp.concatenate([before, x, after], axis=dim)
    return x


def shifted(x, axis, by):
    devices = lax.axis_size(axis)
    return lax.ppermute(x, axis, [(i, (i + by) % devices) for i in range(devices)])


def conv_features(extended, support_rows, conv_weight):
    bands = support_rows.shape[0]
    width = (extended.shape[2] - 1) // 2
    row_index = 2 * jnp.arange(bands, dtype=jnp.int32)[:, None] + support_rows + 2
    picked = jnp.take(extended, row_index, axis=1)
    tapped = jnp.stack(
        [picked[..., column_tap : column_tap + 2 * width : 2] for column_tap in range(3)], axis=3
    )
    patches = jnp.transpose(tapped, (1, 4, 2, 3, 0)).reshape(bands * width, -1)
    raw = jnp.dot(
        patches, conv_weight.reshape(-1, conv_weight.shape[-1]), preferred_element_type=F32
    )
    factor = lax.rsqrt(jnp.mean(raw * raw, axis=-1, keepdims=True) + 1e-06)
    return (raw * factor).astype(BF16).reshape(bands, width, -1)


def absorb(carry, block_keys, block_values, block_area, queries, scale):
    running_max, running_sum, mixed = carry
    scores = (
        jnp.einsum("qhd,khd->qhk", queries, block_keys, preferred_element_type=F32) * scale
        + block_area
    )
    new_max = jnp.maximum(running_max, jnp.max(scores, axis=-1))
    factor = jnp.exp(running_max - new_max)
    weights = jnp.exp(scores - new_max[..., None])
    running_sum = running_sum * factor + jnp.sum(weights, axis=-1)
    update = jnp.einsum(
        "qhk,khd->qhd", weights.astype(BF16), block_values, preferred_element_type=F32
    )
    mixed = mixed * factor[..., None] + update
    return (new_max, running_sum, mixed)


def sweep(carry, keys, values, queries, band_total):
    rows = keys.shape[0]
    lon_tile = keys.shape[1]
    head_size = D // H
    band_block = math.gcd(rows, max(1, 512 // lon_tile))
    blocks = rows // band_block
    block_len = band_block * lon_tile
    keys_blocks = keys.reshape(blocks, block_len, H, head_size)
    values_blocks = values.reshape(blocks, block_len, H, head_size)
    band_index = jnp.arange(rows, dtype=jnp.int32)
    area_rows = jnp.repeat(log_area(band_index, band_total), lon_tile).reshape(blocks, block_len)
    scale = 1.0 / math.sqrt(head_size)

    def step_block(state, inputs):
        return (absorb(state, inputs[0], inputs[1], inputs[2], queries, scale), None)

    result, unused = lax.scan(step_block, carry, (keys_blocks, values_blocks, area_rows))
    return result


def log_area(bands, band_total):
    centre = (bands.astype(F32) + 0.5) * (math.pi / band_total) - math.pi / 2
    return jnp.log(jnp.cos(centre))


def general(state_field, support_rows, window_bands, conv_weight, w_query, w_key, w_value, w_out):
    lat_tile = support_rows.shape[0]
    lon_tile = state_field.shape[2] // 2
    whole_lon = lon_tile * lax.axis_size("lon")
    band_total = lat_tile * lax.axis_size("lat")
    head_size = D // H
    extended = padded(state_field, (("lat", 1),), 2)
    western = shifted(extended[:, :, -1:], "lon", 1)
    extended = jnp.concatenate([western, extended], axis=2)
    features = conv_features(extended, support_rows, conv_weight)
    slot_count = window_bands.shape[0] // lax.axis_size("lat")
    piece = lax.all_gather(features, "lat", axis=0, tiled=True)
    mine = lax.dynamic_slice_in_dim(
        window_bands, lax.axis_index("lat") * slot_count, slot_count, axis=0
    )
    picked = jnp.take(piece, mine, axis=0)
    gathered = lax.all_gather(picked, "lon", axis=1, tiled=True)
    query_count = slot_count * whole_lon
    queries = jnp.dot(gathered.reshape(query_count, D), w_query, preferred_element_type=F32)
    queries = queries.astype(BF16).reshape(query_count, H, head_size)
    initial = (
        jnp.full((query_count, H), -1e30, F32),
        jnp.zeros((query_count, H), F32),
        jnp.zeros((query_count, H, head_size), F32),
    )
    piece_rows = piece.reshape(-1, D)
    keys = jnp.dot(piece_rows, w_key, preferred_element_type=F32).astype(BF16)
    values = jnp.dot(piece_rows, w_value, preferred_element_type=F32).astype(BF16)
    running_max, running_sum, mixed = sweep(
        initial, keys.reshape(piece.shape), values.reshape(piece.shape), queries, band_total
    )
    best = lax.pmax(running_max, "lon")
    factor = jnp.exp(running_max - best)
    scaled_mix = (mixed * factor[..., None]).reshape(slot_count, whole_lon, D)
    scaled_sum = (running_sum * factor).reshape(slot_count, whole_lon, H)
    mix_share, sum_share = (
        lax.psum_scatter(part.astype(BF16), "lon", scatter_dimension=1, tiled=True).astype(F32)
        for part in (scaled_mix, scaled_sum)
    )
    attended = mix_share.reshape(slot_count, lon_tile, H, head_size) / sum_share[..., None]
    attended = attended.astype(BF16).reshape(slot_count * lon_tile, D)
    result = jnp.dot(attended, w_out, preferred_element_type=F32).astype(BF16)
    return result.reshape(slot_count, lon_tile, D)


def exchange(x, lat_mask, lon_mask):
    lats, lons = lax.axis_size("lat"), lax.axis_size("lon")
    pairs = [
        (i * lons + j, (i ^ lat_mask) * lons + (j ^ lon_mask))
        for i in range(lats)
        for j in range(lons)
    ]
    return lax.ppermute(x, AXES, pairs)


def vertical(x):
    lats, lons = lax.axis_size("lat"), lax.axis_size("lon")
    pairs = []
    for i in range(1, lats):
        j = i % lons
        pairs += [((i - 1) * lons + j, i * lons + j), (i * lons + j, (i - 1) * lons + j)]
    return lax.ppermute(x, AXES, pairs)


def lines_of(ref, strided, deep):
    channels, rows, lons = ref.shape
    strided[0 : channels * rows] = ref[...].astype(F32).reshape(channels * rows, lons)
    strided[channels * rows :] = jnp.zeros(((deep - channels) * rows, lons), F32)
    return [strided[pl.ds(row, deep, stride=rows), :].astype(BF16) for row in range(rows)]


def rows_kernel(lower_ref, own_ref, lines_ref, same_ref, cross_ref, strided):
    rows, deep, _ = lines_ref.shape
    edge = same_ref.shape[0]
    lines = lines_of(own_ref, strided, deep)
    for row in range(rows):
        lines_ref[row] = lines[row]
    lower = lower_ref[0] != 0
    for row in range(edge):
        top, bottom = lines[row], lines[rows - edge + row]
        same_ref[row] = jnp.where(lower, bottom, top)
        cross_ref[row] = jnp.where(lower, top, bottom)


def rows_of(lower, own, edge, deep):
    _, rows, lons = own.shape
    vmem = pl.BlockSpec(memory_space=pltpu.VMEM)
    return pl.pallas_call(
        rows_kernel,
        out_shape=(
            jax.ShapeDtypeStruct((rows, deep, lons), BF16),
            jax.ShapeDtypeStruct((edge, deep, lons), BF16),
            jax.ShapeDtypeStruct((edge, deep, lons), BF16),
        ),
        in_specs=[pl.BlockSpec(memory_space=pltpu.SMEM), vmem],
        out_specs=(vmem, vmem, vmem),
        scratch_shapes=[pltpu.VMEM((deep * rows, lons), F32)],
        compiler_params=pltpu.CompilerParams(vmem_limit_bytes=4 * 2**20),
        name="rows",
    )(lower, own)


def weights_kernel(weight_ref, out_ref):
    slots, taps, channels, width = weight_ref.shape
    deep = out_ref.shape[0] // (slots * taps)
    blank = jnp.zeros((deep - channels, width), BF16)
    for slot in range(slots):
        for tap in range(taps):
            at = (slot * taps + tap) * deep
            out_ref[at : at + deep] = jnp.concatenate([weight_ref[slot, tap], blank], axis=0)


def weights_of(conv_weight, deep):
    slots, taps, _, width = conv_weight.shape
    vmem = pl.BlockSpec(memory_space=pltpu.VMEM)
    return pl.pallas_call(
        weights_kernel,
        out_shape=jax.ShapeDtypeStruct((slots * taps * deep, width), BF16),
        in_specs=[vmem],
        out_specs=vmem,
        compiler_params=pltpu.CompilerParams(vmem_limit_bytes=4 * 2**20),
        cost_estimate=pl.CostEstimate(
            flops=0, bytes_accessed=4 * conv_weight.size, transcendentals=0
        ),
        name="weights",
    )(conv_weight)


def conv_kernel(
    rows_ref, own_ref, other_ref, edge_ref, weight_ref, out_ref, taken, patches
):
    rows, deep, lons = own_ref.shape
    edge = edge_ref.shape[0] // 2
    width = lons
    bands = out_ref.shape[0] // width
    slots = rows_ref.shape[1]
    taps = weight_ref.shape[0] // (slots * deep)
    column = lax.broadcasted_iota(jnp.int32, (2 * lons, taps * width), 0)
    place = lax.broadcasted_iota(jnp.int32, (2 * lons, taps * width), 1)
    wanted = lax.rem(2 * (place % width) + place // width - 1 + 2 * lons, 2 * lons)
    choose = (column == wanted).astype(F32).astype(BF16)
    near = [own_ref[row] for row in range(rows)] + [edge_ref[row] for row in range(edge)]
    far = [other_ref[row] for row in range(rows)] + [edge_ref[edge + row] for row in range(edge)]
    both = jnp.concatenate(
        [jnp.concatenate(near, axis=0), jnp.concatenate(far, axis=0)], axis=1
    )
    split = jnp.dot(both, choose, preferred_element_type=F32).astype(BF16)
    for row in range(rows):
        taken[edge + row] = split[row * deep : (row + 1) * deep]
    for row in range(edge):
        piece = split[(rows + row) * deep : (rows + row + 1) * deep]
        taken[row] = piece
        taken[edge + rows + row] = piece
    for slot in range(slots):
        for band in range(bands):
            line = taken[rows_ref[band, slot]]
            for tap in range(taps):
                at = (slot * taps + tap) * deep
                patches[at : at + deep, band * width : (band + 1) * width] = line[
                    :, tap * width : (tap + 1) * width
                ]
    raw = lax.dot_general(
        patches[...], weight_ref[...], (((0,), (0,)), ((), ())), preferred_element_type=F32
    )
    factor = lax.rsqrt(jnp.mean(raw * raw, axis=-1, keepdims=True) + 1e-06)
    out_ref[...] = (raw * factor).astype(BF16)


def features_of(own, other, edge, row_index, weights):
    rows, deep, lons = own.shape
    width = weights.shape[1]
    bands = row_index.shape[0]
    taps = weights.shape[0] // (row_index.shape[1] * deep)
    vmem = pl.BlockSpec(memory_space=pltpu.VMEM)
    return pl.pallas_call(
        conv_kernel,
        out_shape=jax.ShapeDtypeStruct((bands * lons, width), BF16),
        in_specs=[pl.BlockSpec(memory_space=pltpu.SMEM)] + [vmem] * 4,
        out_specs=vmem,
        scratch_shapes=[
            pltpu.VMEM((rows + edge.shape[0], deep, taps * lons), BF16),
            pltpu.VMEM((weights.shape[0], bands * lons), BF16),
        ],
        compiler_params=pltpu.CompilerParams(vmem_limit_bytes=12 * 2**20),
        name="conv",
    )(row_index, own, other, edge, weights)


def select_kernel(where_ref, near_ref, own_ref, pair_ref, other_ref):
    slots, rows, _ = own_ref.shape
    for index in range(4 * slots):
        start = pl.multiple_of(where_ref[index, 1], rows)
        picked = near_ref[pl.ds(start, rows)]
        picked = jnp.where(where_ref[index, 0] != 0, picked, jnp.zeros_like(picked))
        if index < 2 * slots:
            (own_ref if index < slots else pair_ref)[index % slots] = picked
        else:
            other_ref[index - 2 * slots] = picked


def selected(where, near, rows):
    slots = where.shape[0] // 4
    vmem = pl.BlockSpec(memory_space=pltpu.VMEM)
    shape = jax.ShapeDtypeStruct((slots, rows, near.shape[1]), near.dtype)
    both = jax.ShapeDtypeStruct((2 * slots, rows, near.shape[1]), near.dtype)
    return pl.pallas_call(
        select_kernel,
        out_shape=(shape, shape, both),
        in_specs=[pl.BlockSpec(memory_space=pltpu.SMEM), vmem],
        out_specs=(vmem, vmem, vmem),
        compiler_params=pltpu.CompilerParams(vmem_limit_bytes=2**20 + 2 * near.size),
        name="select",
    )(where, near)


def split3(x):
    high = x.astype(BF16).astype(F32)
    middle = (x - high).astype(BF16).astype(F32)
    return high, middle, x - high - middle


def attend_kernel(
    keys_count, sel_ref, got_ref, area_ref, wq_ref, wk_ref, wv_ref, *refs
):
    held, (out_ref, *rest) = refs[:keys_count], refs[keys_count:]
    slots, rows, width = sel_ref.shape
    count = slots * rows
    head_size = width // H
    token = (sel_ref[...] + got_ref[...]).reshape(count, width)
    query = jnp.dot(token, wq_ref[...], preferred_element_type=F32).astype(BF16)
    lane = lax.broadcasted_iota(jnp.int32, (1, width), 1) // head_size
    spread = jnp.concatenate(
        [jnp.where(lane == head, query, jnp.zeros_like(query)) for head in range(H)], axis=0
    )
    turned = lax.dot_general(
        spread, wk_ref[...], (((1,), (1,)), ((), ())), preferred_element_type=F32
    )
    turned = (turned * (LOG2E / math.sqrt(head_size))).astype(BF16)
    parts, begin = [], 0
    for ref in held:
        for at in range(0, ref.shape[0], 512):
            chunk = min(512, ref.shape[0] - at)
            parts.append((ref, at, begin, chunk))
            begin += chunk
    top = None
    for ref, at, begin, chunk in parts:
        keys = ref[at : at + chunk]
        block = lax.dot_general(
            turned, keys, (((1,), (1,)), ((), ())), preferred_element_type=F32
        )
        block = block + area_ref[:, begin : begin + chunk]
        best = block[:, 0:128]
        for lanes in range(128, chunk, 128):
            best = jnp.maximum(best, block[:, lanes : lanes + 128])
        best = jnp.max(best, axis=1, keepdims=True)
        if top is not None:
            best = jnp.maximum(top, best)
        weight = jnp.exp2(block - best)
        added = weight[:, 0:128]
        for lanes in range(128, chunk, 128):
            added = added + weight[:, lanes : lanes + 128]
        update = jnp.dot(weight.astype(BF16), keys, preferred_element_type=F32)
        if top is None:
            total, mixed = added, update
        else:
            factor = jnp.exp2(top - best)
            total, mixed = total * factor + added, mixed * factor + update
        top = best
    total = jnp.sum(total, axis=1, keepdims=True)
    value = jnp.dot((mixed / total).astype(BF16), wv_ref[...], preferred_element_type=F32)
    lse = top + jnp.log2(total)
    out = jnp.zeros((count, width), F32)
    stat_lane = lax.broadcasted_iota(jnp.int32, (1, 128), 1)
    stats = jnp.zeros((count, 128), F32)
    for head in range(H):
        out = jnp.where(lane == head, value[head * count : (head + 1) * count], out)
        for order, piece in enumerate(split3(lse[head * count : (head + 1) * count])):
            stats = jnp.where(stat_lane == 3 * head + order, piece, stats)
    out_ref[:, :, 0:width] = out.reshape(sel_ref.shape).astype(out_ref.dtype)
    stats = stats.reshape(slots, rows, 128)
    if rest:
        rest[0][...] = stats
    else:
        out_ref[:, :, width:] = stats.astype(out_ref.dtype)


def attended(sent, sel, got, area, w_query, w_key, w_value, held):
    slots, rows, width = sel.shape
    keys = sum(part.shape[0] for part in held)
    count = slots * rows
    vmem = pl.BlockSpec(memory_space=pltpu.VMEM)
    if sent:
        out_shape = (jax.ShapeDtypeStruct((slots, rows, width + 128), BF16),)
    else:
        out_shape = (
            jax.ShapeDtypeStruct((slots, rows, width), F32),
            jax.ShapeDtypeStruct((slots, rows, 128), F32),
        )
    return pl.pallas_call(
        functools.partial(attend_kernel, len(held)),
        out_shape=out_shape,
        in_specs=[vmem] * (6 + len(held)),
        out_specs=(vmem,) * len(out_shape),
        compiler_params=pltpu.CompilerParams(vmem_limit_bytes=20 * 2**20),
        cost_estimate=pl.CostEstimate(
            flops=4 * H * count * keys * width,
            bytes_accessed=2 * keys * width,
            transcendentals=H * count * keys,
        ),
        name="attend_sent" if sent else "attend_kept",
    )(sel, got, area, w_query, w_key, w_value, *held)


def finish_kernel(keep_ref, lse_ref, got_ref, wo_ref, out_ref):
    slots, rows, width = keep_ref.shape
    count = slots * rows
    keep = keep_ref[...].reshape(count, width)
    got = got_ref[:, :, 0:width].astype(F32).reshape(count, width)
    ours = lse_ref[...].reshape(count, 128).astype(BF16)
    theirs = got_ref[:, :, width:].reshape(count, 128)
    piece = lax.broadcasted_iota(jnp.int32, (128, width), 0) // 3
    head = lax.broadcasted_iota(jnp.int32, (128, width), 1) // (width // H)
    spread = (piece == head).astype(F32).astype(BF16)
    sums = jnp.dot(
        jnp.concatenate([ours, theirs], axis=0), spread, preferred_element_type=F32
    )
    own, far = sums[:count], sums[count:]
    top = jnp.maximum(own, far)
    own = jnp.exp2(own - top)
    far = jnp.exp2(far - top)
    mixed = ((keep * own + got * far) / (own + far)).astype(BF16)
    result = jnp.dot(mixed, wo_ref[...], preferred_element_type=F32).astype(BF16)
    out_ref[...] = result.reshape(out_ref.shape)


def finished(keep, lse, got, w_out):
    vmem = pl.BlockSpec(memory_space=pltpu.VMEM)
    return pl.pallas_call(
        finish_kernel,
        out_shape=jax.ShapeDtypeStruct(keep.shape, BF16),
        in_specs=[vmem] * 4,
        out_specs=vmem,
        compiler_params=pltpu.CompilerParams(vmem_limit_bytes=4 * 2**20),
        name="finish",
    )(keep, lse, got, w_out)


def gathered(block, masks):
    blocks = {(0, 0): block}
    for mask in masks:
        blocks[mask] = exchange(block, *mask)
    whole = (sum(mask[0] for mask in masks), sum(mask[1] for mask in masks))
    if whole not in blocks:
        blocks[whole] = exchange(block, *whole)
    for size in range(2, len(masks)):
        for start in range(len(masks)):
            chosen = [masks[(start + k) % len(masks)] for k in range(size)]
            key = (sum(mask[0] for mask in chosen), sum(mask[1] for mask in chosen))
            step = chosen[-1]
            blocks[key] = exchange(blocks[key[0] ^ step[0], key[1] ^ step[1]], *step)
    return blocks


def halves(state_field, support_rows, window_bands, conv_weight, w_query, w_key, w_value, w_out):
    lats = lax.axis_size("lat")
    lat, lon = lax.axis_index("lat"), lax.axis_index("lon")
    channels, rows, lons = state_field.shape
    lat_tile = support_rows.shape[0]
    bands = lat_tile // 2
    lon_tile = lons // 2
    band_total = lat_tile * lats
    pair = lats // 2

    deep = -(-channels // 16) * 16
    lower = (lon ^ lat) & 1
    own, same, cross = rows_of(lower.astype(jnp.int32).reshape(1), state_field, 2, deep)
    edge = vertical(jnp.concatenate([same, exchange(cross, 0, 1)], axis=0))
    other = exchange(own, 0, 1)
    weights = weights_of(conv_weight, deep)
    row_index = 2 * jnp.arange(lat_tile, dtype=jnp.int32)[:, None] + support_rows + 2
    row_index = lax.dynamic_slice_in_dim(row_index, lower * bands, bands, axis=0)
    features = features_of(own, other, edge, row_index, weights)

    bits = [1 << k for k in range(1, lats.bit_length() - 1) if 1 << k != pair]
    masks = [(0, 1)] + [(bit, 0) for bit in bits]
    blocks = gathered(features, masks)
    order = [(i, j) for i in range(0, pair, 2) for j in range(2)]
    near = jnp.concatenate([blocks[key] for key in order], axis=0)

    size = bands * lons
    slot_count = window_bands.shape[0] // lats
    sides = jnp.stack([lat, lat ^ pair, lat ^ 1, lat ^ pair ^ 1])
    wanted = window_bands[
        (sides[:, None] * slot_count + jnp.arange(slot_count)[None, :]).reshape(-1)
    ]
    owner = wanted // lat_tile
    band = wanted % lat_tile
    owner_lower = band // bands
    turn = owner_lower ^ (owner & 1) ^ lon
    apart = owner ^ lat
    place = ((apart & (pair - 2)) + turn) * size + band % bands * lons + turn * lon_tile
    within = apart & (pair | 1) == 0
    where = jnp.stack([within.astype(jnp.int32), place.astype(jnp.int32)], axis=1)
    sel_own, sel_pair, sel_other = selected(where, near, lon_tile)
    got_other = exchange(sel_other, 1, 0)
    sel_own = sel_own + got_other[:slot_count]
    sel_pair = sel_pair + got_other[slot_count:]
    sel_own, sel_pair, near = lax.optimization_barrier((sel_own, sel_pair, near))
    got_pair = exchange(sel_own, pair, 0)
    got_own = exchange(sel_pair, pair, 0)
    held = (near, exchange(near, 1, 0))

    step = jnp.arange(2 * len(order) * bands, dtype=jnp.int32)
    masks = (step // bands) % len(order)
    tile = lat ^ ((masks & ~1) | (step // (len(order) * bands)))
    key_band = tile * lat_tile + ((tile ^ lon ^ masks) & 1) * bands + step % bands
    area = LOG2E * log_area(key_band, band_total)
    area = jnp.repeat(area, lons)[None, :]
    shared = (area, w_query, w_key, w_value, held)
    (send,) = attended(True, sel_pair, got_pair, *shared)
    received = exchange(send, pair, 0)
    keep, lse = attended(False, sel_own, got_own, *shared)
    return finished(keep, lse, received, w_out)


def solution(mesh):
    lats, lons = mesh.shape["lat"], mesh.shape["lon"]
    paired = lons == 2 and lats >= 4 and lats & (lats - 1) == 0
    return jax.shard_map(
        halves if paired else general,
        mesh=mesh,
        in_specs=(P(None, "lat", "lon"), P("lat", None), P(), P(), P(), P(), P(), P()),
        out_specs=P("lat", "lon", None),
        check_vma=False,
    )
```

```python
import functools
import math

import jax
import jax.numpy as jnp
from jax import lax
from jax.experimental import pallas as pl
from jax.experimental.pallas import tpu as pltpu
from jax.sharding import PartitionSpec as P

D = 256
H = 4
AXES = ("lat", "lon")
LOG2E = 1.0 / math.log(2.0)
F32 = jnp.float32
BF16 = jnp.bfloat16


def padded(x, sides, width):
    for axis, dim in sides:
        devices, length = (lax.axis_size(axis), x.shape[dim])
        up = [(i, (i + 1) % devices) for i in range(devices - 1)]
        down = [(j, i) for i, j in up]
        last = lax.slice_in_dim(x, length - width, length, axis=dim)
        leading = lax.slice_in_dim(x, 0, width, axis=dim)
        before = lax.ppermute(last, axis, up)
        after = lax.ppermute(leading, axis, down)
        x = jnp.concatenate([before, x, after], axis=dim)
    return x


def shifted(x, axis, by):
    devices = lax.axis_size(axis)
    return lax.ppermute(x, axis, [(i, (i + by) % devices) for i in range(devices)])


def conv_features(extended, support_rows, conv_weight):
    bands = support_rows.shape[0]
    width = (extended.shape[2] - 1) // 2
    row_index = 2 * jnp.arange(bands, dtype=jnp.int32)[:, None] + support_rows + 2
    picked = jnp.take(extended, row_index, axis=1)
    tapped = jnp.stack(
        [picked[..., column_tap : column_tap + 2 * width : 2] for column_tap in range(3)], axis=3
    )
    patches = jnp.transpose(tapped, (1, 4, 2, 3, 0)).reshape(bands * width, -1)
    raw = jnp.dot(
        patches, conv_weight.reshape(-1, conv_weight.shape[-1]), preferred_element_type=F32
    )
    factor = lax.rsqrt(jnp.mean(raw * raw, axis=-1, keepdims=True) + 1e-06)
    return (raw * factor).astype(BF16).reshape(bands, width, -1)


def absorb(carry, block_keys, block_values, block_area, queries, scale):
    running_max, running_sum, mixed = carry
    scores = (
        jnp.einsum("qhd,khd->qhk", queries, block_keys, preferred_element_type=F32) * scale
        + block_area
    )
    new_max = jnp.maximum(running_max, jnp.max(scores, axis=-1))
    factor = jnp.exp(running_max - new_max)
    weights = jnp.exp(scores - new_max[..., None])
    running_sum = running_sum * factor + jnp.sum(weights, axis=-1)
    update = jnp.einsum(
        "qhk,khd->qhd", weights.astype(BF16), block_values, preferred_element_type=F32
    )
    mixed = mixed * factor[..., None] + update
    return (new_max, running_sum, mixed)


def sweep(carry, keys, values, queries, band_total):
    rows = keys.shape[0]
    lon_tile = keys.shape[1]
    head_size = D // H
    band_block = math.gcd(rows, max(1, 512 // lon_tile))
    blocks = rows // band_block
    block_len = band_block * lon_tile
    keys_blocks = keys.reshape(blocks, block_len, H, head_size)
    values_blocks = values.reshape(blocks, block_len, H, head_size)
    band_index = jnp.arange(rows, dtype=jnp.int32)
    area_rows = jnp.repeat(log_area(band_index, band_total), lon_tile).reshape(blocks, block_len)
    scale = 1.0 / math.sqrt(head_size)

    def step_block(state, inputs):
        return (absorb(state, inputs[0], inputs[1], inputs[2], queries, scale), None)

    result, unused = lax.scan(step_block, carry, (keys_blocks, values_blocks, area_rows))
    return result


def log_area(bands, band_total):
    centre = (bands.astype(F32) + 0.5) * (math.pi / band_total) - math.pi / 2
    return jnp.log(jnp.cos(centre))


def general(state_field, support_rows, window_bands, conv_weight, w_query, w_key, w_value, w_out):
    lat_tile = support_rows.shape[0]
    lon_tile = state_field.shape[2] // 2
    whole_lon = lon_tile * lax.axis_size("lon")
    band_total = lat_tile * lax.axis_size("lat")
    head_size = D // H
    extended = padded(state_field, (("lat", 1),), 2)
    western = shifted(extended[:, :, -1:], "lon", 1)
    extended = jnp.concatenate([western, extended], axis=2)
    features = conv_features(extended, support_rows, conv_weight)
    slot_count = window_bands.shape[0] // lax.axis_size("lat")
    piece = lax.all_gather(features, "lat", axis=0, tiled=True)
    mine = lax.dynamic_slice_in_dim(
        window_bands, lax.axis_index("lat") * slot_count, slot_count, axis=0
    )
    picked = jnp.take(piece, mine, axis=0)
    gathered = lax.all_gather(picked, "lon", axis=1, tiled=True)
    query_count = slot_count * whole_lon
    queries = jnp.dot(gathered.reshape(query_count, D), w_query, preferred_element_type=F32)
    queries = queries.astype(BF16).reshape(query_count, H, head_size)
    initial = (
        jnp.full((query_count, H), -1e30, F32),
        jnp.zeros((query_count, H), F32),
        jnp.zeros((query_count, H, head_size), F32),
    )
    piece_rows = piece.reshape(-1, D)
    keys = jnp.dot(piece_rows, w_key, preferred_element_type=F32).astype(BF16)
    values = jnp.dot(piece_rows, w_value, preferred_element_type=F32).astype(BF16)
    running_max, running_sum, mixed = sweep(
        initial, keys.reshape(piece.shape), values.reshape(piece.shape), queries, band_total
    )
    best = lax.pmax(running_max, "lon")
    factor = jnp.exp(running_max - best)
    scaled_mix = (mixed * factor[..., None]).reshape(slot_count, whole_lon, D)
    scaled_sum = (running_sum * factor).reshape(slot_count, whole_lon, H)
    mix_share, sum_share = (
        lax.psum_scatter(part.astype(BF16), "lon", scatter_dimension=1, tiled=True).astype(F32)
        for part in (scaled_mix, scaled_sum)
    )
    attended = mix_share.reshape(slot_count, lon_tile, H, head_size) / sum_share[..., None]
    attended = attended.astype(BF16).reshape(slot_count * lon_tile, D)
    result = jnp.dot(attended, w_out, preferred_element_type=F32).astype(BF16)
    return result.reshape(slot_count, lon_tile, D)


def exchange(x, lat_mask, lon_mask):
    lats, lons = lax.axis_size("lat"), lax.axis_size("lon")
    pairs = [
        (i * lons + j, (i ^ lat_mask) * lons + (j ^ lon_mask))
        for i in range(lats)
        for j in range(lons)
    ]
    return lax.ppermute(x, AXES, pairs)


def across(x):
    lats, lons = lax.axis_size("lat"), lax.axis_size("lon")
    pairs = []
    for i in range(2, lats, 2):
        for j in range(lons):
            pairs += [((i - 1) * lons + j, i * lons + j), (i * lons + j, (i - 1) * lons + j)]
    return lax.ppermute(x, AXES, pairs)


def rows_kernel(odd_ref, own_ref, lines_ref, far_ref, chip_ref, strided):
    channels, rows, lons = own_ref.shape
    deep = lines_ref.shape[1]
    edge = far_ref.shape[0]
    strided[0 : channels * rows] = own_ref[...].astype(F32).reshape(channels * rows, lons)
    strided[channels * rows :] = jnp.zeros(((deep - channels) * rows, lons), F32)
    lines = [strided[pl.ds(row, deep, stride=rows), :].astype(BF16) for row in range(rows)]
    for row in range(rows):
        lines_ref[row] = lines[row]
    odd = odd_ref[0] != 0
    for row in range(edge):
        top, bottom = lines[row], lines[rows - edge + row]
        far_ref[row] = jnp.where(odd, bottom, top)
        chip_ref[row] = jnp.where(odd, top, bottom)


def rows_of(odd, own, edge, deep):
    _, rows, lons = own.shape
    vmem = pl.BlockSpec(memory_space=pltpu.VMEM)
    return pl.pallas_call(
        rows_kernel,
        out_shape=(
            jax.ShapeDtypeStruct((rows, deep, lons), BF16),
            jax.ShapeDtypeStruct((edge, deep, lons), BF16),
            jax.ShapeDtypeStruct((edge, deep, lons), BF16),
        ),
        in_specs=[pl.BlockSpec(memory_space=pltpu.SMEM), vmem],
        out_specs=(vmem, vmem, vmem),
        scratch_shapes=[pltpu.VMEM((deep * rows, lons), F32)],
        compiler_params=pltpu.CompilerParams(vmem_limit_bytes=4 * 2**20),
        name="rows",
    )(odd, own)


def weights_kernel(weight_ref, picks_ref, out_ref, hits_ref):
    slots, taps, channels, width = weight_ref.shape
    deep = out_ref.shape[0] // (slots * taps)
    blank = jnp.zeros((deep - channels, width), BF16)
    for slot in range(slots):
        for tap in range(taps):
            at = (slot * taps + tap) * deep
            out_ref[at : at + deep] = jnp.concatenate([weight_ref[slot, tap], blank], axis=0)
    picks = picks_ref[...]
    row = lax.broadcasted_iota(jnp.int32, (128, 128), 0)
    lane = lax.broadcasted_iota(jnp.int32, (128, 128), 1)
    for slot in range(slots):
        hits = jnp.zeros((128, 128), F32)
        for band in range(picks.shape[0]):
            hits = jnp.where((row == picks[band, slot]) & (lane == band), 1.0, hits)
        hits_ref[:, slot * 128 : (slot + 1) * 128] = hits.astype(BF16)


def weights_of(conv_weight, picks, deep):
    slots, taps, _, width = conv_weight.shape
    vmem = pl.BlockSpec(memory_space=pltpu.VMEM)
    return pl.pallas_call(
        weights_kernel,
        out_shape=(
            jax.ShapeDtypeStruct((slots * taps * deep, width), BF16),
            jax.ShapeDtypeStruct((128, slots * 128), BF16),
        ),
        in_specs=[vmem, vmem],
        out_specs=(vmem, vmem),
        compiler_params=pltpu.CompilerParams(vmem_limit_bytes=4 * 2**20),
        cost_estimate=pl.CostEstimate(
            flops=0, bytes_accessed=4 * conv_weight.size, transcendentals=0
        ),
        name="weights",
    )(conv_weight, picks)


def columns_kernel(lines_ref, above_ref, below_ref, out_ref):
    rows = [ref[k] for ref in (above_ref, lines_ref, below_ref) for k in range(ref.shape[0])]
    lane = lax.broadcasted_iota(jnp.int32, (1, 128), 1)
    out = jnp.zeros(out_ref.shape, F32)
    for index, row in enumerate(rows):
        last = row[:, row.shape[1] - 128 :].astype(F32)[:, 127:128]
        out = jnp.where(lane == index, last, out)
    out_ref[...] = out.astype(BF16)


def last_columns(lines, above, below):
    vmem = pl.BlockSpec(memory_space=pltpu.VMEM)
    return pl.pallas_call(
        columns_kernel,
        out_shape=jax.ShapeDtypeStruct((lines.shape[1], 128), BF16),
        in_specs=[vmem] * 3,
        out_specs=vmem,
        compiler_params=pltpu.CompilerParams(vmem_limit_bytes=4 * 2**20),
        name="columns",
    )(lines, above, below)


def normed(raw):
    return raw * lax.rsqrt(jnp.mean(raw * raw, axis=-1, keepdims=True) + 1e-06)


def conv_kernel(
    picks_ref, lines_ref, above_ref, below_ref, weight_ref, out_ref, first_ref, taken, patches
):
    _, deep, lons = lines_ref.shape
    width = lons // 2
    bands, slots = picks_ref.shape
    taps = weight_ref.shape[0] // (slots * deep)
    rows = [ref[k] for ref in (above_ref, lines_ref, below_ref) for k in range(ref.shape[0])]
    column = lax.broadcasted_iota(jnp.int32, (lons, taps * lons), 0)
    place = lax.broadcasted_iota(jnp.int32, (lons, taps * lons), 1)
    wanted = 2 * (place % width) + place // lons - 1
    choose = (column == wanted).astype(F32).astype(BF16)
    split = jnp.dot(
        jnp.concatenate(rows, axis=0), choose, preferred_element_type=F32
    ).astype(BF16)
    for row in range(len(rows)):
        taken[row] = split[row * deep : (row + 1) * deep]
    left = lax.broadcasted_iota(jnp.int32, (1, lons), 1) < width
    picks = picks_ref[...]
    for slot in range(slots):
        for band in range(0, bands, 2):
            one, two = taken[picks[band, slot]], taken[picks[band + 1, slot]]
            for tap in range(taps):
                at = (slot * taps + tap) * deep
                patches[at : at + deep, band * width : (band + 2) * width] = jnp.where(
                    left,
                    one[:, tap * lons : (tap + 1) * lons],
                    two[:, tap * lons : (tap + 1) * lons],
                )
    raw = lax.dot_general(
        patches[...], weight_ref[...], (((0,), (0,)), ((), ())), preferred_element_type=F32
    )
    out_ref[...] = normed(raw).astype(BF16)
    for band in range(bands):
        first_ref[band] = raw[band * width : band * width + 8]


def local_features(picks, lines, above, below, weights):
    _, deep, lons = lines.shape
    width = weights.shape[1]
    bands = picks.shape[0]
    count = lines.shape[0] + above.shape[0] + below.shape[0]
    taps = weights.shape[0] // (picks.shape[1] * deep)
    tokens = bands * lons // 2
    vmem = pl.BlockSpec(memory_space=pltpu.VMEM)
    return pl.pallas_call(
        conv_kernel,
        out_shape=(
            jax.ShapeDtypeStruct((tokens, width), BF16),
            jax.ShapeDtypeStruct((bands, 8, width), F32),
        ),
        in_specs=[vmem] * 5,
        out_specs=(vmem, vmem),
        scratch_shapes=[
            pltpu.VMEM((count, deep, taps * lons), BF16),
            pltpu.VMEM((weights.shape[0], tokens), BF16),
        ],
        compiler_params=pltpu.CompilerParams(vmem_limit_bytes=12 * 2**20),
        cost_estimate=pl.CostEstimate(
            flops=2 * weights.size * tokens, bytes_accessed=2 * weights.size, transcendentals=0
        ),
        name="conv",
    )(picks, lines, above, below, weights)


def west_kernel(west_ref, hits_ref, weight_ref, some_ref, first_ref, out_ref):
    deep = west_ref.shape[0]
    slots = hits_ref.shape[1] // 128
    stride = weight_ref.shape[0] // slots
    bands = first_ref.shape[0]
    width = out_ref.shape[0] // bands
    chosen = jnp.dot(west_ref[...], hits_ref[...], preferred_element_type=F32).astype(BF16)
    columns = jnp.concatenate(
        [chosen[:, slot * 128 : (slot + 1) * 128] for slot in range(slots)], axis=0
    )
    filters = jnp.concatenate(
        [weight_ref[slot * stride : slot * stride + deep] for slot in range(slots)], axis=0
    )
    more = lax.dot_general(
        columns, filters, (((0,), (0,)), ((), ())), preferred_element_type=F32
    )
    out_ref[...] = some_ref[...]
    head = lax.broadcasted_iota(jnp.int32, (16, 1), 0) == 0
    for band in range(bands):
        fixed = normed(first_ref[band, 0:1] + more[band : band + 1])
        rest = some_ref[band * width : band * width + 16].astype(F32)
        out_ref[band * width : band * width + 16] = jnp.where(head, fixed, rest).astype(BF16)


def west_added(west, hits, weights, some, first):
    vmem = pl.BlockSpec(memory_space=pltpu.VMEM)
    return pl.pallas_call(
        west_kernel,
        out_shape=jax.ShapeDtypeStruct(some.shape, BF16),
        in_specs=[vmem] * 5,
        out_specs=vmem,
        compiler_params=pltpu.CompilerParams(vmem_limit_bytes=6 * 2**20),
        name="west",
    )(west, hits, weights, some, first)


def select_kernel(where_ref, near_ref, own_ref, pair_ref, other_ref):
    slots, rows, _ = own_ref.shape
    where = where_ref[...]
    for index in range(4 * slots):
        start = pl.multiple_of(where[index, 1], rows)
        picked = near_ref[pl.ds(start, rows)]
        picked = jnp.where(where[index, 0] != 0, picked, jnp.zeros_like(picked))
        if index < 2 * slots:
            (own_ref if index < slots else pair_ref)[index % slots] = picked
        else:
            other_ref[index - 2 * slots] = picked


def selected(where, near, rows):
    slots = where.shape[0] // 4
    vmem = pl.BlockSpec(memory_space=pltpu.VMEM)
    shape = jax.ShapeDtypeStruct((slots, rows, near.shape[1]), near.dtype)
    both = jax.ShapeDtypeStruct((2 * slots, rows, near.shape[1]), near.dtype)
    return pl.pallas_call(
        select_kernel,
        out_shape=(shape, shape, both),
        in_specs=[vmem, vmem],
        out_specs=(vmem, vmem, vmem),
        compiler_params=pltpu.CompilerParams(vmem_limit_bytes=2**20 + 2 * near.size),
        name="select",
    )(where, near)


def split3(x):
    high = x.astype(BF16).astype(F32)
    middle = (x - high).astype(BF16).astype(F32)
    return high, middle, x - high - middle


def attend_kernel(
    keys_count, sel_ref, got_ref, area_ref, wq_ref, wk_ref, wv_ref, *refs
):
    held, (out_ref, *rest) = refs[:keys_count], refs[keys_count:]
    slots, rows, width = sel_ref.shape
    count = slots * rows
    head_size = width // H
    token = (sel_ref[...] + got_ref[...]).reshape(count, width)
    query = jnp.dot(token, wq_ref[...], preferred_element_type=F32).astype(BF16)
    lane = lax.broadcasted_iota(jnp.int32, (1, width), 1) // head_size
    spread = jnp.concatenate(
        [jnp.where(lane == head, query, jnp.zeros_like(query)) for head in range(H)], axis=0
    )
    turned = lax.dot_general(
        spread, wk_ref[...], (((1,), (1,)), ((), ())), preferred_element_type=F32
    )
    turned = (turned * (LOG2E / math.sqrt(head_size))).astype(BF16)
    parts, begin = [], 0
    for ref in held:
        for at in range(0, ref.shape[0], 512):
            chunk = min(512, ref.shape[0] - at)
            parts.append((ref, at, begin, chunk))
            begin += chunk
    top = None
    for ref, at, begin, chunk in parts:
        keys = ref[at : at + chunk]
        block = lax.dot_general(
            turned, keys, (((1,), (1,)), ((), ())), preferred_element_type=F32
        )
        block = block + area_ref[:, begin : begin + chunk]
        best = block[:, 0:128]
        for lanes in range(128, chunk, 128):
            best = jnp.maximum(best, block[:, lanes : lanes + 128])
        best = jnp.max(best, axis=1, keepdims=True)
        if top is not None:
            best = jnp.maximum(top, best)
        weight = jnp.exp2(block - best)
        added = weight[:, 0:128]
        for lanes in range(128, chunk, 128):
            added = added + weight[:, lanes : lanes + 128]
        update = jnp.dot(weight.astype(BF16), keys, preferred_element_type=F32)
        if top is None:
            total, mixed = added, update
        else:
            factor = jnp.exp2(top - best)
            total, mixed = total * factor + added, mixed * factor + update
        top = best
    total = jnp.sum(total, axis=1, keepdims=True)
    value = jnp.dot((mixed / total).astype(BF16), wv_ref[...], preferred_element_type=F32)
    lse = top + jnp.log2(total)
    out = jnp.zeros((count, width), F32)
    stat_lane = lax.broadcasted_iota(jnp.int32, (1, 128), 1)
    stats = jnp.zeros((count, 128), F32)
    for head in range(H):
        out = jnp.where(lane == head, value[head * count : (head + 1) * count], out)
        for order, piece in enumerate(split3(lse[head * count : (head + 1) * count])):
            stats = jnp.where(stat_lane == 3 * head + order, piece, stats)
    out_ref[:, :, 0:width] = out.reshape(sel_ref.shape).astype(out_ref.dtype)
    stats = stats.reshape(slots, rows, 128)
    if rest:
        rest[0][...] = stats
    else:
        out_ref[:, :, width:] = stats.astype(out_ref.dtype)


def attended(sent, sel, got, area, w_query, w_key, w_value, held):
    slots, rows, width = sel.shape
    keys = sum(part.shape[0] for part in held)
    count = slots * rows
    vmem = pl.BlockSpec(memory_space=pltpu.VMEM)
    if sent:
        out_shape = (jax.ShapeDtypeStruct((slots, rows, width + 128), BF16),)
    else:
        out_shape = (
            jax.ShapeDtypeStruct((slots, rows, width), F32),
            jax.ShapeDtypeStruct((slots, rows, 128), F32),
        )
    return pl.pallas_call(
        functools.partial(attend_kernel, len(held)),
        out_shape=out_shape,
        in_specs=[vmem] * (6 + len(held)),
        out_specs=(vmem,) * len(out_shape),
        compiler_params=pltpu.CompilerParams(vmem_limit_bytes=20 * 2**20),
        cost_estimate=pl.CostEstimate(
            flops=4 * H * count * keys * width,
            bytes_accessed=2 * keys * width,
            transcendentals=H * count * keys,
        ),
        name="attend_sent" if sent else "attend_kept",
    )(sel, got, area, w_query, w_key, w_value, *held)


def finish_kernel(keep_ref, lse_ref, got_ref, wo_ref, out_ref):
    slots, rows, width = keep_ref.shape
    count = slots * rows
    keep = keep_ref[...].reshape(count, width)
    got = got_ref[:, :, 0:width].astype(F32).reshape(count, width)
    ours = lse_ref[...].reshape(count, 128).astype(BF16)
    theirs = got_ref[:, :, width:].reshape(count, 128)
    piece = lax.broadcasted_iota(jnp.int32, (128, width), 0) // 3
    head = lax.broadcasted_iota(jnp.int32, (128, width), 1) // (width // H)
    spread = (piece == head).astype(F32).astype(BF16)
    sums = jnp.dot(
        jnp.concatenate([ours, theirs], axis=0), spread, preferred_element_type=F32
    )
    own, far = sums[:count], sums[count:]
    top = jnp.maximum(own, far)
    own = jnp.exp2(own - top)
    far = jnp.exp2(far - top)
    mixed = ((keep * own + got * far) / (own + far)).astype(BF16)
    result = jnp.dot(mixed, wo_ref[...], preferred_element_type=F32).astype(BF16)
    out_ref[...] = result.reshape(out_ref.shape)


def finished(keep, lse, got, w_out):
    vmem = pl.BlockSpec(memory_space=pltpu.VMEM)
    return pl.pallas_call(
        finish_kernel,
        out_shape=jax.ShapeDtypeStruct(keep.shape, BF16),
        in_specs=[vmem] * 4,
        out_specs=vmem,
        compiler_params=pltpu.CompilerParams(vmem_limit_bytes=4 * 2**20),
        name="finish",
    )(keep, lse, got, w_out)


def gathered(block, masks):
    blocks = {(0, 0): block}
    for mask in masks:
        blocks[mask] = exchange(block, *mask)
    whole = (sum(mask[0] for mask in masks), sum(mask[1] for mask in masks))
    if whole not in blocks:
        blocks[whole] = exchange(block, *whole)
    for size in range(2, len(masks)):
        for start in range(len(masks)):
            chosen = [masks[(start + k) % len(masks)] for k in range(size)]
            key = (sum(mask[0] for mask in chosen), sum(mask[1] for mask in chosen))
            step = chosen[-1]
            blocks[key] = exchange(blocks[key[0] ^ step[0], key[1] ^ step[1]], *step)
    return blocks


def halves(state_field, support_rows, window_bands, conv_weight, w_query, w_key, w_value, w_out):
    lats = lax.axis_size("lat")
    lat, lon = lax.axis_index("lat"), lax.axis_index("lon")
    channels, rows, lons = state_field.shape
    lat_tile = support_rows.shape[0]
    lon_tile = lons // 2
    band_total = lat_tile * lats
    pair = lats // 2

    deep = -(-channels // 16) * 16
    odd = lat & 1
    lines, out_far, out_chip = rows_of(odd.astype(jnp.int32).reshape(1), state_field, 2, deep)
    far_rows = across(out_far)
    chip_rows = exchange(out_chip, 1, 0)
    above = jnp.where(odd != 0, chip_rows, far_rows)
    below = jnp.where(odd != 0, far_rows, chip_rows)
    west = exchange(last_columns(lines, above, below), 0, 1)
    picks = 2 * jnp.arange(lat_tile, dtype=jnp.int32)[:, None] + support_rows + 2
    weights, hits = weights_of(conv_weight, picks, deep)
    some, first = local_features(picks, lines, above, below, weights)
    features = west_added(west, hits, weights, some, first)

    bits = [1 << k for k in range(1, lats.bit_length() - 1) if 1 << k != pair]
    masks = [(0, 1)] + [(bit, 0) for bit in bits]
    blocks = gathered(features, masks)
    order = [(i, j) for i in range(0, pair, 2) for j in range(2)]
    near = jnp.concatenate([blocks[key] for key in order], axis=0)

    size = lat_tile * lon_tile
    slot_count = window_bands.shape[0] // lats
    sides = jnp.stack([lat, lat ^ pair, lat ^ 1, lat ^ pair ^ 1])
    wanted = window_bands[
        (sides[:, None] * slot_count + jnp.arange(slot_count)[None, :]).reshape(-1)
    ]
    owner = wanted // lat_tile
    apart = owner ^ lat
    place = (apart & (pair - 2)) * size + wanted % lat_tile * lon_tile
    within = apart & (pair | 1) == 0
    where = jnp.stack([within.astype(jnp.int32), place.astype(jnp.int32)], axis=1)
    sel_own, sel_pair, sel_other = selected(where, near, lon_tile)
    got_other = exchange(sel_other, 1, 0)
    sel_own = sel_own + got_other[:slot_count]
    sel_pair = sel_pair + got_other[slot_count:]
    sel_own, sel_pair, near = lax.optimization_barrier((sel_own, sel_pair, near))
    got_pair = exchange(sel_own, pair, 0)
    got_own = exchange(sel_pair, pair, 0)
    held = (near, exchange(near, 1, 0))

    step = jnp.arange(2 * len(order) * lat_tile, dtype=jnp.int32)
    masks = (step // lat_tile) % len(order)
    tile = lat ^ ((masks & ~1) | (step // (len(order) * lat_tile)))
    key_band = tile * lat_tile + step % lat_tile
    area = LOG2E * log_area(key_band, band_total)
    area = jnp.repeat(area, lon_tile)[None, :]
    shared = (area, w_query, w_key, w_value, held)
    (send,) = attended(True, sel_pair, got_pair, *shared)
    received = exchange(send, pair, 0)
    keep, lse = attended(False, sel_own, got_own, *shared)
    return finished(keep, lse, received, w_out)


def solution(mesh):
    lats, lons = mesh.shape["lat"], mesh.shape["lon"]
    paired = lons == 2 and lats >= 4 and lats & (lats - 1) == 0
    return jax.shard_map(
        halves if paired else general,
        mesh=mesh,
        in_specs=(P(None, "lat", "lon"), P("lat", None), P(), P(), P(), P(), P(), P()),
        out_specs=P("lat", "lon", None),
        check_vma=False,
    )
```

```python
import functools
import math

import jax
import jax.numpy as jnp
from jax import lax
from jax.experimental import pallas as pl
from jax.experimental.pallas import tpu as pltpu
from jax.sharding import PartitionSpec as P

D = 256
H = 4
AXES = ("lat", "lon")
LOG2E = 1.0 / math.log(2.0)
F32 = jnp.float32
BF16 = jnp.bfloat16


def padded(x, sides, width):
    for axis, dim in sides:
        devices, length = (lax.axis_size(axis), x.shape[dim])
        up = [(i, (i + 1) % devices) for i in range(devices - 1)]
        down = [(j, i) for i, j in up]
        last = lax.slice_in_dim(x, length - width, length, axis=dim)
        leading = lax.slice_in_dim(x, 0, width, axis=dim)
        before = lax.ppermute(last, axis, up)
        after = lax.ppermute(leading, axis, down)
        x = jnp.concatenate([before, x, after], axis=dim)
    return x


def shifted(x, axis, by):
    devices = lax.axis_size(axis)
    return lax.ppermute(x, axis, [(i, (i + by) % devices) for i in range(devices)])


def conv_features(extended, support_rows, conv_weight):
    bands = support_rows.shape[0]
    width = (extended.shape[2] - 1) // 2
    row_index = 2 * jnp.arange(bands, dtype=jnp.int32)[:, None] + support_rows + 2
    picked = jnp.take(extended, row_index, axis=1)
    tapped = jnp.stack(
        [picked[..., column_tap : column_tap + 2 * width : 2] for column_tap in range(3)], axis=3
    )
    patches = jnp.transpose(tapped, (1, 4, 2, 3, 0)).reshape(bands * width, -1)
    raw = jnp.dot(
        patches, conv_weight.reshape(-1, conv_weight.shape[-1]), preferred_element_type=F32
    )
    factor = lax.rsqrt(jnp.mean(raw * raw, axis=-1, keepdims=True) + 1e-06)
    return (raw * factor).astype(BF16).reshape(bands, width, -1)


def absorb(carry, block_keys, block_values, block_area, queries, scale):
    running_max, running_sum, mixed = carry
    scores = (
        jnp.einsum("qhd,khd->qhk", queries, block_keys, preferred_element_type=F32) * scale
        + block_area
    )
    new_max = jnp.maximum(running_max, jnp.max(scores, axis=-1))
    factor = jnp.exp(running_max - new_max)
    weights = jnp.exp(scores - new_max[..., None])
    running_sum = running_sum * factor + jnp.sum(weights, axis=-1)
    update = jnp.einsum(
        "qhk,khd->qhd", weights.astype(BF16), block_values, preferred_element_type=F32
    )
    mixed = mixed * factor[..., None] + update
    return (new_max, running_sum, mixed)


def sweep(carry, keys, values, queries, band_total):
    rows = keys.shape[0]
    lon_tile = keys.shape[1]
    head_size = D // H
    band_block = math.gcd(rows, max(1, 512 // lon_tile))
    blocks = rows // band_block
    block_len = band_block * lon_tile
    keys_blocks = keys.reshape(blocks, block_len, H, head_size)
    values_blocks = values.reshape(blocks, block_len, H, head_size)
    band_index = jnp.arange(rows, dtype=jnp.int32)
    area_rows = jnp.repeat(log_area(band_index, band_total), lon_tile).reshape(blocks, block_len)
    scale = 1.0 / math.sqrt(head_size)

    def step_block(state, inputs):
        return (absorb(state, inputs[0], inputs[1], inputs[2], queries, scale), None)

    result, unused = lax.scan(step_block, carry, (keys_blocks, values_blocks, area_rows))
    return result


def log_area(bands, band_total):
    centre = (bands.astype(F32) + 0.5) * (math.pi / band_total) - math.pi / 2
    return jnp.log(jnp.cos(centre))


def general(state_field, support_rows, window_bands, conv_weight, w_query, w_key, w_value, w_out):
    lat_tile = support_rows.shape[0]
    lon_tile = state_field.shape[2] // 2
    whole_lon = lon_tile * lax.axis_size("lon")
    band_total = lat_tile * lax.axis_size("lat")
    head_size = D // H
    extended = padded(state_field, (("lat", 1),), 2)
    western = shifted(extended[:, :, -1:], "lon", 1)
    extended = jnp.concatenate([western, extended], axis=2)
    features = conv_features(extended, support_rows, conv_weight)
    slot_count = window_bands.shape[0] // lax.axis_size("lat")
    piece = lax.all_gather(features, "lat", axis=0, tiled=True)
    mine = lax.dynamic_slice_in_dim(
        window_bands, lax.axis_index("lat") * slot_count, slot_count, axis=0
    )
    picked = jnp.take(piece, mine, axis=0)
    gathered = lax.all_gather(picked, "lon", axis=1, tiled=True)
    query_count = slot_count * whole_lon
    queries = jnp.dot(gathered.reshape(query_count, D), w_query, preferred_element_type=F32)
    queries = queries.astype(BF16).reshape(query_count, H, head_size)
    initial = (
        jnp.full((query_count, H), -1e30, F32),
        jnp.zeros((query_count, H), F32),
        jnp.zeros((query_count, H, head_size), F32),
    )
    piece_rows = piece.reshape(-1, D)
    keys = jnp.dot(piece_rows, w_key, preferred_element_type=F32).astype(BF16)
    values = jnp.dot(piece_rows, w_value, preferred_element_type=F32).astype(BF16)
    running_max, running_sum, mixed = sweep(
        initial, keys.reshape(piece.shape), values.reshape(piece.shape), queries, band_total
    )
    best = lax.pmax(running_max, "lon")
    factor = jnp.exp(running_max - best)
    scaled_mix = (mixed * factor[..., None]).reshape(slot_count, whole_lon, D)
    scaled_sum = (running_sum * factor).reshape(slot_count, whole_lon, H)
    mix_share, sum_share = (
        lax.psum_scatter(part.astype(BF16), "lon", scatter_dimension=1, tiled=True).astype(F32)
        for part in (scaled_mix, scaled_sum)
    )
    attended = mix_share.reshape(slot_count, lon_tile, H, head_size) / sum_share[..., None]
    attended = attended.astype(BF16).reshape(slot_count * lon_tile, D)
    result = jnp.dot(attended, w_out, preferred_element_type=F32).astype(BF16)
    return result.reshape(slot_count, lon_tile, D)


def exchange(x, lat_mask, lon_mask):
    lats, lons = lax.axis_size("lat"), lax.axis_size("lon")
    pairs = [
        (i * lons + j, (i ^ lat_mask) * lons + (j ^ lon_mask))
        for i in range(lats)
        for j in range(lons)
    ]
    return lax.ppermute(x, AXES, pairs)


def across(x):
    lats, lons = lax.axis_size("lat"), lax.axis_size("lon")
    pairs = []
    for i in range(2, lats, 2):
        for j in range(lons):
            pairs += [((i - 1) * lons + j, i * lons + j), (i * lons + j, (i - 1) * lons + j)]
    return lax.ppermute(x, AXES, pairs)


def rows_kernel(odd_ref, own_ref, lines_ref, far_ref, chip_ref, strided):
    channels, rows, lons = own_ref.shape
    deep = lines_ref.shape[1]
    edge = far_ref.shape[0]
    strided[0 : channels * rows] = own_ref[...].astype(F32).reshape(channels * rows, lons)
    strided[channels * rows :] = jnp.zeros(((deep - channels) * rows, lons), F32)
    lines = [strided[pl.ds(row, deep, stride=rows), :].astype(BF16) for row in range(rows)]
    for row in range(rows):
        lines_ref[row] = lines[row]
    odd = odd_ref[0] != 0
    for row in range(edge):
        top, bottom = lines[row], lines[rows - edge + row]
        far_ref[row] = jnp.where(odd, bottom, top)
        chip_ref[row] = jnp.where(odd, top, bottom)


def rows_of(odd, own, edge, deep):
    _, rows, lons = own.shape
    vmem = pl.BlockSpec(memory_space=pltpu.VMEM)
    return pl.pallas_call(
        rows_kernel,
        out_shape=(
            jax.ShapeDtypeStruct((rows, deep, lons), BF16),
            jax.ShapeDtypeStruct((edge, deep, lons), BF16),
            jax.ShapeDtypeStruct((edge, deep, lons), BF16),
        ),
        in_specs=[pl.BlockSpec(memory_space=pltpu.SMEM), vmem],
        out_specs=(vmem, vmem, vmem),
        scratch_shapes=[pltpu.VMEM((deep * rows, lons), F32)],
        compiler_params=pltpu.CompilerParams(vmem_limit_bytes=4 * 2**20),
        name="rows",
    )(odd, own)


def weights_kernel(weight_ref, picks_ref, out_ref, hits_ref):
    slots, taps, channels, width = weight_ref.shape
    deep = out_ref.shape[0] // (slots * taps)
    blank = jnp.zeros((deep - channels, width), BF16)
    for slot in range(slots):
        for tap in range(taps):
            at = (slot * taps + tap) * deep
            out_ref[at : at + deep] = jnp.concatenate([weight_ref[slot, tap], blank], axis=0)
    picks = picks_ref[...]
    row = lax.broadcasted_iota(jnp.int32, (128, 128), 0)
    lane = lax.broadcasted_iota(jnp.int32, (128, 128), 1)
    for slot in range(slots):
        hits = jnp.zeros((128, 128), F32)
        for band in range(picks.shape[0]):
            hits = jnp.where((row == picks[band, slot]) & (lane == band), 1.0, hits)
        hits_ref[:, slot * 128 : (slot + 1) * 128] = hits.astype(BF16)


def weights_of(conv_weight, picks, deep):
    slots, taps, _, width = conv_weight.shape
    vmem = pl.BlockSpec(memory_space=pltpu.VMEM)
    return pl.pallas_call(
        weights_kernel,
        out_shape=(
            jax.ShapeDtypeStruct((slots * taps * deep, width), BF16),
            jax.ShapeDtypeStruct((128, slots * 128), BF16),
        ),
        in_specs=[vmem, vmem],
        out_specs=(vmem, vmem),
        compiler_params=pltpu.CompilerParams(vmem_limit_bytes=4 * 2**20),
        cost_estimate=pl.CostEstimate(
            flops=0, bytes_accessed=4 * conv_weight.size, transcendentals=0
        ),
        name="weights",
    )(conv_weight, picks)


def columns_kernel(lines_ref, above_ref, below_ref, out_ref):
    rows = [ref[k] for ref in (above_ref, lines_ref, below_ref) for k in range(ref.shape[0])]
    lane = lax.broadcasted_iota(jnp.int32, (1, 128), 1)
    out = jnp.zeros(out_ref.shape, F32)
    for index, row in enumerate(rows):
        last = row[:, row.shape[1] - 128 :].astype(F32)[:, 127:128]
        out = jnp.where(lane == index, last, out)
    out_ref[...] = out.astype(BF16)


def last_columns(lines, above, below):
    vmem = pl.BlockSpec(memory_space=pltpu.VMEM)
    return pl.pallas_call(
        columns_kernel,
        out_shape=jax.ShapeDtypeStruct((lines.shape[1], 128), BF16),
        in_specs=[vmem] * 3,
        out_specs=vmem,
        compiler_params=pltpu.CompilerParams(vmem_limit_bytes=4 * 2**20),
        name="columns",
    )(lines, above, below)


def normed(raw):
    return raw * lax.rsqrt(jnp.mean(raw * raw, axis=-1, keepdims=True) + 1e-06)


def conv_kernel(
    picks_ref, lines_ref, above_ref, below_ref, weight_ref, out_ref, first_ref, taken, patches
):
    _, deep, lons = lines_ref.shape
    width = lons // 2
    bands, slots = picks_ref.shape
    taps = weight_ref.shape[0] // (slots * deep)
    rows = [ref[k] for ref in (above_ref, lines_ref, below_ref) for k in range(ref.shape[0])]
    column = lax.broadcasted_iota(jnp.int32, (lons, taps * lons), 0)
    place = lax.broadcasted_iota(jnp.int32, (lons, taps * lons), 1)
    wanted = 2 * (place % width) + place // lons - 1
    choose = (column == wanted).astype(F32).astype(BF16)
    split = jnp.dot(
        jnp.concatenate(rows, axis=0), choose, preferred_element_type=F32
    ).astype(BF16)
    for row in range(len(rows)):
        taken[row] = split[row * deep : (row + 1) * deep]
    left = lax.broadcasted_iota(jnp.int32, (1, lons), 1) < width
    picks = picks_ref[...]
    for slot in range(slots):
        for band in range(0, bands, 2):
            one, two = taken[picks[band, slot]], taken[picks[band + 1, slot]]
            for tap in range(taps):
                at = (slot * taps + tap) * deep
                patches[at : at + deep, band * width : (band + 2) * width] = jnp.where(
                    left,
                    one[:, tap * lons : (tap + 1) * lons],
                    two[:, tap * lons : (tap + 1) * lons],
                )
    raw = lax.dot_general(
        patches[...], weight_ref[...], (((0,), (0,)), ((), ())), preferred_element_type=F32
    )
    out_ref[...] = normed(raw).astype(BF16)
    for band in range(bands):
        first_ref[band] = raw[band * width : band * width + 8]


def local_features(picks, lines, above, below, weights):
    _, deep, lons = lines.shape
    width = weights.shape[1]
    bands = picks.shape[0]
    count = lines.shape[0] + above.shape[0] + below.shape[0]
    taps = weights.shape[0] // (picks.shape[1] * deep)
    tokens = bands * lons // 2
    vmem = pl.BlockSpec(memory_space=pltpu.VMEM)
    return pl.pallas_call(
        conv_kernel,
        out_shape=(
            jax.ShapeDtypeStruct((tokens, width), BF16),
            jax.ShapeDtypeStruct((bands, 8, width), F32),
        ),
        in_specs=[vmem] * 5,
        out_specs=(vmem, vmem),
        scratch_shapes=[
            pltpu.VMEM((count, deep, taps * lons), BF16),
            pltpu.VMEM((weights.shape[0], tokens), BF16),
        ],
        compiler_params=pltpu.CompilerParams(vmem_limit_bytes=12 * 2**20),
        cost_estimate=pl.CostEstimate(
            flops=2 * weights.size * tokens, bytes_accessed=2 * weights.size, transcendentals=0
        ),
        name="conv",
    )(picks, lines, above, below, weights)


def west_kernel(west_ref, hits_ref, weight_ref, some_ref, first_ref, out_ref):
    deep = west_ref.shape[0]
    slots = hits_ref.shape[1] // 128
    stride = weight_ref.shape[0] // slots
    bands = first_ref.shape[0]
    width = out_ref.shape[0] // bands
    chosen = jnp.dot(west_ref[...], hits_ref[...], preferred_element_type=F32).astype(BF16)
    columns = jnp.concatenate(
        [chosen[:, slot * 128 : (slot + 1) * 128] for slot in range(slots)], axis=0
    )
    filters = jnp.concatenate(
        [weight_ref[slot * stride : slot * stride + deep] for slot in range(slots)], axis=0
    )
    more = lax.dot_general(
        columns, filters, (((0,), (0,)), ((), ())), preferred_element_type=F32
    )
    out_ref[...] = some_ref[...]
    head = lax.broadcasted_iota(jnp.int32, (16, 1), 0) == 0
    for band in range(bands):
        fixed = normed(first_ref[band, 0:1] + more[band : band + 1])
        rest = some_ref[band * width : band * width + 16].astype(F32)
        out_ref[band * width : band * width + 16] = jnp.where(head, fixed, rest).astype(BF16)


def west_added(west, hits, weights, some, first):
    vmem = pl.BlockSpec(memory_space=pltpu.VMEM)
    return pl.pallas_call(
        west_kernel,
        out_shape=jax.ShapeDtypeStruct(some.shape, BF16),
        in_specs=[vmem] * 5,
        out_specs=vmem,
        compiler_params=pltpu.CompilerParams(vmem_limit_bytes=6 * 2**20),
        name="west",
    )(west, hits, weights, some, first)


def select_kernel(where_ref, near_ref, own_ref, pair_ref, other_ref):
    slots, rows, _ = own_ref.shape
    where = where_ref[...]
    for index in range(4 * slots):
        start = pl.multiple_of(where[index, 1], rows)
        picked = near_ref[pl.ds(start, rows)]
        picked = jnp.where(where[index, 0] != 0, picked, jnp.zeros_like(picked))
        if index < 2 * slots:
            (own_ref if index < slots else pair_ref)[index % slots] = picked
        else:
            other_ref[index - 2 * slots] = picked


def selected(where, near, rows):
    slots = where.shape[0] // 4
    vmem = pl.BlockSpec(memory_space=pltpu.VMEM)
    shape = jax.ShapeDtypeStruct((slots, rows, near.shape[1]), near.dtype)
    both = jax.ShapeDtypeStruct((2 * slots, rows, near.shape[1]), near.dtype)
    return pl.pallas_call(
        select_kernel,
        out_shape=(shape, shape, both),
        in_specs=[vmem, vmem],
        out_specs=(vmem, vmem, vmem),
        compiler_params=pltpu.CompilerParams(vmem_limit_bytes=2**20 + 2 * near.size),
        name="select",
    )(where, near)


def split3(x):
    high = x.astype(BF16).astype(F32)
    middle = (x - high).astype(BF16).astype(F32)
    return high, middle, x - high - middle


def attend_kernel(
    keys_count, sel_ref, got_ref, area_ref, wq_ref, wk_ref, wv_ref, *refs
):
    held, (out_ref, *rest) = refs[:keys_count], refs[keys_count:]
    slots, rows, width = sel_ref.shape
    count = slots * rows
    head_size = width // H
    token = (sel_ref[...] + got_ref[...]).reshape(count, width)
    query = jnp.dot(token, wq_ref[...], preferred_element_type=F32).astype(BF16)
    lane = lax.broadcasted_iota(jnp.int32, (1, width), 1) // head_size
    spread = jnp.concatenate(
        [jnp.where(lane == head, query, jnp.zeros_like(query)) for head in range(H)], axis=0
    )
    turned = lax.dot_general(
        spread, wk_ref[...], (((1,), (1,)), ((), ())), preferred_element_type=F32
    )
    turned = (turned * (LOG2E / math.sqrt(head_size))).astype(BF16)
    parts, begin = [], 0
    for ref in held:
        for at in range(0, ref.shape[0], 512):
            chunk = min(512, ref.shape[0] - at)
            parts.append((ref, at, begin, chunk))
            begin += chunk
    top = None
    for ref, at, begin, chunk in parts:
        keys = ref[at : at + chunk]
        block = lax.dot_general(
            turned, keys, (((1,), (1,)), ((), ())), preferred_element_type=F32
        )
        block = block + area_ref[:, begin : begin + chunk]
        best = block[:, 0:128]
        for lanes in range(128, chunk, 128):
            best = jnp.maximum(best, block[:, lanes : lanes + 128])
        best = jnp.max(best, axis=1, keepdims=True)
        if top is not None:
            best = jnp.maximum(top, best)
        weight = jnp.exp2(block - best)
        added = weight[:, 0:128]
        for lanes in range(128, chunk, 128):
            added = added + weight[:, lanes : lanes + 128]
        update = jnp.dot(weight.astype(BF16), keys, preferred_element_type=F32)
        if top is None:
            total, mixed = added, update
        else:
            factor = jnp.exp2(top - best)
            total, mixed = total * factor + added, mixed * factor + update
        top = best
    total = jnp.sum(total, axis=1, keepdims=True)
    value = jnp.dot((mixed / total).astype(BF16), wv_ref[...], preferred_element_type=F32)
    lse = top + jnp.log2(total)
    out = jnp.zeros((count, width), F32)
    stat_lane = lax.broadcasted_iota(jnp.int32, (1, 128), 1)
    stats = jnp.zeros((count, 128), F32)
    for head in range(H):
        out = jnp.where(lane == head, value[head * count : (head + 1) * count], out)
        for order, piece in enumerate(split3(lse[head * count : (head + 1) * count])):
            stats = jnp.where(stat_lane == 3 * head + order, piece, stats)
    out_ref[:, 0:rows, :] = out.reshape(sel_ref.shape).astype(out_ref.dtype)
    stats = stats.reshape(slots, rows, 128)
    if rest:
        rest[0][...] = stats
    else:
        out_ref[:, rows:, :] = jnp.zeros((slots, 16, width), out_ref.dtype)
        for slot in range(slots):
            out_ref[slot, rows:, 0:rows] = stats[slot].T[0:16].astype(out_ref.dtype)


def attended(sent, sel, got, area, w_query, w_key, w_value, held):
    slots, rows, width = sel.shape
    keys = sum(part.shape[0] for part in held)
    count = slots * rows
    vmem = pl.BlockSpec(memory_space=pltpu.VMEM)
    if sent:
        out_shape = (jax.ShapeDtypeStruct((slots, rows + 16, width), BF16),)
    else:
        out_shape = (
            jax.ShapeDtypeStruct((slots, rows, width), F32),
            jax.ShapeDtypeStruct((slots, rows, 128), F32),
        )
    return pl.pallas_call(
        functools.partial(attend_kernel, len(held)),
        out_shape=out_shape,
        in_specs=[vmem] * (6 + len(held)),
        out_specs=(vmem,) * len(out_shape),
        compiler_params=pltpu.CompilerParams(vmem_limit_bytes=20 * 2**20),
        cost_estimate=pl.CostEstimate(
            flops=4 * H * count * keys * width,
            bytes_accessed=2 * keys * width,
            transcendentals=H * count * keys,
        ),
        name="attend_sent" if sent else "attend_kept",
    )(sel, got, area, w_query, w_key, w_value, *held)


def finish_kernel(keep_ref, lse_ref, got_ref, wo_ref, out_ref):
    slots, rows, width = keep_ref.shape
    count = slots * rows
    keep = keep_ref[...].reshape(count, width)
    got = got_ref[:, 0:rows, :].astype(F32).reshape(count, width)
    ours = lse_ref[...].reshape(count, 128).astype(BF16)
    piece = lax.broadcasted_iota(jnp.int32, (128, width), 0) // 3
    head = lax.broadcasted_iota(jnp.int32, (128, width), 1) // (width // H)
    spread = (piece == head).astype(F32).astype(BF16)
    own = jnp.dot(ours, spread, preferred_element_type=F32)
    far = jnp.concatenate(
        [
            lax.dot_general(
                got_ref[slot, rows:, 0:rows], spread[0:16], (((0,), (0,)), ((), ())),
                preferred_element_type=F32,
            )
            for slot in range(slots)
        ],
        axis=0,
    )
    top = jnp.maximum(own, far)
    own = jnp.exp2(own - top)
    far = jnp.exp2(far - top)
    mixed = ((keep * own + got * far) / (own + far)).astype(BF16)
    result = jnp.dot(mixed, wo_ref[...], preferred_element_type=F32).astype(BF16)
    out_ref[...] = result.reshape(out_ref.shape)


def finished(keep, lse, got, w_out):
    vmem = pl.BlockSpec(memory_space=pltpu.VMEM)
    return pl.pallas_call(
        finish_kernel,
        out_shape=jax.ShapeDtypeStruct(keep.shape, BF16),
        in_specs=[vmem] * 4,
        out_specs=vmem,
        compiler_params=pltpu.CompilerParams(vmem_limit_bytes=4 * 2**20),
        name="finish",
    )(keep, lse, got, w_out)


def gathered(block, masks):
    blocks = {(0, 0): block}
    for mask in masks:
        blocks[mask] = exchange(block, *mask)
    whole = (sum(mask[0] for mask in masks), sum(mask[1] for mask in masks))
    if whole not in blocks:
        blocks[whole] = exchange(block, *whole)
    for size in range(2, len(masks)):
        for start in range(len(masks)):
            chosen = [masks[(start + k) % len(masks)] for k in range(size)]
            key = (sum(mask[0] for mask in chosen), sum(mask[1] for mask in chosen))
            step = chosen[-1]
            blocks[key] = exchange(blocks[key[0] ^ step[0], key[1] ^ step[1]], *step)
    return blocks


def halves(state_field, support_rows, window_bands, conv_weight, w_query, w_key, w_value, w_out):
    lats = lax.axis_size("lat")
    lat, lon = lax.axis_index("lat"), lax.axis_index("lon")
    channels, rows, lons = state_field.shape
    lat_tile = support_rows.shape[0]
    lon_tile = lons // 2
    band_total = lat_tile * lats
    pair = lats // 2

    deep = -(-channels // 16) * 16
    odd = lat & 1
    lines, out_far, out_chip = rows_of(odd.astype(jnp.int32).reshape(1), state_field, 2, deep)
    far_rows = across(out_far)
    chip_rows = exchange(out_chip, 1, 0)
    above = jnp.where(odd != 0, chip_rows, far_rows)
    below = jnp.where(odd != 0, far_rows, chip_rows)
    west = exchange(last_columns(lines, above, below), 0, 1)
    picks = 2 * jnp.arange(lat_tile, dtype=jnp.int32)[:, None] + support_rows + 2
    weights, hits = weights_of(conv_weight, picks, deep)
    some, first = local_features(picks, lines, above, below, weights)
    features = west_added(west, hits, weights, some, first)

    bits = [1 << k for k in range(1, lats.bit_length() - 1) if 1 << k != pair]
    masks = [(0, 1)] + [(bit, 0) for bit in bits]
    blocks = gathered(features, masks)
    order = [(i, j) for i in range(0, pair, 2) for j in range(2)]
    near = jnp.concatenate([blocks[key] for key in order], axis=0)

    size = lat_tile * lon_tile
    slot_count = window_bands.shape[0] // lats
    sides = jnp.stack([lat, lat ^ pair, lat ^ 1, lat ^ pair ^ 1])
    wanted = window_bands[
        (sides[:, None] * slot_count + jnp.arange(slot_count)[None, :]).reshape(-1)
    ]
    owner = wanted // lat_tile
    apart = owner ^ lat
    place = (apart & (pair - 2)) * size + wanted % lat_tile * lon_tile
    within = apart & (pair | 1) == 0
    where = jnp.stack([within.astype(jnp.int32), place.astype(jnp.int32)], axis=1)
    sel_own, sel_pair, sel_other = selected(where, near, lon_tile)
    got_other = exchange(sel_other, 1, 0)
    sel_own = sel_own + got_other[:slot_count]
    sel_pair = sel_pair + got_other[slot_count:]
    sel_own, sel_pair, near = lax.optimization_barrier((sel_own, sel_pair, near))
    got_pair = exchange(sel_own, pair, 0)
    got_own = exchange(sel_pair, pair, 0)
    held = (near, exchange(near, 1, 0))

    step = jnp.arange(2 * len(order) * lat_tile, dtype=jnp.int32)
    masks = (step // lat_tile) % len(order)
    tile = lat ^ ((masks & ~1) | (step // (len(order) * lat_tile)))
    key_band = tile * lat_tile + step % lat_tile
    area = LOG2E * log_area(key_band, band_total)
    area = jnp.repeat(area, lon_tile)[None, :]
    shared = (area, w_query, w_key, w_value, held)
    (send,) = attended(True, sel_pair, got_pair, *shared)
    received = exchange(send, pair, 0)
    keep, lse = attended(False, sel_own, got_own, *shared)
    return finished(keep, lse, received, w_out)


def per_device(state_field, support_rows, *rest):
    lats, lons = lax.axis_size("lat"), lax.axis_size("lon")
    _, rows, columns = state_field.shape
    paired = lons == 2 and lats >= 4 and lats & (lats - 1) == 0
    tiled = columns == 128 and rows % 8 == 0 and support_rows.shape[0] % 2 == 0
    plan = halves if paired and tiled else general
    return plan(state_field, support_rows, *rest)


def solution(mesh):
    return jax.shard_map(
        per_device,
        mesh=mesh,
        in_specs=(P(None, "lat", "lon"), P("lat", None), P(), P(), P(), P(), P(), P()),
        out_specs=P("lat", "lon", None),
        check_vma=False,
    )
```

```python
import functools
import math

import jax
import jax.numpy as jnp
from jax import lax
from jax.experimental import pallas as pl
from jax.experimental.pallas import tpu as pltpu
from jax.sharding import PartitionSpec as P

D = 256
H = 4
AXES = ("lat", "lon")
LOG2E = 1.0 / math.log(2.0)
F32 = jnp.float32
BF16 = jnp.bfloat16


def padded(x, sides, width):
    for axis, dim in sides:
        devices, length = (lax.axis_size(axis), x.shape[dim])
        up = [(i, (i + 1) % devices) for i in range(devices - 1)]
        down = [(j, i) for i, j in up]
        last = lax.slice_in_dim(x, length - width, length, axis=dim)
        leading = lax.slice_in_dim(x, 0, width, axis=dim)
        before = lax.ppermute(last, axis, up)
        after = lax.ppermute(leading, axis, down)
        x = jnp.concatenate([before, x, after], axis=dim)
    return x


def shifted(x, axis, by):
    devices = lax.axis_size(axis)
    return lax.ppermute(x, axis, [(i, (i + by) % devices) for i in range(devices)])


def conv_features(extended, support_rows, conv_weight):
    bands = support_rows.shape[0]
    width = (extended.shape[2] - 1) // 2
    row_index = 2 * jnp.arange(bands, dtype=jnp.int32)[:, None] + support_rows + 2
    picked = jnp.take(extended, row_index, axis=1)
    tapped = jnp.stack(
        [picked[..., column_tap : column_tap + 2 * width : 2] for column_tap in range(3)], axis=3
    )
    patches = jnp.transpose(tapped, (1, 4, 2, 3, 0)).reshape(bands * width, -1)
    raw = jnp.dot(
        patches, conv_weight.reshape(-1, conv_weight.shape[-1]), preferred_element_type=F32
    )
    factor = lax.rsqrt(jnp.mean(raw * raw, axis=-1, keepdims=True) + 1e-06)
    return (raw * factor).astype(BF16).reshape(bands, width, -1)


def absorb(carry, block_keys, block_values, block_area, queries, scale):
    running_max, running_sum, mixed = carry
    scores = (
        jnp.einsum("qhd,khd->qhk", queries, block_keys, preferred_element_type=F32) * scale
        + block_area
    )
    new_max = jnp.maximum(running_max, jnp.max(scores, axis=-1))
    factor = jnp.exp(running_max - new_max)
    weights = jnp.exp(scores - new_max[..., None])
    running_sum = running_sum * factor + jnp.sum(weights, axis=-1)
    update = jnp.einsum(
        "qhk,khd->qhd", weights.astype(BF16), block_values, preferred_element_type=F32
    )
    mixed = mixed * factor[..., None] + update
    return (new_max, running_sum, mixed)


def sweep(carry, keys, values, queries, band_total):
    rows = keys.shape[0]
    lon_tile = keys.shape[1]
    head_size = D // H
    band_block = math.gcd(rows, max(1, 512 // lon_tile))
    blocks = rows // band_block
    block_len = band_block * lon_tile
    keys_blocks = keys.reshape(blocks, block_len, H, head_size)
    values_blocks = values.reshape(blocks, block_len, H, head_size)
    band_index = jnp.arange(rows, dtype=jnp.int32)
    area_rows = jnp.repeat(log_area(band_index, band_total), lon_tile).reshape(blocks, block_len)
    scale = 1.0 / math.sqrt(head_size)

    def step_block(state, inputs):
        return (absorb(state, inputs[0], inputs[1], inputs[2], queries, scale), None)

    result, unused = lax.scan(step_block, carry, (keys_blocks, values_blocks, area_rows))
    return result


def log_area(bands, band_total):
    centre = (bands.astype(F32) + 0.5) * (math.pi / band_total) - math.pi / 2
    return jnp.log(jnp.cos(centre))


def general(state_field, support_rows, window_bands, conv_weight, w_query, w_key, w_value, w_out):
    lat_tile = support_rows.shape[0]
    lon_tile = state_field.shape[2] // 2
    whole_lon = lon_tile * lax.axis_size("lon")
    band_total = lat_tile * lax.axis_size("lat")
    head_size = D // H
    extended = padded(state_field, (("lat", 1),), 2)
    western = shifted(extended[:, :, -1:], "lon", 1)
    extended = jnp.concatenate([western, extended], axis=2)
    features = conv_features(extended, support_rows, conv_weight)
    slot_count = window_bands.shape[0] // lax.axis_size("lat")
    piece = lax.all_gather(features, "lat", axis=0, tiled=True)
    mine = lax.dynamic_slice_in_dim(
        window_bands, lax.axis_index("lat") * slot_count, slot_count, axis=0
    )
    picked = jnp.take(piece, mine, axis=0)
    gathered = lax.all_gather(picked, "lon", axis=1, tiled=True)
    query_count = slot_count * whole_lon
    queries = jnp.dot(gathered.reshape(query_count, D), w_query, preferred_element_type=F32)
    queries = queries.astype(BF16).reshape(query_count, H, head_size)
    initial = (
        jnp.full((query_count, H), -1e30, F32),
        jnp.zeros((query_count, H), F32),
        jnp.zeros((query_count, H, head_size), F32),
    )
    piece_rows = piece.reshape(-1, D)
    keys = jnp.dot(piece_rows, w_key, preferred_element_type=F32).astype(BF16)
    values = jnp.dot(piece_rows, w_value, preferred_element_type=F32).astype(BF16)
    running_max, running_sum, mixed = sweep(
        initial, keys.reshape(piece.shape), values.reshape(piece.shape), queries, band_total
    )
    best = lax.pmax(running_max, "lon")
    factor = jnp.exp(running_max - best)
    scaled_mix = (mixed * factor[..., None]).reshape(slot_count, whole_lon, D)
    scaled_sum = (running_sum * factor).reshape(slot_count, whole_lon, H)
    mix_share, sum_share = (
        lax.psum_scatter(part.astype(BF16), "lon", scatter_dimension=1, tiled=True).astype(F32)
        for part in (scaled_mix, scaled_sum)
    )
    attended = mix_share.reshape(slot_count, lon_tile, H, head_size) / sum_share[..., None]
    attended = attended.astype(BF16).reshape(slot_count * lon_tile, D)
    result = jnp.dot(attended, w_out, preferred_element_type=F32).astype(BF16)
    return result.reshape(slot_count, lon_tile, D)


def exchange(x, lat_mask, lon_mask):
    lats, lons = lax.axis_size("lat"), lax.axis_size("lon")
    pairs = [
        (i * lons + j, (i ^ lat_mask) * lons + (j ^ lon_mask))
        for i in range(lats)
        for j in range(lons)
    ]
    return lax.ppermute(x, AXES, pairs)


def across(x):
    lats, lons = lax.axis_size("lat"), lax.axis_size("lon")
    pairs = []
    for i in range(2, lats, 2):
        for j in range(lons):
            pairs += [((i - 1) * lons + j, i * lons + j), (i * lons + j, (i - 1) * lons + j)]
    return lax.ppermute(x, AXES, pairs)


def rows_kernel(odd_ref, own_ref, lines_ref, far_ref, chip_ref, strided):
    channels, rows, lons = own_ref.shape
    deep = lines_ref.shape[1]
    edge = far_ref.shape[0]
    strided[0 : channels * rows] = own_ref[...].astype(F32).reshape(channels * rows, lons)
    strided[channels * rows :] = jnp.zeros(((deep - channels) * rows, lons), F32)
    lines = [strided[pl.ds(row, deep, stride=rows), :].astype(BF16) for row in range(rows)]
    for row in range(rows):
        lines_ref[row] = lines[row]
    odd = odd_ref[0] != 0
    for row in range(edge):
        top, bottom = lines[row], lines[rows - edge + row]
        far_ref[row] = jnp.where(odd, bottom, top)
        chip_ref[row] = jnp.where(odd, top, bottom)


def rows_of(odd, own, edge, deep):
    _, rows, lons = own.shape
    vmem = pl.BlockSpec(memory_space=pltpu.VMEM)
    return pl.pallas_call(
        rows_kernel,
        out_shape=(
            jax.ShapeDtypeStruct((rows, deep, lons), BF16),
            jax.ShapeDtypeStruct((edge, deep, lons), BF16),
            jax.ShapeDtypeStruct((edge, deep, lons), BF16),
        ),
        in_specs=[pl.BlockSpec(memory_space=pltpu.SMEM), vmem],
        out_specs=(vmem, vmem, vmem),
        scratch_shapes=[pltpu.VMEM((deep * rows, lons), F32)],
        compiler_params=pltpu.CompilerParams(vmem_limit_bytes=4 * 2**20),
        name="rows",
    )(odd, own)


def weights_kernel(weight_ref, picks_ref, out_ref, hits_ref):
    slots, taps, channels, width = weight_ref.shape
    deep = out_ref.shape[0] // (slots * taps)
    blank = jnp.zeros((deep - channels, width), BF16)
    for slot in range(slots):
        for tap in range(taps):
            at = (slot * taps + tap) * deep
            out_ref[at : at + deep] = jnp.concatenate([weight_ref[slot, tap], blank], axis=0)
    picks = picks_ref[...]
    row = lax.broadcasted_iota(jnp.int32, (128, 128), 0)
    lane = lax.broadcasted_iota(jnp.int32, (128, 128), 1)
    for slot in range(slots):
        hits = jnp.zeros((128, 128), F32)
        for band in range(picks.shape[0]):
            hits = jnp.where((row == picks[band, slot]) & (lane == band), 1.0, hits)
        hits_ref[:, slot * 128 : (slot + 1) * 128] = hits.astype(BF16)


def weights_of(conv_weight, picks, deep):
    slots, taps, _, width = conv_weight.shape
    vmem = pl.BlockSpec(memory_space=pltpu.VMEM)
    return pl.pallas_call(
        weights_kernel,
        out_shape=(
            jax.ShapeDtypeStruct((slots * taps * deep, width), BF16),
            jax.ShapeDtypeStruct((128, slots * 128), BF16),
        ),
        in_specs=[vmem, vmem],
        out_specs=(vmem, vmem),
        compiler_params=pltpu.CompilerParams(vmem_limit_bytes=4 * 2**20),
        cost_estimate=pl.CostEstimate(
            flops=0, bytes_accessed=4 * conv_weight.size, transcendentals=0
        ),
        name="weights",
    )(conv_weight, picks)


def columns_kernel(lines_ref, above_ref, below_ref, out_ref):
    rows = [ref[k] for ref in (above_ref, lines_ref, below_ref) for k in range(ref.shape[0])]
    lane = lax.broadcasted_iota(jnp.int32, (1, 128), 1)
    out = jnp.zeros(out_ref.shape, F32)
    for index, row in enumerate(rows):
        last = row[:, row.shape[1] - 128 :].astype(F32)[:, 127:128]
        out = jnp.where(lane == index, last, out)
    out_ref[...] = out.astype(BF16)


def last_columns(lines, above, below):
    vmem = pl.BlockSpec(memory_space=pltpu.VMEM)
    return pl.pallas_call(
        columns_kernel,
        out_shape=jax.ShapeDtypeStruct((lines.shape[1], 128), BF16),
        in_specs=[vmem] * 3,
        out_specs=vmem,
        compiler_params=pltpu.CompilerParams(vmem_limit_bytes=4 * 2**20),
        name="columns",
    )(lines, above, below)


def normed(raw):
    return raw * lax.rsqrt(jnp.mean(raw * raw, axis=-1, keepdims=True) + 1e-06)


def conv_kernel(
    picks_ref, lines_ref, above_ref, below_ref, weight_ref, out_ref, first_ref, taken, patches
):
    _, deep, lons = lines_ref.shape
    width = lons // 2
    bands, slots = picks_ref.shape
    taps = weight_ref.shape[0] // (slots * deep)
    rows = [ref[k] for ref in (above_ref, lines_ref, below_ref) for k in range(ref.shape[0])]
    column = lax.broadcasted_iota(jnp.int32, (lons, taps * lons), 0)
    place = lax.broadcasted_iota(jnp.int32, (lons, taps * lons), 1)
    wanted = 2 * (place % width) + place // lons - 1
    choose = (column == wanted).astype(F32).astype(BF16)
    split = jnp.dot(
        jnp.concatenate(rows, axis=0), choose, preferred_element_type=F32
    ).astype(BF16)
    for row in range(len(rows)):
        taken[row] = split[row * deep : (row + 1) * deep]
    left = lax.broadcasted_iota(jnp.int32, (1, lons), 1) < width
    picks = picks_ref[...]
    for slot in range(slots):
        for band in range(0, bands, 2):
            one, two = taken[picks[band, slot]], taken[picks[band + 1, slot]]
            for tap in range(taps):
                at = (slot * taps + tap) * deep
                patches[at : at + deep, band * width : (band + 2) * width] = jnp.where(
                    left,
                    one[:, tap * lons : (tap + 1) * lons],
                    two[:, tap * lons : (tap + 1) * lons],
                )
    raw = lax.dot_general(
        patches[...], weight_ref[...], (((0,), (0,)), ((), ())), preferred_element_type=F32
    )
    out_ref[...] = normed(raw).astype(BF16)
    for band in range(bands):
        first_ref[band] = raw[band * width : band * width + 8]


def local_features(picks, lines, above, below, weights):
    _, deep, lons = lines.shape
    width = weights.shape[1]
    bands = picks.shape[0]
    count = lines.shape[0] + above.shape[0] + below.shape[0]
    taps = weights.shape[0] // (picks.shape[1] * deep)
    tokens = bands * lons // 2
    vmem = pl.BlockSpec(memory_space=pltpu.VMEM)
    return pl.pallas_call(
        conv_kernel,
        out_shape=(
            jax.ShapeDtypeStruct((tokens, width), BF16),
            jax.ShapeDtypeStruct((bands, 8, width), F32),
        ),
        in_specs=[vmem] * 5,
        out_specs=(vmem, vmem),
        scratch_shapes=[
            pltpu.VMEM((count, deep, taps * lons), BF16),
            pltpu.VMEM((weights.shape[0], tokens), BF16),
        ],
        compiler_params=pltpu.CompilerParams(vmem_limit_bytes=12 * 2**20),
        cost_estimate=pl.CostEstimate(
            flops=2 * weights.size * tokens, bytes_accessed=2 * weights.size, transcendentals=0
        ),
        name="conv",
    )(picks, lines, above, below, weights)


def west_kernel(west_ref, hits_ref, weight_ref, some_ref, first_ref, out_ref):
    deep = west_ref.shape[0]
    slots = hits_ref.shape[1] // 128
    stride = weight_ref.shape[0] // slots
    bands = first_ref.shape[0]
    width = out_ref.shape[0] // bands
    chosen = jnp.dot(west_ref[...], hits_ref[...], preferred_element_type=F32).astype(BF16)
    columns = jnp.concatenate(
        [chosen[:, slot * 128 : (slot + 1) * 128] for slot in range(slots)], axis=0
    )
    filters = jnp.concatenate(
        [weight_ref[slot * stride : slot * stride + deep] for slot in range(slots)], axis=0
    )
    more = lax.dot_general(
        columns, filters, (((0,), (0,)), ((), ())), preferred_element_type=F32
    )
    out_ref[...] = some_ref[...]
    head = lax.broadcasted_iota(jnp.int32, (16, 1), 0) == 0
    for band in range(bands):
        fixed = normed(first_ref[band, 0:1] + more[band : band + 1])
        rest = some_ref[band * width : band * width + 16].astype(F32)
        out_ref[band * width : band * width + 16] = jnp.where(head, fixed, rest).astype(BF16)


def west_added(west, hits, weights, some, first):
    vmem = pl.BlockSpec(memory_space=pltpu.VMEM)
    return pl.pallas_call(
        west_kernel,
        out_shape=jax.ShapeDtypeStruct(some.shape, BF16),
        in_specs=[vmem] * 5,
        out_specs=vmem,
        compiler_params=pltpu.CompilerParams(vmem_limit_bytes=6 * 2**20),
        name="west",
    )(west, hits, weights, some, first)


def select_kernel(where_ref, near_ref, own_ref, pair_ref, other_ref):
    slots, rows, _ = own_ref.shape
    where = where_ref[...]
    for index in range(4 * slots):
        start = pl.multiple_of(where[index, 1], rows)
        picked = near_ref[pl.ds(start, rows)]
        picked = jnp.where(where[index, 0] != 0, picked, jnp.zeros_like(picked))
        if index < 2 * slots:
            (own_ref if index < slots else pair_ref)[index % slots] = picked
        else:
            other_ref[index - 2 * slots] = picked


def selected(where, near, rows):
    slots = where.shape[0] // 4
    vmem = pl.BlockSpec(memory_space=pltpu.VMEM)
    shape = jax.ShapeDtypeStruct((slots, rows, near.shape[1]), near.dtype)
    both = jax.ShapeDtypeStruct((2 * slots, rows, near.shape[1]), near.dtype)
    return pl.pallas_call(
        select_kernel,
        out_shape=(shape, shape, both),
        in_specs=[vmem, vmem],
        out_specs=(vmem, vmem, vmem),
        compiler_params=pltpu.CompilerParams(vmem_limit_bytes=2**20 + 2 * near.size),
        name="select",
    )(where, near)


def split3(x):
    high = x.astype(BF16).astype(F32)
    middle = (x - high).astype(BF16).astype(F32)
    return high, middle, x - high - middle


def fold_kernel(wq_ref, wk_ref, out_ref):
    width = wq_ref.shape[1]
    head_size = width // H
    lane = lax.broadcasted_iota(jnp.int32, (1, width), 1) // head_size
    query = wq_ref[...]
    for head in range(H):
        part = jnp.where(lane == head, query, jnp.zeros_like(query))
        both = lax.dot_general(
            part, wk_ref[...], (((1,), (1,)), ((), ())), preferred_element_type=F32
        )
        both = both * (LOG2E / math.sqrt(head_size))
        out_ref[:, head * width : (head + 1) * width] = both.astype(BF16)


def folded(w_query, w_key):
    vmem = pl.BlockSpec(memory_space=pltpu.VMEM)
    return pl.pallas_call(
        fold_kernel,
        out_shape=jax.ShapeDtypeStruct((w_query.shape[0], H * w_key.shape[0]), BF16),
        in_specs=[vmem, vmem],
        out_specs=vmem,
        compiler_params=pltpu.CompilerParams(vmem_limit_bytes=4 * 2**20),
        name="fold",
    )(w_query, w_key)


def attend_kernel(
    keys_count, sel_ref, got_ref, area_ref, fold_ref, wv_ref, *refs
):
    held, (out_ref, *rest) = refs[:keys_count], refs[keys_count:]
    slots, rows, width = sel_ref.shape
    count = slots * rows
    head_size = width // H
    token = (sel_ref[...] + got_ref[...]).reshape(count, width)
    lane = lax.broadcasted_iota(jnp.int32, (1, width), 1) // head_size
    turned = jnp.dot(token, fold_ref[...], preferred_element_type=F32).astype(BF16)
    turned = jnp.concatenate(
        [turned[:, head * width : (head + 1) * width] for head in range(H)], axis=0
    )
    parts, begin = [], 0
    for ref in held:
        for at in range(0, ref.shape[0], 512):
            chunk = min(512, ref.shape[0] - at)
            parts.append((ref, at, begin, chunk))
            begin += chunk
    top = None
    for ref, at, begin, chunk in parts:
        keys = ref[at : at + chunk]
        block = lax.dot_general(
            turned, keys, (((1,), (1,)), ((), ())), preferred_element_type=F32
        )
        block = block + area_ref[:, begin : begin + chunk]
        best = block[:, 0:128]
        for lanes in range(128, chunk, 128):
            best = jnp.maximum(best, block[:, lanes : lanes + 128])
        best = jnp.max(best, axis=1, keepdims=True)
        if top is not None:
            best = jnp.maximum(top, best)
        weight = jnp.exp2(block - best)
        added = weight[:, 0:128]
        for lanes in range(128, chunk, 128):
            added = added + weight[:, lanes : lanes + 128]
        update = jnp.dot(weight.astype(BF16), keys, preferred_element_type=F32)
        if top is None:
            total, mixed = added, update
        else:
            factor = jnp.exp2(top - best)
            total, mixed = total * factor + added, mixed * factor + update
        top = best
    total = jnp.sum(total, axis=1, keepdims=True)
    value = jnp.dot((mixed / total).astype(BF16), wv_ref[...], preferred_element_type=F32)
    lse = top + jnp.log2(total)
    out = jnp.zeros((count, width), F32)
    stat_lane = lax.broadcasted_iota(jnp.int32, (1, 128), 1)
    stats = jnp.zeros((count, 128), F32)
    for head in range(H):
        out = jnp.where(lane == head, value[head * count : (head + 1) * count], out)
        for order, piece in enumerate(split3(lse[head * count : (head + 1) * count])):
            stats = jnp.where(stat_lane == 3 * head + order, piece, stats)
    out_ref[:, 0:rows, :] = out.reshape(sel_ref.shape).astype(out_ref.dtype)
    stats = stats.reshape(slots, rows, 128)
    if rest:
        rest[0][...] = stats
    else:
        out_ref[:, rows:, :] = jnp.zeros((slots, 16, width), out_ref.dtype)
        for slot in range(slots):
            out_ref[slot, rows:, 0:rows] = stats[slot].T[0:16].astype(out_ref.dtype)


def attended(sent, sel, got, area, fold, w_value, held):
    slots, rows, width = sel.shape
    keys = sum(part.shape[0] for part in held)
    count = slots * rows
    vmem = pl.BlockSpec(memory_space=pltpu.VMEM)
    if sent:
        out_shape = (jax.ShapeDtypeStruct((slots, rows + 16, width), BF16),)
    else:
        out_shape = (
            jax.ShapeDtypeStruct((slots, rows, width), F32),
            jax.ShapeDtypeStruct((slots, rows, 128), F32),
        )
    return pl.pallas_call(
        functools.partial(attend_kernel, len(held)),
        out_shape=out_shape,
        in_specs=[vmem] * (5 + len(held)),
        out_specs=(vmem,) * len(out_shape),
        compiler_params=pltpu.CompilerParams(vmem_limit_bytes=20 * 2**20),
        cost_estimate=pl.CostEstimate(
            flops=4 * H * count * keys * width,
            bytes_accessed=2 * keys * width,
            transcendentals=H * count * keys,
        ),
        name="attend_sent" if sent else "attend_kept",
    )(sel, got, area, fold, w_value, *held)


def finish_kernel(keep_ref, lse_ref, got_ref, wo_ref, out_ref):
    slots, rows, width = keep_ref.shape
    count = slots * rows
    keep = keep_ref[...].reshape(count, width)
    got = got_ref[:, 0:rows, :].astype(F32).reshape(count, width)
    ours = lse_ref[...].reshape(count, 128).astype(BF16)
    piece = lax.broadcasted_iota(jnp.int32, (128, width), 0) // 3
    head = lax.broadcasted_iota(jnp.int32, (128, width), 1) // (width // H)
    spread = (piece == head).astype(F32).astype(BF16)
    own = jnp.dot(ours, spread, preferred_element_type=F32)
    far = jnp.concatenate(
        [
            lax.dot_general(
                got_ref[slot, rows:, 0:rows], spread[0:16], (((0,), (0,)), ((), ())),
                preferred_element_type=F32,
            )
            for slot in range(slots)
        ],
        axis=0,
    )
    top = jnp.maximum(own, far)
    own = jnp.exp2(own - top)
    far = jnp.exp2(far - top)
    mixed = ((keep * own + got * far) / (own + far)).astype(BF16)
    result = jnp.dot(mixed, wo_ref[...], preferred_element_type=F32).astype(BF16)
    out_ref[...] = result.reshape(out_ref.shape)


def finished(keep, lse, got, w_out):
    vmem = pl.BlockSpec(memory_space=pltpu.VMEM)
    return pl.pallas_call(
        finish_kernel,
        out_shape=jax.ShapeDtypeStruct(keep.shape, BF16),
        in_specs=[vmem] * 4,
        out_specs=vmem,
        compiler_params=pltpu.CompilerParams(vmem_limit_bytes=4 * 2**20),
        name="finish",
    )(keep, lse, got, w_out)


def gathered(block, masks):
    blocks = {(0, 0): block}
    for mask in masks:
        blocks[mask] = exchange(block, *mask)
    whole = (sum(mask[0] for mask in masks), sum(mask[1] for mask in masks))
    if whole not in blocks:
        blocks[whole] = exchange(block, *whole)
    for size in range(2, len(masks)):
        for start in range(len(masks)):
            chosen = [masks[(start + k) % len(masks)] for k in range(size)]
            key = (sum(mask[0] for mask in chosen), sum(mask[1] for mask in chosen))
            step = chosen[-1]
            blocks[key] = exchange(blocks[key[0] ^ step[0], key[1] ^ step[1]], *step)
    return blocks


def halves(state_field, support_rows, window_bands, conv_weight, w_query, w_key, w_value, w_out):
    lats = lax.axis_size("lat")
    lat, lon = lax.axis_index("lat"), lax.axis_index("lon")
    channels, rows, lons = state_field.shape
    lat_tile = support_rows.shape[0]
    lon_tile = lons // 2
    band_total = lat_tile * lats
    pair = lats // 2

    deep = -(-channels // 16) * 16
    odd = lat & 1
    lines, out_far, out_chip = rows_of(odd.astype(jnp.int32).reshape(1), state_field, 2, deep)
    far_rows = across(out_far)
    chip_rows = exchange(out_chip, 1, 0)
    above = jnp.where(odd != 0, chip_rows, far_rows)
    below = jnp.where(odd != 0, far_rows, chip_rows)
    west = exchange(last_columns(lines, above, below), 0, 1)
    picks = 2 * jnp.arange(lat_tile, dtype=jnp.int32)[:, None] + support_rows + 2
    fold = folded(w_query, w_key)
    weights, hits = weights_of(conv_weight, picks, deep)
    some, first = local_features(picks, lines, above, below, weights)
    features = west_added(west, hits, weights, some, first)

    bits = [1 << k for k in range(1, lats.bit_length() - 1) if 1 << k != pair]
    masks = [(0, 1)] + [(bit, 0) for bit in bits]
    blocks = gathered(features, masks)
    order = [(i, j) for i in range(0, pair, 2) for j in range(2)]
    near = jnp.concatenate([blocks[key] for key in order], axis=0)

    size = lat_tile * lon_tile
    slot_count = window_bands.shape[0] // lats
    sides = jnp.stack([lat, lat ^ pair, lat ^ 1, lat ^ pair ^ 1])
    wanted = window_bands[
        (sides[:, None] * slot_count + jnp.arange(slot_count)[None, :]).reshape(-1)
    ]
    owner = wanted // lat_tile
    apart = owner ^ lat
    place = (apart & (pair - 2)) * size + wanted % lat_tile * lon_tile
    within = apart & (pair | 1) == 0
    where = jnp.stack([within.astype(jnp.int32), place.astype(jnp.int32)], axis=1)
    sel_own, sel_pair, sel_other = selected(where, near, lon_tile)
    got_other = exchange(sel_other, 1, 0)
    sel_own = sel_own + got_other[:slot_count]
    sel_pair = sel_pair + got_other[slot_count:]
    sel_own, sel_pair, near = lax.optimization_barrier((sel_own, sel_pair, near))
    got_pair = exchange(sel_own, pair, 0)
    got_own = exchange(sel_pair, pair, 0)
    held = (near, exchange(near, 1, 0))

    step = jnp.arange(2 * len(order) * lat_tile, dtype=jnp.int32)
    masks = (step // lat_tile) % len(order)
    tile = lat ^ ((masks & ~1) | (step // (len(order) * lat_tile)))
    key_band = tile * lat_tile + step % lat_tile
    area = LOG2E * log_area(key_band, band_total)
    area = jnp.repeat(area, lon_tile)[None, :]
    shared = (area, fold, w_value, held)
    (send,) = attended(True, sel_pair, got_pair, *shared)
    received = exchange(send, pair, 0)
    keep, lse = attended(False, sel_own, got_own, *shared)
    return finished(keep, lse, received, w_out)


def per_device(state_field, support_rows, *rest):
    lats, lons = lax.axis_size("lat"), lax.axis_size("lon")
    _, rows, columns = state_field.shape
    paired = lons == 2 and lats >= 4 and lats & (lats - 1) == 0
    tiled = columns == 128 and rows % 8 == 0 and support_rows.shape[0] % 2 == 0
    plan = halves if paired and tiled else general
    return plan(state_field, support_rows, *rest)


def solution(mesh):
    return jax.shard_map(
        per_device,
        mesh=mesh,
        in_specs=(P(None, "lat", "lon"), P("lat", None), P(), P(), P(), P(), P(), P()),
        out_specs=P("lat", "lon", None),
        check_vma=False,
    )
```

```python
import functools
import math

import jax
import jax.numpy as jnp
from jax import lax
from jax.experimental import pallas as pl
from jax.experimental.pallas import tpu as pltpu
from jax.sharding import PartitionSpec as P

D = 256
H = 4
AXES = ("lat", "lon")
LOG2E = 1.0 / math.log(2.0)
F32 = jnp.float32
BF16 = jnp.bfloat16


def padded(x, sides, width):
    for axis, dim in sides:
        devices, length = (lax.axis_size(axis), x.shape[dim])
        up = [(i, (i + 1) % devices) for i in range(devices - 1)]
        down = [(j, i) for i, j in up]
        last = lax.slice_in_dim(x, length - width, length, axis=dim)
        leading = lax.slice_in_dim(x, 0, width, axis=dim)
        before = lax.ppermute(last, axis, up)
        after = lax.ppermute(leading, axis, down)
        x = jnp.concatenate([before, x, after], axis=dim)
    return x


def shifted(x, axis, by):
    devices = lax.axis_size(axis)
    return lax.ppermute(x, axis, [(i, (i + by) % devices) for i in range(devices)])


def conv_features(extended, support_rows, conv_weight):
    bands = support_rows.shape[0]
    width = (extended.shape[2] - 1) // 2
    row_index = 2 * jnp.arange(bands, dtype=jnp.int32)[:, None] + support_rows + 2
    picked = jnp.take(extended, row_index, axis=1)
    tapped = jnp.stack(
        [picked[..., column_tap : column_tap + 2 * width : 2] for column_tap in range(3)], axis=3
    )
    patches = jnp.transpose(tapped, (1, 4, 2, 3, 0)).reshape(bands * width, -1)
    raw = jnp.dot(
        patches, conv_weight.reshape(-1, conv_weight.shape[-1]), preferred_element_type=F32
    )
    factor = lax.rsqrt(jnp.mean(raw * raw, axis=-1, keepdims=True) + 1e-06)
    return (raw * factor).astype(BF16).reshape(bands, width, -1)


def absorb(carry, block_keys, block_values, block_area, queries, scale):
    running_max, running_sum, mixed = carry
    scores = (
        jnp.einsum("qhd,khd->qhk", queries, block_keys, preferred_element_type=F32) * scale
        + block_area
    )
    new_max = jnp.maximum(running_max, jnp.max(scores, axis=-1))
    factor = jnp.exp(running_max - new_max)
    weights = jnp.exp(scores - new_max[..., None])
    running_sum = running_sum * factor + jnp.sum(weights, axis=-1)
    update = jnp.einsum(
        "qhk,khd->qhd", weights.astype(BF16), block_values, preferred_element_type=F32
    )
    mixed = mixed * factor[..., None] + update
    return (new_max, running_sum, mixed)


def sweep(carry, keys, values, queries, band_total):
    rows = keys.shape[0]
    lon_tile = keys.shape[1]
    head_size = D // H
    band_block = math.gcd(rows, max(1, 512 // lon_tile))
    blocks = rows // band_block
    block_len = band_block * lon_tile
    keys_blocks = keys.reshape(blocks, block_len, H, head_size)
    values_blocks = values.reshape(blocks, block_len, H, head_size)
    band_index = jnp.arange(rows, dtype=jnp.int32)
    area_rows = jnp.repeat(log_area(band_index, band_total), lon_tile).reshape(blocks, block_len)
    scale = 1.0 / math.sqrt(head_size)

    def step_block(state, inputs):
        return (absorb(state, inputs[0], inputs[1], inputs[2], queries, scale), None)

    result, unused = lax.scan(step_block, carry, (keys_blocks, values_blocks, area_rows))
    return result


def log_area(bands, band_total):
    centre = (bands.astype(F32) + 0.5) * (math.pi / band_total) - math.pi / 2
    return jnp.log(jnp.cos(centre))


def general(state_field, support_rows, window_bands, conv_weight, w_query, w_key, w_value, w_out):
    lat_tile = support_rows.shape[0]
    lon_tile = state_field.shape[2] // 2
    whole_lon = lon_tile * lax.axis_size("lon")
    band_total = lat_tile * lax.axis_size("lat")
    head_size = D // H
    extended = padded(state_field, (("lat", 1),), 2)
    western = shifted(extended[:, :, -1:], "lon", 1)
    extended = jnp.concatenate([western, extended], axis=2)
    features = conv_features(extended, support_rows, conv_weight)
    slot_count = window_bands.shape[0] // lax.axis_size("lat")
    piece = lax.all_gather(features, "lat", axis=0, tiled=True)
    mine = lax.dynamic_slice_in_dim(
        window_bands, lax.axis_index("lat") * slot_count, slot_count, axis=0
    )
    picked = jnp.take(piece, mine, axis=0)
    gathered = lax.all_gather(picked, "lon", axis=1, tiled=True)
    query_count = slot_count * whole_lon
    queries = jnp.dot(gathered.reshape(query_count, D), w_query, preferred_element_type=F32)
    queries = queries.astype(BF16).reshape(query_count, H, head_size)
    initial = (
        jnp.full((query_count, H), -1e30, F32),
        jnp.zeros((query_count, H), F32),
        jnp.zeros((query_count, H, head_size), F32),
    )
    piece_rows = piece.reshape(-1, D)
    keys = jnp.dot(piece_rows, w_key, preferred_element_type=F32).astype(BF16)
    values = jnp.dot(piece_rows, w_value, preferred_element_type=F32).astype(BF16)
    running_max, running_sum, mixed = sweep(
        initial, keys.reshape(piece.shape), values.reshape(piece.shape), queries, band_total
    )
    best = lax.pmax(running_max, "lon")
    factor = jnp.exp(running_max - best)
    scaled_mix = (mixed * factor[..., None]).reshape(slot_count, whole_lon, D)
    scaled_sum = (running_sum * factor).reshape(slot_count, whole_lon, H)
    mix_share, sum_share = (
        lax.psum_scatter(part.astype(BF16), "lon", scatter_dimension=1, tiled=True).astype(F32)
        for part in (scaled_mix, scaled_sum)
    )
    attended = mix_share.reshape(slot_count, lon_tile, H, head_size) / sum_share[..., None]
    attended = attended.astype(BF16).reshape(slot_count * lon_tile, D)
    result = jnp.dot(attended, w_out, preferred_element_type=F32).astype(BF16)
    return result.reshape(slot_count, lon_tile, D)


def exchange(x, lat_mask, lon_mask):
    lats, lons = lax.axis_size("lat"), lax.axis_size("lon")
    pairs = [
        (i * lons + j, (i ^ lat_mask) * lons + (j ^ lon_mask))
        for i in range(lats)
        for j in range(lons)
    ]
    return lax.ppermute(x, AXES, pairs)


def across(x):
    lats, lons = lax.axis_size("lat"), lax.axis_size("lon")
    pairs = []
    for i in range(2, lats, 2):
        for j in range(lons):
            pairs += [((i - 1) * lons + j, i * lons + j), (i * lons + j, (i - 1) * lons + j)]
    return lax.ppermute(x, AXES, pairs)


def rows_kernel(odd_ref, own_ref, lines_ref, far_ref, chip_ref, strided):
    channels, rows, lons = own_ref.shape
    deep = lines_ref.shape[1]
    edge = far_ref.shape[0]
    strided[0 : channels * rows] = own_ref[...].astype(F32).reshape(channels * rows, lons)
    strided[channels * rows :] = jnp.zeros(((deep - channels) * rows, lons), F32)
    lines = [strided[pl.ds(row, deep, stride=rows), :].astype(BF16) for row in range(rows)]
    for row in range(rows):
        lines_ref[row] = lines[row]
    odd = odd_ref[0] != 0
    for row in range(edge):
        top, bottom = lines[row], lines[rows - edge + row]
        far_ref[row] = jnp.where(odd, bottom, top)
        chip_ref[row] = jnp.where(odd, top, bottom)


def rows_of(odd, own, edge, deep):
    _, rows, lons = own.shape
    vmem = pl.BlockSpec(memory_space=pltpu.VMEM)
    return pl.pallas_call(
        rows_kernel,
        out_shape=(
            jax.ShapeDtypeStruct((rows, deep, lons), BF16),
            jax.ShapeDtypeStruct((edge, deep, lons), BF16),
            jax.ShapeDtypeStruct((edge, deep, lons), BF16),
        ),
        in_specs=[pl.BlockSpec(memory_space=pltpu.SMEM), vmem],
        out_specs=(vmem, vmem, vmem),
        scratch_shapes=[pltpu.VMEM((deep * rows, lons), F32)],
        compiler_params=pltpu.CompilerParams(vmem_limit_bytes=4 * 2**20),
        name="rows",
    )(odd, own)


def weights_kernel(weight_ref, picks_ref, out_ref, hits_ref):
    slots, taps, channels, width = weight_ref.shape
    deep = out_ref.shape[0] // (slots * taps)
    blank = jnp.zeros((deep - channels, width), BF16)
    for slot in range(slots):
        for tap in range(taps):
            at = (slot * taps + tap) * deep
            out_ref[at : at + deep] = jnp.concatenate([weight_ref[slot, tap], blank], axis=0)
    picks = picks_ref[...]
    row = lax.broadcasted_iota(jnp.int32, (128, 128), 0)
    lane = lax.broadcasted_iota(jnp.int32, (128, 128), 1)
    for slot in range(slots):
        hits = jnp.zeros((128, 128), F32)
        for band in range(picks.shape[0]):
            hits = jnp.where((row == picks[band, slot]) & (lane == band), 1.0, hits)
        hits_ref[:, slot * 128 : (slot + 1) * 128] = hits.astype(BF16)


def weights_of(conv_weight, picks, deep):
    slots, taps, _, width = conv_weight.shape
    vmem = pl.BlockSpec(memory_space=pltpu.VMEM)
    return pl.pallas_call(
        weights_kernel,
        out_shape=(
            jax.ShapeDtypeStruct((slots * taps * deep, width), BF16),
            jax.ShapeDtypeStruct((128, slots * 128), BF16),
        ),
        in_specs=[vmem, vmem],
        out_specs=(vmem, vmem),
        compiler_params=pltpu.CompilerParams(vmem_limit_bytes=4 * 2**20),
        cost_estimate=pl.CostEstimate(
            flops=0, bytes_accessed=4 * conv_weight.size, transcendentals=0
        ),
        name="weights",
    )(conv_weight, picks)


def columns_kernel(lines_ref, above_ref, below_ref, out_ref):
    rows = [ref[k] for ref in (above_ref, lines_ref, below_ref) for k in range(ref.shape[0])]
    lane = lax.broadcasted_iota(jnp.int32, (1, 128), 1)
    out = jnp.zeros(out_ref.shape, F32)
    for index, row in enumerate(rows):
        last = row[:, row.shape[1] - 128 :].astype(F32)[:, 127:128]
        out = jnp.where(lane == index, last, out)
    out_ref[...] = out.astype(BF16)


def last_columns(lines, above, below):
    vmem = pl.BlockSpec(memory_space=pltpu.VMEM)
    return pl.pallas_call(
        columns_kernel,
        out_shape=jax.ShapeDtypeStruct((lines.shape[1], 128), BF16),
        in_specs=[vmem] * 3,
        out_specs=vmem,
        compiler_params=pltpu.CompilerParams(vmem_limit_bytes=4 * 2**20),
        name="columns",
    )(lines, above, below)


def normed(raw):
    return raw * lax.rsqrt(jnp.mean(raw * raw, axis=-1, keepdims=True) + 1e-06)


def conv_kernel(
    picks_ref, lines_ref, above_ref, below_ref, weight_ref, out_ref, first_ref, taken, patches
):
    _, deep, lons = lines_ref.shape
    width = lons // 2
    bands, slots = picks_ref.shape
    taps = weight_ref.shape[0] // (slots * deep)
    rows = [ref[k] for ref in (above_ref, lines_ref, below_ref) for k in range(ref.shape[0])]
    column = lax.broadcasted_iota(jnp.int32, (lons, taps * lons), 0)
    place = lax.broadcasted_iota(jnp.int32, (lons, taps * lons), 1)
    wanted = 2 * (place % width) + place // lons - 1
    choose = (column == wanted).astype(F32).astype(BF16)
    split = jnp.dot(
        jnp.concatenate(rows, axis=0), choose, preferred_element_type=F32
    ).astype(BF16)
    for row in range(len(rows)):
        taken[row] = split[row * deep : (row + 1) * deep]
    left = lax.broadcasted_iota(jnp.int32, (1, lons), 1) < width
    picks = picks_ref[...]
    for slot in range(slots):
        for band in range(0, bands, 2):
            one, two = taken[picks[band, slot]], taken[picks[band + 1, slot]]
            for tap in range(taps):
                at = (slot * taps + tap) * deep
                patches[at : at + deep, band * width : (band + 2) * width] = jnp.where(
                    left,
                    one[:, tap * lons : (tap + 1) * lons],
                    two[:, tap * lons : (tap + 1) * lons],
                )
    raw = lax.dot_general(
        patches[...], weight_ref[...], (((0,), (0,)), ((), ())), preferred_element_type=F32
    )
    out_ref[...] = normed(raw).astype(BF16)
    for band in range(bands):
        first_ref[band] = raw[band * width : band * width + 8]


def local_features(picks, lines, above, below, weights):
    _, deep, lons = lines.shape
    width = weights.shape[1]
    bands = picks.shape[0]
    count = lines.shape[0] + above.shape[0] + below.shape[0]
    taps = weights.shape[0] // (picks.shape[1] * deep)
    tokens = bands * lons // 2
    vmem = pl.BlockSpec(memory_space=pltpu.VMEM)
    return pl.pallas_call(
        conv_kernel,
        out_shape=(
            jax.ShapeDtypeStruct((tokens, width), BF16),
            jax.ShapeDtypeStruct((bands, 8, width), F32),
        ),
        in_specs=[vmem] * 5,
        out_specs=(vmem, vmem),
        scratch_shapes=[
            pltpu.VMEM((count, deep, taps * lons), BF16),
            pltpu.VMEM((weights.shape[0], tokens), BF16),
        ],
        compiler_params=pltpu.CompilerParams(vmem_limit_bytes=12 * 2**20),
        cost_estimate=pl.CostEstimate(
            flops=2 * weights.size * tokens, bytes_accessed=2 * weights.size, transcendentals=0
        ),
        name="conv",
    )(picks, lines, above, below, weights)


def west_kernel(west_ref, hits_ref, weight_ref, some_ref, first_ref, out_ref):
    deep = west_ref.shape[0]
    slots = hits_ref.shape[1] // 128
    stride = weight_ref.shape[0] // slots
    bands = first_ref.shape[0]
    width = out_ref.shape[0] // bands
    chosen = jnp.dot(west_ref[...], hits_ref[...], preferred_element_type=F32).astype(BF16)
    columns = jnp.concatenate(
        [chosen[:, slot * 128 : (slot + 1) * 128] for slot in range(slots)], axis=0
    )
    filters = jnp.concatenate(
        [weight_ref[slot * stride : slot * stride + deep] for slot in range(slots)], axis=0
    )
    more = lax.dot_general(
        columns, filters, (((0,), (0,)), ((), ())), preferred_element_type=F32
    )
    out_ref[...] = some_ref[...]
    head = lax.broadcasted_iota(jnp.int32, (16, 1), 0) == 0
    for band in range(bands):
        fixed = normed(first_ref[band, 0:1] + more[band : band + 1])
        rest = some_ref[band * width : band * width + 16].astype(F32)
        out_ref[band * width : band * width + 16] = jnp.where(head, fixed, rest).astype(BF16)


def west_added(west, hits, weights, some, first):
    vmem = pl.BlockSpec(memory_space=pltpu.VMEM)
    return pl.pallas_call(
        west_kernel,
        out_shape=jax.ShapeDtypeStruct(some.shape, BF16),
        in_specs=[vmem] * 5,
        out_specs=vmem,
        compiler_params=pltpu.CompilerParams(vmem_limit_bytes=6 * 2**20),
        name="west",
    )(west, hits, weights, some, first)


def select_kernel(where_ref, near_ref, own_ref, pair_ref, other_ref):
    slots, rows, _ = own_ref.shape
    where = where_ref[...]
    for index in range(4 * slots):
        start = pl.multiple_of(where[index, 1], rows)
        picked = near_ref[pl.ds(start, rows)]
        picked = jnp.where(where[index, 0] != 0, picked, jnp.zeros_like(picked))
        if index < 2 * slots:
            (own_ref if index < slots else pair_ref)[index % slots] = picked
        else:
            other_ref[index - 2 * slots] = picked


def selected(where, near, rows):
    slots = where.shape[0] // 4
    vmem = pl.BlockSpec(memory_space=pltpu.VMEM)
    shape = jax.ShapeDtypeStruct((slots, rows, near.shape[1]), near.dtype)
    both = jax.ShapeDtypeStruct((2 * slots, rows, near.shape[1]), near.dtype)
    return pl.pallas_call(
        select_kernel,
        out_shape=(shape, shape, both),
        in_specs=[vmem, vmem],
        out_specs=(vmem, vmem, vmem),
        compiler_params=pltpu.CompilerParams(vmem_limit_bytes=2**20 + 2 * near.size),
        name="select",
    )(where, near)


def split3(x):
    high = x.astype(BF16).astype(F32)
    middle = (x - high).astype(BF16).astype(F32)
    return high, middle, x - high - middle


def attend_kernel(
    keys_count, sel_ref, got_ref, area_ref, wq_ref, wk_ref, wv_ref, *refs
):
    held, (out_ref, *rest) = refs[:keys_count], refs[keys_count:]
    slots, rows, width = sel_ref.shape
    count = slots * rows
    head_size = width // H
    token = (sel_ref[...] + got_ref[...]).reshape(count, width)
    query = jnp.dot(token, wq_ref[...], preferred_element_type=F32).astype(BF16)
    lane = lax.broadcasted_iota(jnp.int32, (1, width), 1) // head_size
    spread = jnp.concatenate(
        [jnp.where(lane == head, query, jnp.zeros_like(query)) for head in range(H)], axis=0
    )
    turned = lax.dot_general(
        spread, wk_ref[...], (((1,), (1,)), ((), ())), preferred_element_type=F32
    )
    turned = (turned * (LOG2E / math.sqrt(head_size))).astype(BF16)
    parts, begin = [], 0
    for ref in held:
        for at in range(0, ref.shape[0], 512):
            chunk = min(512, ref.shape[0] - at)
            parts.append((ref, at, begin, chunk))
            begin += chunk
    top = None
    for ref, at, begin, chunk in parts:
        keys = ref[at : at + chunk]
        block = lax.dot_general(
            turned, keys, (((1,), (1,)), ((), ())), preferred_element_type=F32
        )
        block = block + area_ref[:, begin : begin + chunk]
        best = block[:, 0:128]
        for lanes in range(128, chunk, 128):
            best = jnp.maximum(best, block[:, lanes : lanes + 128])
        best = jnp.max(best, axis=1, keepdims=True)
        if top is not None:
            best = jnp.maximum(top, best)
        weight = jnp.exp2(block - best)
        added = weight[:, 0:128]
        for lanes in range(128, chunk, 128):
            added = added + weight[:, lanes : lanes + 128]
        update = jnp.dot(weight.astype(BF16), keys, preferred_element_type=F32)
        if top is None:
            total, mixed = added, update
        else:
            factor = jnp.exp2(top - best)
            total, mixed = total * factor + added, mixed * factor + update
        top = best
    total = jnp.sum(total, axis=1, keepdims=True)
    value = jnp.dot((mixed / total).astype(BF16), wv_ref[...], preferred_element_type=F32)
    lse = top + jnp.log2(total)
    out = jnp.zeros((count, width), F32)
    stat_lane = lax.broadcasted_iota(jnp.int32, (1, 128), 1)
    stats = jnp.zeros((count, 128), F32)
    for head in range(H):
        out = jnp.where(lane == head, value[head * count : (head + 1) * count], out)
        for order, piece in enumerate(split3(lse[head * count : (head + 1) * count])):
            stats = jnp.where(stat_lane == 3 * head + order, piece, stats)
    out_ref[:, 0:rows, :] = out.reshape(sel_ref.shape).astype(out_ref.dtype)
    stats = stats.reshape(slots, rows, 128)
    if rest:
        rest[0][...] = stats
    else:
        out_ref[:, rows:, :] = jnp.zeros((slots, 16, width), out_ref.dtype)
        for slot in range(slots):
            out_ref[slot, rows:, 0:rows] = stats[slot].T[0:16].astype(out_ref.dtype)


def attended(sent, sel, got, area, w_query, w_key, w_value, held):
    slots, rows, width = sel.shape
    keys = sum(part.shape[0] for part in held)
    count = slots * rows
    vmem = pl.BlockSpec(memory_space=pltpu.VMEM)
    if sent:
        out_shape = (jax.ShapeDtypeStruct((slots, rows + 16, width), BF16),)
    else:
        out_shape = (
            jax.ShapeDtypeStruct((slots, rows, width), F32),
            jax.ShapeDtypeStruct((slots, rows, 128), F32),
        )
    return pl.pallas_call(
        functools.partial(attend_kernel, len(held)),
        out_shape=out_shape,
        in_specs=[vmem] * (6 + len(held)),
        out_specs=(vmem,) * len(out_shape),
        compiler_params=pltpu.CompilerParams(vmem_limit_bytes=20 * 2**20),
        cost_estimate=pl.CostEstimate(
            flops=4 * H * count * keys * width,
            bytes_accessed=2 * keys * width,
            transcendentals=H * count * keys,
        ),
        name="attend_sent" if sent else "attend_kept",
    )(sel, got, area, w_query, w_key, w_value, *held)


def finish_kernel(keep_ref, lse_ref, got_ref, out_ref):
    slots, rows, width = keep_ref.shape
    count = slots * rows
    keep = keep_ref[...].reshape(count, width)
    got = got_ref[:, 0:rows, :].astype(F32).reshape(count, width)
    ours = lse_ref[...].reshape(count, 128).astype(BF16)
    piece = lax.broadcasted_iota(jnp.int32, (128, width), 0) // 3
    head = lax.broadcasted_iota(jnp.int32, (128, width), 1) // (width // H)
    spread = (piece == head).astype(F32).astype(BF16)
    own = jnp.dot(ours, spread, preferred_element_type=F32)
    far = jnp.concatenate(
        [
            lax.dot_general(
                got_ref[slot, rows:, 0:rows], spread[0:16], (((0,), (0,)), ((), ())),
                preferred_element_type=F32,
            )
            for slot in range(slots)
        ],
        axis=0,
    )
    top = jnp.maximum(own, far)
    own = jnp.exp2(own - top)
    far = jnp.exp2(far - top)
    mixed = ((keep * own + got * far) / (own + far)).astype(BF16)
    out_ref[...] = mixed.reshape(out_ref.shape)


def finished(keep, lse, got, w_out):
    vmem = pl.BlockSpec(memory_space=pltpu.VMEM)
    mixed = pl.pallas_call(
        finish_kernel,
        out_shape=jax.ShapeDtypeStruct(keep.shape, BF16),
        in_specs=[vmem] * 3,
        out_specs=vmem,
        compiler_params=pltpu.CompilerParams(vmem_limit_bytes=4 * 2**20),
        name="finish",
    )(keep, lse, got)
    result = jnp.dot(mixed.reshape(-1, keep.shape[2]), w_out, preferred_element_type=F32)
    return result.astype(BF16).reshape(keep.shape)


def gathered(block, masks):
    blocks = {(0, 0): block}
    for mask in masks:
        blocks[mask] = exchange(block, *mask)
    whole = (sum(mask[0] for mask in masks), sum(mask[1] for mask in masks))
    if whole not in blocks:
        blocks[whole] = exchange(block, *whole)
    for size in range(2, len(masks)):
        for start in range(len(masks)):
            chosen = [masks[(start + k) % len(masks)] for k in range(size)]
            key = (sum(mask[0] for mask in chosen), sum(mask[1] for mask in chosen))
            step = chosen[-1]
            blocks[key] = exchange(blocks[key[0] ^ step[0], key[1] ^ step[1]], *step)
    return blocks


def halves(state_field, support_rows, window_bands, conv_weight, w_query, w_key, w_value, w_out):
    lats = lax.axis_size("lat")
    lat, lon = lax.axis_index("lat"), lax.axis_index("lon")
    channels, rows, lons = state_field.shape
    lat_tile = support_rows.shape[0]
    lon_tile = lons // 2
    band_total = lat_tile * lats
    pair = lats // 2

    deep = -(-channels // 16) * 16
    odd = lat & 1
    lines, out_far, out_chip = rows_of(odd.astype(jnp.int32).reshape(1), state_field, 2, deep)
    far_rows = across(out_far)
    chip_rows = exchange(out_chip, 1, 0)
    above = jnp.where(odd != 0, chip_rows, far_rows)
    below = jnp.where(odd != 0, far_rows, chip_rows)
    west = exchange(last_columns(lines, above, below), 0, 1)
    picks = 2 * jnp.arange(lat_tile, dtype=jnp.int32)[:, None] + support_rows + 2
    weights, hits = weights_of(conv_weight, picks, deep)
    some, first = local_features(picks, lines, above, below, weights)
    features = west_added(west, hits, weights, some, first)

    bits = [1 << k for k in range(1, lats.bit_length() - 1) if 1 << k != pair]
    masks = [(0, 1)] + [(bit, 0) for bit in bits]
    blocks = gathered(features, masks)
    order = [(i, j) for i in range(0, pair, 2) for j in range(2)]
    near = jnp.concatenate([blocks[key] for key in order], axis=0)

    size = lat_tile * lon_tile
    slot_count = window_bands.shape[0] // lats
    sides = jnp.stack([lat, lat ^ pair, lat ^ 1, lat ^ pair ^ 1])
    wanted = window_bands[
        (sides[:, None] * slot_count + jnp.arange(slot_count)[None, :]).reshape(-1)
    ]
    owner = wanted // lat_tile
    apart = owner ^ lat
    place = (apart & (pair - 2)) * size + wanted % lat_tile * lon_tile
    within = apart & (pair | 1) == 0
    where = jnp.stack([within.astype(jnp.int32), place.astype(jnp.int32)], axis=1)
    sel_own, sel_pair, sel_other = selected(where, near, lon_tile)
    got_other = exchange(sel_other, 1, 0)
    sel_own = sel_own + got_other[:slot_count]
    sel_pair = sel_pair + got_other[slot_count:]
    sel_own, sel_pair, near = lax.optimization_barrier((sel_own, sel_pair, near))
    got_pair = exchange(sel_own, pair, 0)
    got_own = exchange(sel_pair, pair, 0)
    held = (near, exchange(near, 1, 0))

    step = jnp.arange(2 * len(order) * lat_tile, dtype=jnp.int32)
    masks = (step // lat_tile) % len(order)
    tile = lat ^ ((masks & ~1) | (step // (len(order) * lat_tile)))
    key_band = tile * lat_tile + step % lat_tile
    area = LOG2E * log_area(key_band, band_total)
    area = jnp.repeat(area, lon_tile)[None, :]
    shared = (area, w_query, w_key, w_value, held)
    (send,) = attended(True, sel_pair, got_pair, *shared)
    received = exchange(send, pair, 0)
    keep, lse = attended(False, sel_own, got_own, *shared)
    return finished(keep, lse, received, w_out)


def per_device(state_field, support_rows, *rest):
    lats, lons = lax.axis_size("lat"), lax.axis_size("lon")
    _, rows, columns = state_field.shape
    paired = lons == 2 and lats >= 4 and lats & (lats - 1) == 0
    tiled = columns == 128 and rows % 8 == 0 and support_rows.shape[0] % 2 == 0
    plan = halves if paired and tiled else general
    return plan(state_field, support_rows, *rest)


def solution(mesh):
    return jax.shard_map(
        per_device,
        mesh=mesh,
        in_specs=(P(None, "lat", "lon"), P("lat", None), P(), P(), P(), P(), P(), P()),
        out_specs=P("lat", "lon", None),
        check_vma=False,
    )
```
